32 devices in a mesh: xy: 16 (over z, y, core), gz: 2 (over x).
Axes of the slice: x: 2, y: 2, z: 4, core: 2. Of those that a mesh axis runs over, the one named last changes fastest.
Arguments:
- noise: float32 [16, 8, 4, 32], P('xy', 'gz'), may hold values from -3.5 to 3.5
- w_first: bfloat16 [2, 81, 64, 1], replicated, may hold values from -0.625 to 0.625
- b_first: float32 [2, 64], replicated, may hold values from -3 to 3
- w_mid: bfloat16 [2, 81, 64, 64], replicated, may hold values from -0.078125 to 0.078125
- b_mid: float32 [2, 64], replicated, may hold values from -3 to 3
- w_last: bfloat16 [2, 81, 2, 64], replicated, may hold values from -0.078125 to 0.078125
- b_last: float32 [2, 2], replicated, may hold values from -3 to 3
Outputs:
- sample: float32 [16, 8, 4, 32], P('xy', 'gz')
- noise_force: float32 [16, 8, 4, 32], P('xy', 'gz')
- loss: float32 [], replicated
- grad_w_first: float32 [2, 81, 64, 1], replicated
- grad_b_first: float32 [2, 64], replicated
- grad_w_mid: float32 [2, 81, 64, 64], replicated
- grad_b_mid: float32 [2, 64], replicated
- grad_w_last: float32 [2, 81, 2, 64], replicated
- grad_b_last: float32 [2, 2], replicated
The draws below stay inside these ranges and needn't reach their ends.
All inputs are finite; a program needn't handle non-finite values.
Results may differ from the reference program's by a relative error of at most 0.022.
Values may be sent and summed in bfloat16 or wider, within the bound.
No kernel may reach another device: no remote copies, remote signals or barrier semaphores. Data moves between devices by JAX's collectives and lax.ppermute only.
A program may use at most 320 MiB of HBM per device.

```python
import jax
import jax.numpy as jnp
from jax import lax

HID = 64
TAPS = 81
LAYERS = 2
LY = 4
LT = 32
LX = 16
LZ = 8


def draw_noise(key, part):
    base_key = jax.random.fold_in(key, 11)
    extents = (LX, LZ, LY, LT)
    position = lax.broadcasted_iota(jnp.float32, extents, 0) / max(LX - 1, 1)
    values = jax.random.normal(base_key, extents, jnp.float32)
    spread_factor = 0.4 * jnp.exp(jnp.log(3.0) * position)
    return jnp.clip(values * spread_factor, -3.5, 3.5)


def centred(rng, extent, deviation, reach, dtype=jnp.bfloat16):
    result = jax.random.normal(rng, extent, jnp.float32) * deviation
    return jnp.minimum(jnp.maximum(result, -reach), reach).astype(dtype)


def setup_inputs(seed: int = 0) -> dict:
    seeds = jax.random.split(jax.random.key(seed), 8)
    return {
        "noise": draw_noise(jax.random.fold_in(seeds[7], 71), 0),
        "w_first": centred(seeds[1], (LAYERS, TAPS, HID, 1), TAPS ** -0.5, 0.625),
        "b_first": centred(seeds[2], (LAYERS, HID), 0.5, 3.0, jnp.float32),
        "w_mid": centred(seeds[3], (LAYERS, TAPS, HID, HID), (TAPS * HID) ** -0.5, 0.078125),
        "b_mid": centred(seeds[4], (LAYERS, HID), 0.5, 3.0, jnp.float32),
        "w_last": centred(seeds[5], (LAYERS, TAPS, 2, HID), (TAPS * HID) ** -0.5, 0.078125),
        "b_last": centred(seeds[6], (LAYERS, 2), 0.5, 3.0, jnp.float32),
    }


hopping = 0.3
quartic = 0.05

def all_taps():
    return [(delta_x, delta_z, delta_y, delta_t) for delta_x in (-1, 0, 1) for delta_z in (-1, 0, 1) for delta_y in (-1, 0, 1) for delta_t in (-1, 0, 1)]

def convolve(inputs, weight):
    channels = inputs.shape[0]
    summed = jnp.zeros((weight.shape[1], inputs[0].size), jnp.float32)
    for tap_index, offset in enumerate(all_taps()):
        shifted = jnp.roll(inputs, tuple((-amount for amount in offset)), axis=(1, 2, 3, 4))
        summed = summed + jnp.dot(weight[tap_index], shifted.reshape(channels, -1), preferred_element_type=jnp.float32)
    return summed.reshape((weight.shape[1],) + inputs.shape[1:])

def weight_grad(grad_out, inputs):
    flat_grad = grad_out.reshape(grad_out.shape[0], -1)
    blocks = []
    for offset in all_taps():
        shifted = jnp.roll(inputs, tuple((-amount for amount in offset)), axis=(1, 2, 3, 4)).reshape(inputs.shape[0], -1)
        blocks.append(lax.dot_general(flat_grad, shifted, (((1,), (1,)), ((), ())), preferred_element_type=jnp.float32))
    return jnp.stack(blocks)

def mirrored(weight):
    return weight[::-1].transpose(0, 2, 1)

def expand(bias):
    return bias[:, None, None, None, None]

def reference(noise, w_first, b_first, w_mid, b_mid, w_last, b_last):
    extents = noise.shape
    coords = lax.broadcasted_iota(jnp.int32, extents, 0) + lax.broadcasted_iota(jnp.int32, extents, 1)
    coords = coords + lax.broadcasted_iota(jnp.int32, extents, 2) + lax.broadcasted_iota(jnp.int32, extents, 3)
    oddness = (coords % 2).astype(jnp.float32)
    volume = float(noise.size)
    field = noise
    saved = []
    logdet = jnp.zeros((), jnp.float32)
    for layer in range(2):
        frozen = oddness if layer == 0 else 1.0 - oddness
        moving = 1.0 - frozen
        net_input = (frozen * field)[None].astype(jnp.bfloat16)
        first = jnp.tanh(convolve(net_input, w_first[layer]) + expand(b_first[layer])).astype(jnp.bfloat16)
        second = jnp.tanh(convolve(first, w_mid[layer]) + expand(b_mid[layer])).astype(jnp.bfloat16)
        output = convolve(second, w_last[layer]) + expand(b_last[layer])
        growth = jnp.exp(output[0])
        saved.append((field, frozen, net_input, first, second, growth))
        field = frozen * field + moving * (field * growth + output[1])
        logdet = logdet + jnp.sum(moving * output[0])
    ahead = jnp.roll(field, -1, 0) + jnp.roll(field, -1, 1) + jnp.roll(field, -1, 2) + jnp.roll(field, -1, 3)
    behind = jnp.roll(field, 1, 0) + jnp.roll(field, 1, 1) + jnp.roll(field, 1, 2) + jnp.roll(field, 1, 3)
    squared = field * field
    action = jnp.sum(-2.0 * hopping * field * ahead + squared + quartic * (squared - 1.0) * (squared - 1.0))
    loss = (action - logdet) / volume
    upstream = -2.0 * hopping * (ahead + behind) + 2.0 * field + 4.0 * quartic * (squared - 1.0) * field
    collected = [None, None]
    for layer in (1, 0):
        field_in, frozen, net_input, first, second, growth = saved[layer]
        moving = 1.0 - frozen
        grad_scale = upstream * moving * field_in * growth - moving
        grad_shift = upstream * moving
        grad_output = jnp.stack([grad_scale, grad_shift]).astype(jnp.bfloat16)
        bias_last = lax.optimization_barrier(jnp.sum(grad_output.astype(jnp.float32), axis=(1, 2, 3, 4)))
        weight_last = weight_grad(grad_output, second)
        second_wide = second.astype(jnp.float32)
        grad_second = (convolve(grad_output, mirrored(w_last[layer])) * (1.0 - second_wide * second_wide)).astype(jnp.bfloat16)
        bias_mid = lax.optimization_barrier(jnp.sum(grad_second.astype(jnp.float32), axis=(1, 2, 3, 4)))
        weight_mid = weight_grad(grad_second, first)
        first_wide = first.astype(jnp.float32)
        grad_first = (convolve(grad_second, mirrored(w_mid[layer])) * (1.0 - first_wide * first_wide)).astype(jnp.bfloat16)
        bias_first = lax.optimization_barrier(jnp.sum(grad_first.astype(jnp.float32), axis=(1, 2, 3, 4)))
        weight_first = weight_grad(grad_first, net_input)
        grad_input = convolve(grad_first, mirrored(w_first[layer]))[0]
        upstream = upstream * (frozen + moving * growth) + frozen * grad_input
        collected[layer] = (weight_first, bias_first, weight_mid, bias_mid, weight_last, bias_last)
    stacked = [jnp.stack([collected[0][slot], collected[1][slot]]) / volume for slot in range(6)]
    return (field, upstream, loss, stacked[0], stacked[1], stacked[2], stacked[3], stacked[4], stacked[5])
```

```python
import functools

import jax
import jax.numpy as jnp
import numpy as np
from jax import lax
from jax.experimental import pallas as pl
from jax.experimental.pallas import tpu as pltpu
from jax.sharding import PartitionSpec as P

hopping = 0.3
quartic = 0.05

STEPS = (-1, 0, 1)
ROWS = 8
MID = 3
BF = jnp.bfloat16
F32 = jnp.float32
HIGH = lax.Precision.HIGHEST


def ring_order(count):
    if count % 4:
        return list(range(count))
    depth = count // 4
    chips = [(z, 0) for z in range(depth)] + [(z, 1) for z in reversed(range(depth))]
    order = []
    for place, (z, y) in enumerate(chips):
        cores = (0, 1) if place % 2 == 0 else (1, 0)
        order += [z * 4 + y * 2 + core for core in cores]
    return order


def spread_first():
    out = np.zeros((81, 5, 256), np.float32)
    for tap in range(81):
        dx, rest = divmod(tap, 27)
        for dest in range(5):
            out[tap, dest, rest * ROWS + dest + dx] = 1
    return out.reshape(81, 5 * 256)


def spread_last():
    out = np.zeros((216, 54), np.float32)
    for rest in range(27):
        for o in range(2):
            out[rest * 8 + o, rest * 2 + o] = 1
    return out


def spread_last_back():
    out = np.zeros((81, 2, 3, 512), np.float32)
    for tap in range(81):
        dx, rest = divmod(tap, 27)
        for o in range(2):
            for dest in range(3):
                out[tap, o, dest, rest * 16 + o * ROWS + 2 + dest - (dx - 1)] = 1
    return out.reshape(162, 3 * 512)


def spread_first_back():
    out = np.zeros((216, 81), np.float32)
    for tap in range(81):
        dx, rest = divmod(tap, 27)
        out[rest * 8 + dx, tap] = 1
    return out


def z_shift(values, dz):
    length = values.shape[1]
    return values if dz == 0 else pltpu.roll(values, (-dz * 128) % length, 1)


def by_plane(values, fn):
    parts = [fn(values[:, at : at + 128]) for at in range(0, values.shape[1], 128)]
    return parts[0] if len(parts) == 1 else jnp.concatenate(parts, axis=1)


def y_shift(values, dy, period):
    if dy == 0:
        return values
    return by_plane(values, lambda v: pltpu.roll(v, (-dy * period) % 128, 1))


def t_shift(values, dt, period):
    if dt == 0:
        return values

    def one(v):
        place = lax.broadcasted_iota(jnp.int32, v.shape, 1) % period
        main = pltpu.roll(v, (-dt) % 128, 1)
        wrap = pltpu.roll(v, (dt * (period - 1)) % 128, 1)
        return jnp.where(place == (period - 1 if dt == 1 else 0), wrap, main)

    return by_plane(values, one)


def all_shifts(values, sign, period):
    in_t = [t_shift(values, sign * dt, period) for dt in STEPS]
    in_y = [[y_shift(v, sign * dy, period) for v in in_t] for dy in STEPS]
    return [z_shift(in_y[dy][dt], sign * dz) for dz in STEPS for dy in range(3) for dt in range(3)]


def gather_narrow(values, sign, period):
    block = lambda k: values[k * 8 : k * 8 + 8]
    total = None
    for dt in range(3):
        over_y = None
        for dy in range(3):
            over_z = sum(z_shift(block(dz * 9 + dy * 3 + dt), sign * (dz - 1)) for dz in range(3))
            over_z = y_shift(over_z, sign * (dy - 1), period)
            over_y = over_z if over_y is None else over_y + over_z
        over_y = t_shift(over_y, sign * (dt - 1), period)
        total = over_y if total is None else total + over_y
    return total


def gather_wide(values, channels, sign, period):
    block = lambda k: values[k * channels : (k + 1) * channels]
    total = None
    for dt in range(3):
        over_y = None
        for dy in range(3):
            part = y_shift(block(dy * 3 + dt), sign * (dy - 1), period)
            over_y = part if over_y is None else over_y + part
        over_y = t_shift(over_y, sign * (dt - 1), period)
        total = over_y if total is None else total + over_y
    return total


def dot(a, b):
    return jnp.dot(a, b, preferred_element_type=F32)


def dot_nt(a, b):
    return lax.dot_general(a, b, (((1,), (1,)), ((), ())), preferred_element_type=F32)


def stack_planes(stack, planes, channels, order):
    length = stack.shape[1]
    for dx in range(3):
        for dz in range(3):
            plane, step = order(dx, dz)
            rows = pl.ds((dx * 3 + dz) * channels, channels)
            source = planes[plane * channels : (plane + 1) * channels, :]
            if step == 0:
                stack[rows, :] = source
            elif step == 1:
                stack[rows, : length - 128] = source[:, 128:]
                stack[rows, length - 128 :] = source[:, :128]
            else:
                stack[rows, 128:] = source[:, : length - 128]
                stack[rows, :128] = source[:, length - 128 :]


def place_windows(refs, row, target):
    target[...] = jnp.zeros_like(target)
    for r, ref in enumerate(refs):
        target[r : r + 1, :] = ref[row : row + 1, :]


def forward_kernel(
    period, layer, many, *refs
):
    windows, refs = refs[:many], refs[many:]
    (odd, w_first, b_first, w_mid, b_mid, w_last, b_last,
     field_out, state, first_out, second_out, logdet, first, stack, *scratch) = refs
    channels = w_mid.shape[0] // 9
    length = odd.shape[1]
    if many == 1:
        field_out[...] = windows[0][...]
    else:
        growth_out, = scratch
        place_windows(windows, 0, field_out)
        place_windows(windows, 1, growth_out)
    field = field_out[...]
    frozen = odd[...] if layer == 0 else 1.0 - odd[...]
    net = frozen * field
    taps = jnp.concatenate(all_shifts(net, 1, period), axis=0).astype(BF)
    for dest in range(5):
        part = dot(w_first[:, dest * 256 : dest * 256 + 216], taps)
        first[dest * channels : (dest + 1) * channels, :] = jnp.tanh(part + b_first[...]).astype(BF)
    first_out[...] = first[channels : 4 * channels, :]
    for dest in range(3):
        stack_planes(stack, first, channels, lambda dx, dz: (dest + dx, dz - 1))
        for at in range(0, length, 256):
            wide = dot(w_mid[...], stack[:, at : at + 256])
            wide = gather_wide(wide, channels, 1, period)
            second_out[dest * channels : (dest + 1) * channels, at : at + 256] = jnp.tanh(
                wide + b_mid[...]
            ).astype(BF)
    narrow = sum(
        dot(w_last[dx], second_out[dx * channels : (dx + 1) * channels, :]) for dx in range(3)
    )
    narrow = gather_narrow(narrow, 1, period) + b_last[...]
    growth = jnp.exp(narrow[0:1])
    mine = field[MID : MID + 1]
    still = frozen[MID : MID + 1]
    moving = 1.0 - still
    state[0:1, :] = still * mine + moving * (mine * growth + narrow[1:2])
    state[1:2, :] = growth
    flow = moving * narrow[0:1]
    logdet[...] = sum(flow[:, at : at + 128] for at in range(0, length, 128))


def backward_kernel(period, layer, *refs):
    if layer == 1:
        windows, refs = refs[:7], refs[7:]
        (odd, field_in, first_in, second_in, w_last, w_mid, w_first,
         base_out, part_out, action, g_first, gb_first, g_mid, gb_mid, g_last, gb_last,
         field_end, growth, stack, turned) = refs
        place_windows(windows, 0, field_end)
        place_windows(windows, 1, growth)
    else:
        windows, refs = refs[:7], refs[7:]
        (base_in, growth, odd, field_in, first_in, second_in, w_last, w_mid, w_first,
         part_out, g_first, gb_first, g_mid, gb_mid, g_last, gb_last,
         upstream_ref, stack, turned) = refs
    channels = w_mid.shape[0] // 9
    length = odd.shape[1]
    frozen = odd[...] if layer == 0 else 1.0 - odd[...]
    moving = 1.0 - frozen
    place = lax.broadcasted_iota(jnp.int32, (ROWS, length), 0)
    inner = jnp.logical_and(place >= 1, place <= 5)
    if layer == 1:
        field = field_end[...]
        ahead = (
            pltpu.roll(field, ROWS - 1, 0)
            + z_shift(field, 1)
            + y_shift(field, 1, period)
            + t_shift(field, 1, period)
        )
        behind = (
            pltpu.roll(field, 1, 0)
            + z_shift(field, -1)
            + y_shift(field, -1, period)
            + t_shift(field, -1, period)
        )
        squared = field * field
        density = (
            -2.0 * hopping * field * ahead
            + squared
            + quartic * (squared - 1.0) * (squared - 1.0)
        )[MID : MID + 1]
        action[...] = sum(density[:, at : at + 128] for at in range(0, length, 128))
        upstream = (
            -2.0 * hopping * (ahead + behind)
            + 2.0 * field
            + 4.0 * quartic * (squared - 1.0) * field
        )
        upstream = jnp.where(inner, upstream, 0.0)
    else:
        upstream_ref[...] = base_in[...]
        for r in range(1, 6):
            upstream_ref[r : r + 1, :] += (
                windows[r - 1][2:3, :] + windows[r][1:2, :] + windows[r + 1][0:1, :]
            )
        upstream = upstream_ref[...]
    grow = growth[...]
    grad_scale = upstream * moving * field_in[...] * grow - moving
    grad_shift = upstream * moving
    grad_output = jnp.where(
        jnp.concatenate([inner, inner], axis=0),
        jnp.concatenate([grad_scale, grad_shift], axis=0),
        0.0,
    )
    own = jnp.concatenate([grad_output[MID : MID + 1], grad_output[8 + MID : 9 + MID]], axis=0)
    gb_last[...] = jnp.sum(own.astype(BF).astype(F32), axis=1, keepdims=True)
    taps = jnp.concatenate(all_shifts(grad_output, -1, period), axis=0).astype(BF)
    g_last[...] = dot_nt(taps, second_in[channels : 2 * channels, :])
    mids = []
    for dest in range(3):
        part = dot(w_last[:, dest * 512 : dest * 512 + 432], taps)
        wide = second_in[dest * channels : (dest + 1) * channels, :].astype(F32)
        mids.append(part * (1.0 - wide * wide))
    gb_mid[...] = jnp.sum(mids[1].astype(BF).astype(F32), axis=1, keepdims=True)
    rounded = mids[1].astype(BF).astype(F32)
    in_t = [t_shift(rounded, -dt, period) for dt in STEPS]
    for dy in range(3):
        for dt in range(3):
            turned[(dy * 3 + dt) * channels : (dy * 3 + dt + 1) * channels, :] = y_shift(
                in_t[dt], -STEPS[dy], period
            ).astype(BF)
    stack_planes(stack, first_in, channels, lambda dx, dz: (dx, dz - 1))
    g_mid[...] = dot_nt(turned[...], stack[...])
    planes = jnp.concatenate([m.astype(BF) for m in mids], axis=0)
    stack_planes(stack, planes, channels, lambda dx, dz: (2 - dx, 1 - dz))
    firsts = []
    for at in range(0, length, 256):
        wide = dot(w_mid[...], stack[:, at : at + 256])
        wide = gather_wide(wide, channels, -1, period)
        seen = first_in[channels : 2 * channels, at : at + 256].astype(F32)
        firsts.append((wide * (1.0 - seen * seen)).astype(BF))
    grad_first = jnp.concatenate(firsts, axis=1)
    gb_first[...] = jnp.sum(grad_first.astype(F32), axis=1, keepdims=True)
    net = frozen * field_in[...]
    taps = jnp.concatenate(all_shifts(net, 1, period), axis=0).astype(BF)
    g_first[...] = dot_nt(taps, grad_first)
    narrow = gather_narrow(dot(w_first[...], grad_first), -1, period)
    base = upstream * (frozen + moving * grow)
    for d in range(3):
        row = frozen[MID - 1 + d : MID + d] * narrow[d : d + 1]
        if layer == 0 and d == 1:
            row = row + base[MID : MID + 1]
        part_out[d : d + 1, :] = row
    if layer == 1:
        base_out[...] = base


def kernel_call(body, outs, scratch, args, flops):
    vmem = pl.BlockSpec(memory_space=pltpu.VMEM)
    return pl.pallas_call(
        body,
        out_shape=tuple(outs),
        in_specs=[vmem] * len(args),
        out_specs=tuple([vmem] * len(outs)),
        scratch_shapes=scratch,
        compiler_params=pltpu.CompilerParams(vmem_limit_bytes=52 * 2**20),
        cost_estimate=pl.CostEstimate(flops=flops, bytes_accessed=4_000_000, transcendentals=500_000),
    )(*args)


def shape(dims, dtype=F32):
    return jax.ShapeDtypeStruct(dims, dtype)


def forward(period, layer, windows, odd, weights, channels):
    length = odd.shape[1]
    many = len(windows)
    outs = [
        shape((ROWS, length)),
        shape((2, length)),
        shape((3 * channels, length), BF),
        shape((3 * channels, length), BF),
        shape((1, 128)),
    ]
    scratch = [
        pltpu.VMEM((5 * channels, length), BF),
        pltpu.VMEM((9 * channels, length), BF),
    ]
    if many > 1:
        scratch.append(pltpu.VMEM((ROWS, length), F32))
    body = functools.partial(forward_kernel, period, layer, many)
    if many > 1:
        outs.append(shape((ROWS, length)))

        def body(*refs):
            ins = refs[: many + 7]
            field, state, first, second, logdet, growth = refs[many + 7 : many + 13]
            a, b, _ = refs[many + 13 :]
            forward_kernel(
                period, layer, many, *ins, field, state, first, second, logdet, a, b, growth
            )

    return kernel_call(body, outs, scratch, [*windows, odd, *weights], 3 * 2 * 81 * 64 * 64 * length)


def backward(period, layer, windows, extra, odd, field, first, second, weights, channels):
    length = odd.shape[1]
    grads = [
        shape((216, channels)),
        shape((channels, 1)),
        shape((9 * channels, 9 * channels)),
        shape((channels, 1)),
        shape((432, channels)),
        shape((2, 1)),
    ]
    if layer == 1:
        outs = [shape((ROWS, length)), shape((3, length)), shape((1, 128))] + grads
        scratch = [pltpu.VMEM((ROWS, length), F32), pltpu.VMEM((ROWS, length), F32)]
    else:
        outs = [shape((3, length))] + grads
        scratch = [pltpu.VMEM((ROWS, length), F32)]
    scratch += [pltpu.VMEM((9 * channels, length), BF), pltpu.VMEM((9 * channels, length), BF)]
    args = [*windows, *extra, odd, field, first, second, *weights]
    body = functools.partial(backward_kernel, period, layer)
    return kernel_call(body, outs, scratch, args, 2 * 2 * 81 * 64 * 64 * length)


def per_device(noise, w_first, b_first, w_mid, b_mid, w_last, b_last):
    period = noise.shape[3]
    count = lax.axis_size("xy")
    halves = lax.axis_size("gz")
    channels = w_mid.shape[2]
    order = ring_order(count)
    places = np.argsort(np.array(order))
    volume = float(noise.size * count * halves)
    place = jnp.asarray(places, jnp.int32)[lax.axis_index("xy")]
    half = lax.axis_index("gz")

    def step(values, offset):
        return lax.ppermute(
            values, "xy", [(order[(p + offset) % count], order[p]) for p in range(count)]
        )

    flat = noise.reshape(1, -1)
    whole = lax.all_gather(flat, "gz", axis=1, tiled=True)
    length = whole.shape[1]
    near = [
        lax.ppermute(whole, "xy", [((p + d) % count, order[p]) for p in range(count)])
        for d in STEPS
    ]
    near = jnp.concatenate(near, axis=0)
    below = step(near[0:2], -2)
    above = step(near[1:3], 2)
    window = jnp.concatenate([below, near, above, jnp.zeros_like(flat, shape=(1, length))], axis=0)

    lane = lax.broadcasted_iota(jnp.int32, (ROWS, length), 1)
    row = lax.broadcasted_iota(jnp.int32, (ROWS, length), 0)
    within = lane % 128
    odd = ((place + row + 1 + lane // 128 + within // period + within % period) % 2).astype(F32)

    first_spread = jnp.asarray(spread_first(), BF)
    last_spread = jnp.asarray(spread_last(), BF)
    last_back = jnp.asarray(spread_last_back(), BF)
    first_back = jnp.asarray(spread_first_back(), BF)
    ahead_weights, back_weights = [], []
    for layer in range(2):
        wf = w_first[layer, :, :, 0]
        wl = w_last[layer]
        wm = w_mid[layer].reshape(9, 9, channels, channels)
        narrow = jnp.stack(
            [dot(last_spread, wl[27 * dx : 27 * dx + 27].reshape(54, channels)) for dx in range(3)]
        ).astype(BF)
        tail = jnp.zeros((8, 1), F32).at[:2, 0].set(b_last[layer])
        ahead_weights.append((
            lax.dot_general(wf, first_spread, (((0,), (0,)), ((), ())), preferred_element_type=F32).astype(BF),
            b_first[layer][:, None],
            wm.transpose(1, 2, 0, 3).reshape(9 * channels, 9 * channels),
            b_mid[layer][:, None],
            narrow,
            tail,
        ))
        back_weights.append((
            lax.dot_general(
                wl.reshape(162, channels), last_back, (((0,), (0,)), ((), ())),
                preferred_element_type=F32,
            ).astype(BF),
            wm.transpose(1, 3, 0, 2).reshape(9 * channels, 9 * channels),
            dot(first_back, wf).astype(BF),
        ))

    def exchange(values):
        return [values if m == 0 else step(values, m) for m in range(-3, 4)]

    field0, state, first0, second0, logdet0 = forward(
        period, 0, [window], odd, ahead_weights[0], channels
    )
    field1, state, first1, second1, logdet1, growth0 = forward(
        period, 1, exchange(state), odd, ahead_weights[1], channels
    )

    def own_half(values):
        return lax.dynamic_slice_in_dim(values, half * (length // halves), length // halves, axis=1)

    sample = lax.ppermute(
        own_half(state[0:1]), "xy", [(order[p], p) for p in range(count)]
    )
    base, part, action, *grads1 = backward(
        period, 1, exchange(state), [], odd, field1, first1, second1, back_weights[1], channels
    )
    part, *grads0 = backward(
        period, 0, exchange(part), [base, growth0], odd, field0, first0, second0, back_weights[0],
        channels,
    )
    mine = own_half(part)
    force = sum(
        lax.ppermute(mine[d : d + 1], "xy", [(order[p], (p + d - 1) % count) for p in range(count)])
        for d in range(3)
    )
    loss = jnp.sum(action - logdet0 - logdet1)
    pairs = [jnp.stack([a, b]) for a, b in zip(grads0, grads1)]
    loss, pairs = lax.psum((loss, pairs), "xy")
    g_first, gb_first, g_mid, gb_mid, g_last, gb_last = [v / volume for v in pairs]
    g_first = g_first.reshape(2, 27, 8, channels)[:, :, 2:5].transpose(0, 2, 1, 3)
    g_mid = g_mid.reshape(2, 9, channels, 9, channels).transpose(0, 3, 1, 2, 4)
    g_last = g_last.reshape(2, 27, 2, 8, channels)[:, :, :, 4:1:-1].transpose(0, 3, 1, 2, 4)
    return (
        sample.reshape(noise.shape),
        force.reshape(noise.shape),
        loss / volume,
        g_first.reshape(2, 81, channels, 1),
        gb_first[:, :, 0],
        g_mid.reshape(2, 81, channels, channels),
        gb_mid[:, :, 0],
        g_last.reshape(2, 81, 2, channels),
        gb_last[:, :, 0],
    )


def solution(mesh):
    return jax.shard_map(
        per_device,
        mesh=mesh,
        in_specs=(P("xy", "gz", None, None), P(), P(), P(), P(), P(), P()),
        out_specs=(
            P("xy", "gz", None, None),
            P("xy", "gz", None, None),
            P(),
            P(),
            P(),
            P(),
            P(),
            P(),
            P(),
        ),
        check_vma=False,
    )
```

```python
import functools

import jax
import jax.numpy as jnp
import numpy as np
from jax import lax
from jax.experimental import pallas as pl
from jax.experimental.pallas import tpu as pltpu
from jax.sharding import PartitionSpec as P

hopping = 0.3
quartic = 0.05

STEPS = (-1, 0, 1)
ROWS = 8
MID = 3
BF = jnp.bfloat16
F32 = jnp.float32
TAPS = 81


def ring_order(count):
    if count % 4:
        return list(range(count))
    depth = count // 4
    chips = [(z, 0) for z in range(depth)] + [(z, 1) for z in reversed(range(depth))]
    order = []
    for place, (z, y) in enumerate(chips):
        cores = (0, 1) if place % 2 == 0 else (1, 0)
        order += [z * 4 + y * 2 + core for core in cores]
    return order


def spread_first():
    out = np.zeros((81, 5, 256), np.float32)
    for tap in range(81):
        dx, rest = divmod(tap, 27)
        for dest in range(5):
            out[tap, dest, rest * ROWS + dest + dx] = 1
    return out.reshape(81, 5 * 256)


def spread_last():
    out = np.zeros((3, 2, 216, 81), np.float32)
    for tap in range(81):
        dx, rest = divmod(tap, 27)
        for o in range(2):
            out[dx, o, rest * 8 + o, tap] = 1
    return out


def spread_last_back():
    out = np.zeros((2, 81, 3, 512), np.float32)
    for tap in range(81):
        dx, rest = divmod(tap, 27)
        for o in range(2):
            for dest in range(3):
                out[o, tap, dest, rest * 16 + o * ROWS + 2 + dest - (dx - 1)] = 1
    return out.reshape(2, 81, 3 * 512)


def spread_first_back():
    out = np.zeros((216, 81), np.float32)
    for tap in range(81):
        dx, rest = divmod(tap, 27)
        out[rest * 8 + dx, tap] = 1
    return out


def pick_last():
    out = np.zeros((432, 2, 128), np.float32)
    for tap in range(81):
        dx, rest = divmod(tap, 27)
        for o in range(2):
            out[rest * 16 + o * ROWS + MID - (dx - 1), o, tap] = 1
    return out.reshape(432, 256)


def pick_first():
    out = np.zeros((216, 128), np.float32)
    for tap in range(81):
        dx, rest = divmod(tap, 27)
        out[rest * ROWS + MID + dx - 1, tap] = 1
    return out


def z_shift(values, dz):
    length = values.shape[1]
    return values if dz == 0 else pltpu.roll(values, (-dz * 128) % length, 1)


def by_plane(values, fn):
    parts = [fn(values[:, at : at + 128]) for at in range(0, values.shape[1], 128)]
    return parts[0] if len(parts) == 1 else jnp.concatenate(parts, axis=1)


def y_shift(values, dy, period):
    if dy == 0:
        return values
    return by_plane(values, lambda v: pltpu.roll(v, (-dy * period) % 128, 1))


def t_shift(values, dt, period):
    if dt == 0:
        return values

    def one(v):
        place = lax.broadcasted_iota(jnp.int32, v.shape, 1) % period
        main = pltpu.roll(v, (-dt) % 128, 1)
        wrap = pltpu.roll(v, (dt * (period - 1)) % 128, 1)
        return jnp.where(place == (period - 1 if dt == 1 else 0), wrap, main)

    return by_plane(values, one)


def all_shifts(values, sign, period):
    in_t = [t_shift(values, sign * dt, period) for dt in STEPS]
    in_y = [[y_shift(v, sign * dy, period) for v in in_t] for dy in STEPS]
    return [z_shift(in_y[dy][dt], sign * dz) for dz in STEPS for dy in range(3) for dt in range(3)]


def gather_narrow(values, sign, period):
    block = lambda k: values[k * 8 : k * 8 + 8]
    total = None
    for dt in range(3):
        over_y = None
        for dy in range(3):
            over_z = sum(z_shift(block(dz * 9 + dy * 3 + dt), sign * (dz - 1)) for dz in range(3))
            over_z = y_shift(over_z, sign * (dy - 1), period)
            over_y = over_z if over_y is None else over_y + over_z
        over_y = t_shift(over_y, sign * (dt - 1), period)
        total = over_y if total is None else total + over_y
    return total


def gather_wide(values, channels, sign, period):
    block = lambda k: values[k * channels : (k + 1) * channels]
    total = None
    for dt in range(3):
        over_y = None
        for dy in range(3):
            part = y_shift(block(dy * 3 + dt), sign * (dy - 1), period)
            over_y = part if over_y is None else over_y + part
        over_y = t_shift(over_y, sign * (dt - 1), period)
        total = over_y if total is None else total + over_y
    return total


def dot(a, b):
    return jnp.dot(a, b, preferred_element_type=F32)


def dot_nt(a, b):
    return lax.dot_general(a, b, (((1,), (1,)), ((), ())), preferred_element_type=F32)


def stack_planes(stack, planes, channels, order):
    length = stack.shape[1]
    for dx in range(3):
        for dz in range(3):
            plane, step = order(dx, dz)
            rows = pl.ds((dx * 3 + dz) * channels, channels)
            source = planes[plane * channels : (plane + 1) * channels, :]
            if step == 0:
                stack[rows, :] = source
            elif step == 1:
                stack[rows, : length - 128] = source[:, 128:]
                stack[rows, length - 128 :] = source[:, :128]
            else:
                stack[rows, 128:] = source[:, : length - 128]
                stack[rows, :128] = source[:, length - 128 :]


def pack_kernel(w_mid, w_first, w_last, pick_f, pick_l, pick_lb, pick_fb,
                matrix, first, narrow, last_back, first_back, taps):
    channels = w_mid.shape[1]
    for o in range(0, channels, 2):
        pair = w_mid[0, o : o + 2].reshape(2 * channels, TAPS).astype(F32).T
        taps[pl.ds(o, TAPS, stride=channels), :] = pair[:, :channels]
        taps[pl.ds(o + 1, TAPS, stride=channels), :] = pair[:, channels:]
    block = lambda tap: taps[tap * channels : (tap + 1) * channels, :]
    for inner in range(9):
        rows = pl.ds(inner * channels, channels)
        for outer in range(0, 9, 2):
            if outer < 8:
                both = jnp.concatenate([block(outer * 9 + inner), block(outer * 9 + 9 + inner)], axis=1)
                matrix[rows, outer * channels : (outer + 2) * channels] = both.astype(BF)
            else:
                matrix[rows, outer * channels :] = block(outer * 9 + inner).astype(BF)
    wf = w_first[0]
    first[...] = dot(wf, pick_f[...]).astype(BF)
    first_back[...] = dot_nt(pick_fb[...], wf).astype(BF)
    for dx in range(3):
        narrow[dx] = sum(dot_nt(pick_l[dx, o], w_last[0, o]) for o in range(2)).astype(BF)
    last_back[...] = sum(dot(w_last[0, o], pick_lb[o]) for o in range(2)).astype(BF)


def turn_kernel(matrix, turned):
    channels = matrix.shape[0] // 9
    for inner in range(9):
        rows = pl.ds(inner * channels, channels)
        for outer in range(0, 9, 2):
            if outer < 8:
                block = matrix[rows, outer * channels : (outer + 2) * channels].astype(F32).T
                both = jnp.concatenate([block[:channels], block[channels:]], axis=1)
                turned[rows, outer * channels : (outer + 2) * channels] = both.astype(BF)
            else:
                block = matrix[rows, outer * channels :].astype(F32).T
                turned[rows, outer * channels :] = block.astype(BF)


def unpack_kernel(layout, volume, coords, mine, other, *refs):
    g_mid, g_last, g_first, bulk, taps = refs[-5:]
    channels = g_mid.shape[1]
    halves, depth, chunk = layout
    g, c, y, z = (coords[i] for i in range(1, 5))
    for from_core, ref in ((c, mine), (1 - c, other)):
        at = 0
        for rg in range(halves):
            for ry in range(2):
                for rz in range(depth):
                    to = (((lax.rem(g + rg, halves) * 2 + from_core) * 2 + (1 - y if ry else y)) * depth
                          + lax.rem(z + rz, depth)) * chunk
                    bulk[pl.ds(pl.multiple_of(to, 16), chunk), :] = ref[at : at + chunk, :]
                    at += chunk
    rows = 9 * channels
    for tap in range(TAPS):
        outer, inner = divmod(tap, 9)
        start = (outer // 2) * rows + inner * channels
        low = (outer % 2) * channels
        taps[tap * channels : (tap + 1) * channels, :] = (
            bulk[start : start + channels, low : low + channels].astype(F32) * (1.0 / volume)
        )
    for o in range(0, channels, 2):
        pair = jnp.concatenate(
            [taps[pl.ds(o, TAPS, stride=channels), :], taps[pl.ds(o + 1, TAPS, stride=channels), :]],
            axis=1,
        )
        g_mid[0, o : o + 2] = pair.T.reshape(2, channels, TAPS)
    rest = bulk[5 * rows : 5 * rows + 3 * channels, :].astype(F32) * (1.0 / volume)
    for o in range(2):
        g_last[0, o] = rest[o * channels : (o + 1) * channels, :TAPS]
    g_first[0] = rest[2 * channels : 3 * channels, :TAPS]


def place_windows(refs, row, target):
    target[...] = jnp.zeros_like(target)
    for r, ref in enumerate(refs):
        target[r : r + 1, :] = ref[row : row + 1, :]


def oddness(shape, place, period):
    lane = lax.broadcasted_iota(jnp.int32, shape, 1)
    row = lax.broadcasted_iota(jnp.int32, shape, 0)
    within = lane % 128
    return ((place + row + 1 + lane // 128 + within // period + within % period) % 2).astype(F32)


def forward_kernel(period, layer, halves, *refs):
    if layer == 0:
        (coords, below, near, above, w_first, b_first, w_mid, b_mid, w_last, b_last,
         field_out, state, own_out, first_out, second_out, logdet, first, stack) = refs
        field_out[...] = jnp.zeros_like(field_out)
        piece = field_out.shape[1] // halves
        for rel in range(halves):
            to = pl.multiple_of(lax.rem(coords[1] + rel, halves) * piece, 128)
            lanes = slice(rel * piece, (rel + 1) * piece)
            field_out[0:2, pl.ds(to, piece)] = below[0:2, lanes]
            field_out[2:5, pl.ds(to, piece)] = near[0:3, lanes]
            field_out[5:7, pl.ds(to, piece)] = above[1:3, lanes]
    else:
        windows, refs = refs[:7], refs[7:]
        (coords, w_first, b_first, w_mid, b_mid, w_last, b_last,
         field_out, state, own_out, first_out, second_out, logdet, growth_out, first, stack) = refs
        place_windows(windows, 0, field_out)
        place_windows(windows, 1, growth_out)
    channels = w_mid.shape[0] // 9
    field = field_out[...]
    length = field.shape[1]
    frozen = oddness(field.shape, coords[0], period)
    if layer == 1:
        frozen = 1.0 - frozen
    net = frozen * field
    taps = jnp.concatenate(all_shifts(net, 1, period), axis=0).astype(BF)
    for dest in range(5):
        part = dot(w_first[:, dest * 256 : dest * 256 + 216], taps)
        first[dest * channels : (dest + 1) * channels, :] = jnp.tanh(part + b_first[...]).astype(BF)
    first_out[...] = first[channels : 4 * channels, :]
    for dest in range(3):
        stack_planes(stack, first, channels, lambda dx, dz: (dest + dx, dz - 1))
        for at in range(0, length, 256):
            wide = dot(w_mid[...], stack[:, at : at + 256])
            wide = gather_wide(wide, channels, 1, period)
            second_out[dest * channels : (dest + 1) * channels, at : at + 256] = jnp.tanh(
                wide + b_mid[...]
            ).astype(BF)
    narrow = sum(
        dot(w_last[dx], second_out[dx * channels : (dx + 1) * channels, :]) for dx in range(3)
    )
    narrow = gather_narrow(narrow, 1, period) + b_last[...]
    growth = jnp.exp(narrow[0:1])
    mine = field[MID : MID + 1]
    still = frozen[MID : MID + 1]
    moving = 1.0 - still
    state[0:1, :] = still * mine + moving * (mine * growth + narrow[1:2])
    state[1:2, :] = growth
    piece = own_out.shape[1]
    own_out[...] = state[0:1, pl.ds(pl.multiple_of(coords[1] * piece, 128), piece)]
    flow = moving * narrow[0:1]
    logdet[...] = sum(flow[:, at : at + 128] for at in range(0, length, 128))


def backward_kernel(period, layer, layout, *refs):
    windows, refs = refs[:7], refs[7:]
    if layer == 1:
        (logdet0, logdet1, coords, field_in, first_in, second_in, w_last, w_mid, w_first, pick_l, pick_f,
         base_out, part_out, small, send, keep,
         field_end, growth, stack, turned, bulk) = refs
        place_windows(windows, 0, field_end)
        place_windows(windows, 1, growth)
    else:
        (base_in, growth, small_in, coords, field_in, first_in, second_in, w_last, w_mid, w_first,
         pick_l, pick_f,
         part_low, part_mid, part_high, small, send, keep,
         upstream_ref, part_out, stack, turned, bulk) = refs
    channels = w_mid.shape[0] // 9
    length = field_in.shape[1]
    frozen = oddness(field_in.shape, coords[0], period)
    if layer == 1:
        frozen = 1.0 - frozen
    moving = 1.0 - frozen
    place = lax.broadcasted_iota(jnp.int32, (ROWS, length), 0)
    inner = jnp.logical_and(place >= 1, place <= 5)
    if layer == 1:
        field = field_end[...]
        ahead = (
            pltpu.roll(field, ROWS - 1, 0)
            + z_shift(field, 1)
            + y_shift(field, 1, period)
            + t_shift(field, 1, period)
        )
        behind = (
            pltpu.roll(field, 1, 0)
            + z_shift(field, -1)
            + y_shift(field, -1, period)
            + t_shift(field, -1, period)
        )
        squared = field * field
        density = (
            -2.0 * hopping * field * ahead
            + squared
            + quartic * (squared - 1.0) * (squared - 1.0)
        )[MID : MID + 1]
        action = sum(density[:, at : at + 128] for at in range(0, length, 128))
        upstream = (
            -2.0 * hopping * (ahead + behind)
            + 2.0 * field
            + 4.0 * quartic * (squared - 1.0) * field
        )
        upstream = jnp.where(inner, upstream, 0.0)
        small[...] = jnp.zeros_like(small)
        small[3:4, :] = action - logdet0[...] - logdet1[...]
    else:
        upstream_ref[...] = base_in[...]
        for r in range(1, 6):
            upstream_ref[r : r + 1, :] += (
                windows[r - 1][2:3, :] + windows[r][1:2, :] + windows[r + 1][0:1, :]
            )
        upstream = upstream_ref[...]
        small[0:8, :] = jnp.zeros((8, 128), F32)
        small[8:16, :] = small_in[...]
    grow = growth[...]
    grad_scale = upstream * moving * field_in[...] * grow - moving
    grad_shift = upstream * moving
    grad_output = jnp.where(
        jnp.concatenate([inner, inner], axis=0),
        jnp.concatenate([grad_scale, grad_shift], axis=0),
        0.0,
    )
    ones = jnp.ones((8, length), BF)
    sums = dot_nt(ones, grad_output.astype(BF))
    small[2:3, 0:1] = sums[0:1, MID : MID + 1]
    small[2:3, 1:2] = sums[0:1, 8 + MID : 9 + MID]
    taps = jnp.concatenate(all_shifts(grad_output, -1, period), axis=0).astype(BF)
    rows = 9 * channels
    if bulk.shape[0] > 5 * rows + 3 * channels:
        bulk[5 * rows + 3 * channels :, :] = jnp.zeros(
            (bulk.shape[0] - 5 * rows - 3 * channels, 128), BF
        )
    g_last = dot_nt(second_in[channels : 2 * channels, :], taps).astype(BF)
    g_last = dot(g_last, pick_l[...]).astype(BF)
    for o in range(2):
        bulk[5 * rows + o * channels : 5 * rows + (o + 1) * channels, :] = g_last[
            :, o * 128 : (o + 1) * 128
        ]
    mids = []
    for dest in range(3):
        part = dot(w_last[:, dest * 512 : dest * 512 + 432], taps)
        wide = second_in[dest * channels : (dest + 1) * channels, :].astype(F32)
        mids.append((part * (1.0 - wide * wide)).astype(BF))
    small[1:2, 0:channels] = dot_nt(ones, mids[1])[0:1]
    rounded = mids[1].astype(F32)
    in_t = [t_shift(rounded, -dt, period) for dt in STEPS]
    for dy in range(3):
        for dt in range(3):
            turned[(dy * 3 + dt) * channels : (dy * 3 + dt + 1) * channels, :] = y_shift(
                in_t[dt], -STEPS[dy], period
            ).astype(BF)
    stack_planes(stack, first_in, channels, lambda dx, dz: (dx, dz - 1))
    g_mid = dot_nt(turned[...], stack[...]).astype(BF)
    for b in range(5):
        part = g_mid[:, b * 128 : (b + 1) * 128]
        if part.shape[1] < 128:
            part = jnp.concatenate([part, jnp.zeros((rows, 128 - part.shape[1]), BF)], axis=1)
        bulk[b * rows : (b + 1) * rows, :] = part
    planes = jnp.concatenate(mids, axis=0)
    stack_planes(stack, planes, channels, lambda dx, dz: (2 - dx, 1 - dz))
    firsts = []
    for at in range(0, length, 256):
        wide = dot(w_mid[...], stack[:, at : at + 256])
        wide = gather_wide(wide, channels, -1, period)
        seen = first_in[channels : 2 * channels, at : at + 256].astype(F32)
        firsts.append((wide * (1.0 - seen * seen)).astype(BF))
    grad_first = jnp.concatenate(firsts, axis=1)
    small[0:1, 0:channels] = dot_nt(ones, grad_first)[0:1]
    net = frozen * field_in[...]
    taps = jnp.concatenate(all_shifts(net, 1, period), axis=0).astype(BF)
    g_first = dot_nt(grad_first, taps).astype(BF)
    bulk[5 * rows + 2 * channels : 5 * rows + 3 * channels, :] = dot(g_first, pick_f[...]).astype(BF)
    narrow = gather_narrow(dot(w_first[...], grad_first), -1, period)
    base = upstream * (frozen + moving * grow)
    for d in range(3):
        row = frozen[MID - 1 + d : MID + d] * narrow[d : d + 1]
        if layer == 0 and d == 1:
            row = row + base[MID : MID + 1]
        part_out[d : d + 1, :] = row
    if layer == 1:
        base_out[...] = base
    else:
        piece = part_low.shape[1]
        lanes = pl.ds(pl.multiple_of(coords[1] * piece, 128), piece)
        for d, ref in enumerate((part_low, part_mid, part_high)):
            ref[...] = part_out[d : d + 1, lanes]
    halves, depth, chunk = layout
    g, c, y, z = (coords[i] for i in range(1, 5))
    for core, ref in ((c, keep), (1 - c, send)):
        at = 0
        for ry in range(2):
            for rz in range(depth):
                source = (((g * 2 + core) * 2 + (1 - y if ry else y)) * depth
                          + lax.rem(z + rz, depth)) * chunk
                ref[at : at + chunk, :] = bulk[pl.ds(pl.multiple_of(source, 16), chunk), :]
                at += chunk


SMEM = pl.BlockSpec(memory_space=pltpu.SMEM)
VMEM = pl.BlockSpec(memory_space=pltpu.VMEM)


def kernel_call(body, outs, scratch, args, flops, small=None):
    return pl.pallas_call(
        body,
        out_shape=tuple(outs),
        in_specs=[SMEM if a is small else VMEM for a in args],
        out_specs=tuple([VMEM] * len(outs)),
        scratch_shapes=scratch,
        compiler_params=pltpu.CompilerParams(vmem_limit_bytes=52 * 2**20),
        cost_estimate=pl.CostEstimate(flops=flops, bytes_accessed=4_000_000, transcendentals=500_000),
    )(*args)


def shape(dims, dtype=F32):
    return jax.ShapeDtypeStruct(dims, dtype)


def forward(period, layer, windows, coords, weights, channels, halves):
    length = windows[0].shape[1]
    outs = [
        shape((ROWS, length)),
        shape((2, length)),
        shape((1, length // halves)),
        shape((3 * channels, length), BF),
        shape((3 * channels, length), BF),
        shape((1, 128)),
    ]
    scratch = [
        pltpu.VMEM((5 * channels, length), BF),
        pltpu.VMEM((9 * channels, length), BF),
    ]
    if layer == 1:
        outs.append(shape((ROWS, length)))
        args = [*windows, coords, *weights]
    else:
        args = [coords, *windows, *weights]
    body = functools.partial(forward_kernel, period, layer, halves)
    return kernel_call(body, outs, scratch, args, 3 * 2 * 81 * 64 * 64 * length, coords)


def backward(period, layer, layout, windows, extra, coords, field, first, second, weights, channels):
    length = field.shape[1]
    halves, depth, chunk = layout
    part = 2 * depth * chunk
    if layer == 1:
        outs = [shape((ROWS, length)), shape((3, length)), shape((8, 128))]
        scratch = [pltpu.VMEM((ROWS, length), F32), pltpu.VMEM((ROWS, length), F32)]
    else:
        outs = [shape((1, length // halves))] * 3 + [shape((16, 128))]
        scratch = [pltpu.VMEM((ROWS, length), F32), pltpu.VMEM((ROWS, length), F32)]
    outs += [shape((part, 128), BF)] * 2
    scratch += [
        pltpu.VMEM((9 * channels, length), BF),
        pltpu.VMEM((9 * channels, length), BF),
        pltpu.VMEM((part * 2 * halves, 128), BF),
    ]
    args = [*windows, *extra, coords, field, first, second, *weights]
    body = functools.partial(backward_kernel, period, layer, layout)
    return kernel_call(body, outs, scratch, args, 2 * 2 * 81 * 64 * 64 * length, coords)


def pack(layer, w_mid, w_first, w_last, picks):
    channels = w_mid.shape[1]
    whole = lambda a: pl.BlockSpec(a.shape, lambda i: (0,) * len(a.shape))
    one = lambda a: pl.BlockSpec((1,) + a.shape[1:], lambda i: (layer,) + (0,) * (len(a.shape) - 1))
    outs = (
        shape((9 * channels, 9 * channels), BF),
        shape((channels, 5 * 256), BF),
        shape((3, 216, channels), BF),
        shape((channels, 3 * 512), BF),
        shape((216, channels), BF),
    )
    return pl.pallas_call(
        pack_kernel,
        grid=(1,),
        out_shape=outs,
        in_specs=[one(w_mid), one(w_first), one(w_last)] + [whole(a) for a in picks],
        out_specs=tuple(whole(a) for a in outs),
        scratch_shapes=[pltpu.VMEM((TAPS * channels, channels), F32)],
        compiler_params=pltpu.CompilerParams(vmem_limit_bytes=40 * 2**20),
        cost_estimate=pl.CostEstimate(flops=2_000_000_000, bytes_accessed=8_000_000, transcendentals=0),
    )(w_mid, w_first, w_last, *picks)


def unpack(layer, layout, volume, coords, mine, other, channels, before):
    halves, depth, chunk = layout
    rows = 4 * halves * depth * chunk
    outs = (
        shape((2, channels, channels, TAPS)),
        shape((2, 2, channels, TAPS)),
        shape((2, channels, TAPS)),
    )
    block = lambda a: pl.BlockSpec(
        (1,) + a.shape[1:], lambda i: (layer,) + (0,) * (len(a.shape) - 1)
    )
    whole = lambda a: pl.BlockSpec(a.shape, lambda i: (0,) * len(a.shape))
    return pl.pallas_call(
        functools.partial(unpack_kernel, layout, volume),
        grid=(1,),
        out_shape=outs,
        in_specs=[SMEM, whole(mine), whole(other)] + [pl.BlockSpec(memory_space=pl.ANY)] * len(before),
        out_specs=tuple(block(a) for a in outs),
        scratch_shapes=[pltpu.VMEM((rows, 128), BF), pltpu.VMEM((TAPS * channels, channels), F32)],
        input_output_aliases={3 + i: i for i in range(len(before))},
        compiler_params=pltpu.CompilerParams(vmem_limit_bytes=40 * 2**20),
        cost_estimate=pl.CostEstimate(flops=2_000_000_000, bytes_accessed=8_000_000, transcendentals=0),
    )(coords, mine, other, *before)


def add(*parts):
    return sum(p.astype(F32) for p in parts).astype(BF)


def sum_gradients(send, keep, layout, count):
    halves, depth, chunk = layout
    xy = lambda fn: [(fn(a), a) for a in range(count)]
    core = xy(lambda a: a ^ 1)
    got = lax.ppermute(send, "xy", core)
    half = depth * chunk
    away = add(keep[half:], got[half:])
    stay = add(keep[:half], got[:half])
    got = lax.ppermute(away, "xy", xy(lambda a: a ^ 2))
    pieces = [
        add(stay[s * chunk : (s + 1) * chunk], got[s * chunk : (s + 1) * chunk]) for s in range(depth)
    ]
    got = [
        lax.ppermute(pieces[s], "xy", xy(lambda a, s=s: (a - 4 * s) % count)) for s in range(1, depth)
    ]
    total = add(pieces[0], *got)
    line = [total] + [
        lax.ppermute(total, "xy", xy(lambda a, s=s: (a + 4 * s) % count)) for s in range(1, depth)
    ]
    line = jnp.concatenate(line, axis=0)
    square = []
    for rg in range(halves):
        for ry in range(2):
            if rg == 0 and ry == 0:
                square.append(line)
                continue
            pairs = [
                ((a ^ (2 * ry)) * halves + (j + rg) % halves, a * halves + j)
                for a in range(count)
                for j in range(halves)
            ]
            square.append(lax.ppermute(line, ("xy", "gz"), pairs))
    square = jnp.concatenate(square, axis=0)
    return square, lax.ppermute(square, "xy", core)


def per_device(noise, w_first, b_first, w_mid, b_mid, w_last, b_last):
    period = noise.shape[3]
    count = lax.axis_size("xy")
    halves = lax.axis_size("gz")
    channels = w_mid.shape[2]
    order = ring_order(count)
    places = np.argsort(np.array(order))
    volume = float(noise.size * count * halves)
    index = lax.axis_index("xy")
    depth = count // 4
    coords = jnp.stack(
        [
            jnp.asarray(places, jnp.int32)[index],
            lax.axis_index("gz"),
            index % 2,
            index // 2 % 2,
            index // 4,
        ]
    ).astype(jnp.int32)
    need = 45 * channels + 3 * channels
    chunk = -(-need // (4 * halves * depth * 16)) * 16
    layout = (halves, depth, chunk)

    def step(values, offset):
        return lax.ppermute(
            values, "xy", [(order[(p + offset) % count], order[p]) for p in range(count)]
        )

    flat = noise.reshape(1, -1)
    near = []
    for d in STEPS:
        parts = []
        for rel in range(halves):
            pairs = [
                ((p + d) % count * halves + (j + rel) % halves, order[p] * halves + j)
                for p in range(count)
                for j in range(halves)
            ]
            parts.append(lax.ppermute(flat, ("xy", "gz"), pairs))
        near.append(jnp.concatenate(parts, axis=1))
    near = jnp.concatenate(near, axis=0)
    noises = [step(near, -2), near, step(near, 2)]

    mid = w_mid.transpose(0, 2, 3, 1)
    firsts = w_first.transpose(0, 2, 3, 1).reshape(2, channels, TAPS)
    lasts = w_last.transpose(0, 2, 3, 1)
    picks = [
        jnp.asarray(fn(), BF) for fn in (spread_first, spread_last, spread_last_back, spread_first_back)
    ]
    pick_l, pick_f = jnp.asarray(pick_last(), BF), jnp.asarray(pick_first(), BF)
    ahead_weights, back_weights = [], []
    for layer in range(2):
        matrix, first, narrow, last_back, first_back = pack(layer, mid, firsts, lasts, picks)
        (turned,) = kernel_call(
            turn_kernel, [shape(matrix.shape, BF)], [], [matrix], 1_000_000_000
        )
        tail = jnp.pad(b_last[layer][:, None], ((0, 6), (0, 0)))
        ahead_weights.append(
            (first, b_first[layer][:, None], matrix, b_mid[layer][:, None], narrow, tail)
        )
        back_weights.append((last_back, turned, first_back, pick_l, pick_f))

    def exchange(values):
        return [values if m == 0 else step(values, m) for m in range(-3, 4)]

    field0, state, _, first0, second0, logdet0 = forward(
        period, 0, noises, coords, ahead_weights[0], channels, halves
    )
    field1, state, own, first1, second1, logdet1, growth0 = forward(
        period, 1, exchange(state), coords, ahead_weights[1], channels, halves
    )
    sample = lax.ppermute(own, "xy", [(order[p], p) for p in range(count)])
    base, part, small, send1, keep1 = backward(
        period, 1, layout, exchange(state), [logdet0, logdet1], coords, field1, first1, second1,
        back_weights[1], channels,
    )
    *mine, small, send0, keep0 = backward(
        period, 0, layout, exchange(part), [base, growth0, small], coords, field0, first0, second0,
        back_weights[0], channels,
    )
    force = sum(
        lax.ppermute(mine[d], "xy", [(order[p], (p + d - 1) % count) for p in range(count)])
        for d in range(3)
    )
    outs = unpack(1, layout, volume, coords, *sum_gradients(send1, keep1, layout, count), channels, [])
    jump = 1
    while jump < count:
        small = small + lax.ppermute(small, "xy", [(a ^ jump, a) for a in range(count)])
        jump *= 2
    g_mid, g_last, g_first = unpack(
        0, layout, volume, coords, *sum_gradients(send0, keep0, layout, count), channels, list(outs)
    )
    small = small.reshape(2, 8, 128) / volume
    return (
        sample.reshape(noise.shape),
        force.reshape(noise.shape),
        jnp.sum(small[1, 3]),
        g_first.reshape(2, channels, 1, TAPS).transpose(0, 3, 1, 2),
        small[:, 0, :channels],
        g_mid.transpose(0, 3, 1, 2),
        small[:, 1, :channels],
        g_last.transpose(0, 3, 1, 2),
        small[:, 2, :2],
    )


def solution(mesh):
    return jax.shard_map(
        per_device,
        mesh=mesh,
        in_specs=(P("xy", "gz", None, None), P(), P(), P(), P(), P(), P()),
        out_specs=(
            P("xy", "gz", None, None),
            P("xy", "gz", None, None),
            P(),
            P(),
            P(),
            P(),
            P(),
            P(),
            P(),
        ),
        check_vma=False,
    )
```

```python
import functools

import jax
import jax.numpy as jnp
import numpy as np
from jax import lax
from jax.experimental import pallas as pl
from jax.experimental.pallas import tpu as pltpu
from jax.sharding import PartitionSpec as P

hopping = 0.3
quartic = 0.05

STEPS = (-1, 0, 1)
ROWS = 8
MID = 3
BF = jnp.bfloat16
F32 = jnp.float32
TAPS = 81
VMEM_MB = 20


def ring_order(count):
    if count % 4:
        return list(range(count))
    depth = count // 4
    chips = [(z, 0) for z in range(depth)] + [(z, 1) for z in reversed(range(depth))]
    order = []
    for place, (z, y) in enumerate(chips):
        cores = (0, 1) if place % 2 == 0 else (1, 0)
        order += [z * 4 + y * 2 + core for core in cores]
    return order


def spread_first():
    out = np.zeros((81, 5, 256), np.float32)
    for tap in range(81):
        dx, rest = divmod(tap, 27)
        for dest in range(5):
            out[tap, dest, rest * ROWS + dest + dx] = 1
    return out.reshape(81, 5 * 256)


def spread_last():
    out = np.zeros((3, 2, 216, 81), np.float32)
    for tap in range(81):
        dx, rest = divmod(tap, 27)
        for o in range(2):
            out[dx, o, rest * 8 + o, tap] = 1
    return out


def spread_last_back():
    out = np.zeros((2, 81, 3, 512), np.float32)
    for tap in range(81):
        dx, rest = divmod(tap, 27)
        for o in range(2):
            for dest in range(3):
                out[o, tap, dest, rest * 16 + o * ROWS + 2 + dest - (dx - 1)] = 1
    return out.reshape(2, 81, 3 * 512)


def spread_first_back():
    out = np.zeros((216, 81), np.float32)
    for tap in range(81):
        dx, rest = divmod(tap, 27)
        out[rest * 8 + dx, tap] = 1
    return out


def pick_last():
    out = np.zeros((432, 2, 128), np.float32)
    for tap in range(81):
        dx, rest = divmod(tap, 27)
        for o in range(2):
            out[rest * 16 + o * ROWS + MID - (dx - 1), o, tap] = 1
    return out.reshape(432, 256)


def pick_first():
    out = np.zeros((216, 128), np.float32)
    for tap in range(81):
        dx, rest = divmod(tap, 27)
        out[rest * ROWS + MID + dx - 1, tap] = 1
    return out


def z_shift(values, dz):
    length = values.shape[1]
    return values if dz == 0 else pltpu.roll(values, (-dz * 128) % length, 1)


def by_plane(values, fn):
    parts = [fn(values[:, at : at + 128]) for at in range(0, values.shape[1], 128)]
    return parts[0] if len(parts) == 1 else jnp.concatenate(parts, axis=1)


def y_shift(values, dy, period):
    if dy == 0:
        return values
    return by_plane(values, lambda v: pltpu.roll(v, (-dy * period) % 128, 1))


def t_shift(values, dt, period):
    if dt == 0:
        return values

    def one(v):
        place = lax.broadcasted_iota(jnp.int32, v.shape, 1) % period
        main = pltpu.roll(v, (-dt) % 128, 1)
        wrap = pltpu.roll(v, (dt * (period - 1)) % 128, 1)
        return jnp.where(place == (period - 1 if dt == 1 else 0), wrap, main)

    return by_plane(values, one)


def all_shifts(values, sign, period):
    in_t = [t_shift(values, sign * dt, period) for dt in STEPS]
    in_y = [[y_shift(v, sign * dy, period) for v in in_t] for dy in STEPS]
    return [z_shift(in_y[dy][dt], sign * dz) for dz in STEPS for dy in range(3) for dt in range(3)]


def gather_narrow(values, sign, period):
    block = lambda k: values[k * 8 : k * 8 + 8]
    total = None
    for dt in range(3):
        over_y = None
        for dy in range(3):
            over_z = sum(z_shift(block(dz * 9 + dy * 3 + dt), sign * (dz - 1)) for dz in range(3))
            over_z = y_shift(over_z, sign * (dy - 1), period)
            over_y = over_z if over_y is None else over_y + over_z
        over_y = t_shift(over_y, sign * (dt - 1), period)
        total = over_y if total is None else total + over_y
    return total


def gather_wide(values, channels, sign, period):
    block = lambda k: values[k * channels : (k + 1) * channels]
    total = None
    for dt in range(3):
        over_y = None
        for dy in range(3):
            part = y_shift(block(dy * 3 + dt), sign * (dy - 1), period)
            over_y = part if over_y is None else over_y + part
        over_y = t_shift(over_y, sign * (dt - 1), period)
        total = over_y if total is None else total + over_y
    return total


def dot(a, b):
    return jnp.dot(a, b, preferred_element_type=F32)


def dot_nt(a, b):
    return lax.dot_general(a, b, (((1,), (1,)), ((), ())), preferred_element_type=F32)


def stack_planes(stack, planes, channels, order):
    length = stack.shape[1]
    for dx in range(3):
        for dz in range(3):
            plane, step = order(dx, dz)
            rows = pl.ds((dx * 3 + dz) * channels, channels)
            source = planes[plane * channels : (plane + 1) * channels, :]
            if step == 0:
                stack[rows, :] = source
            elif step == 1:
                stack[rows, : length - 128] = source[:, 128:]
                stack[rows, length - 128 :] = source[:, :128]
            else:
                stack[rows, 128:] = source[:, : length - 128]
                stack[rows, :128] = source[:, length - 128 :]


def pack_kernel(layer, ready, w_mid, w_first, w_last, b_first, b_mid, b_last, lanes, rows_81,
                matrix, first, narrow, last_back, first_back, turned, columns, taps, rows):
    channels = w_mid.shape[1]
    for o in range(0, channels, 2):
        pair = w_mid[layer, o : o + 2].reshape(2 * channels, TAPS).astype(F32).T
        taps[pl.ds(o, TAPS, stride=channels), :] = pair[:, :channels]
        taps[pl.ds(o + 1, TAPS, stride=channels), :] = pair[:, channels:]
    block = lambda tap: taps[tap * channels : (tap + 1) * channels, :]
    for inner in range(9):
        at = pl.ds(inner * channels, channels)
        for outer in range(0, 9, 2):
            low = block(outer * 9 + inner)
            if outer < 8:
                high = block(outer * 9 + 9 + inner)
                wide = slice(outer * channels, (outer + 2) * channels)
                matrix[at, wide] = jnp.concatenate([low, high], axis=1).astype(BF)
            else:
                matrix[at, outer * channels :] = low.astype(BF)
    for inner in range(9):
        at = pl.ds(inner * channels, channels)
        for outer in range(0, 9, 2):
            if outer < 8:
                wide = slice(outer * channels, (outer + 2) * channels)
                both = matrix[at, wide].astype(F32).T
                turned[at, wide] = jnp.concatenate([both[:channels], both[channels:]], axis=1).astype(BF)
            else:
                turned[at, outer * channels :] = matrix[at, outer * channels :].astype(F32).T.astype(BF)
    wf = w_first[layer]
    first[...] = dot(wf, lanes[:, : 5 * 256]).astype(BF)
    first_back[...] = dot_nt(rows_81[6 * 216 : 7 * 216, :TAPS], wf).astype(BF)
    for dx in range(3):
        narrow[dx] = sum(
            dot_nt(rows_81[(dx * 2 + o) * 216 : (dx * 2 + o + 1) * 216, :TAPS], w_last[layer, o])
            for o in range(2)
        ).astype(BF)
    last_back[...] = sum(
        dot(w_last[layer, o], lanes[:, 5 * 256 + o * 1536 : 5 * 256 + (o + 1) * 1536]) for o in range(2)
    ).astype(BF)
    rows[...] = jnp.zeros_like(rows)
    rows[0:1, :channels] = b_first[layer : layer + 1, :]
    rows[1:2, :channels] = b_mid[layer : layer + 1, :]
    rows[2:3, :2] = b_last[layer : layer + 1, :]
    columns[...] = rows[...].T


def unpack_kernel(layout, volume, last, ready, coords, pieces, *refs):
    if last:
        refs = refs[3:]
        g_mid, g_last, g_first, gb_first, gb_mid, gb_last, loss = refs[:7]
        bulk, taps, mid, lasts, firsts, sems = refs[7:]
    else:
        g_mid, g_last, g_first = refs[:3]
        bulk, taps, mid, lasts, firsts, sems = refs[3:]
    channels = g_mid.shape[2]
    few = channels // 2
    halves, depth, chunk = layout
    g, y, z = coords[1], coords[3], coords[4]
    core = 1 - coords[2] if last else coords[2]
    per_layer = 2 * halves * depth * chunk
    at = 0
    for rg in range(halves):
        for ry in range(2):
            for rz in range(depth):
                to = ((lax.rem(g + rg, halves) * 2 + (1 - y if ry else y)) * depth
                      + lax.rem(z + rz, depth)) * chunk
                for layer in range(2):
                    bulk[layer, pl.ds(pl.multiple_of(to, 16), chunk), :] = pieces[at : at + chunk, :]
                    at += chunk
    rows = 9 * few
    copies = []
    for layer in range(2):
        for tap in range(TAPS):
            outer, inner = divmod(tap, 9)
            start = (outer // 2) * rows + inner * few
            low = (outer % 2) * channels
            taps[tap * few : (tap + 1) * few, :] = (
                bulk[layer, start : start + few, low : low + channels].astype(F32) * (1.0 / volume)
            )
        for o in range(0, few, 2):
            pair = jnp.concatenate(
                [taps[pl.ds(o, TAPS, stride=few), :], taps[pl.ds(o + 1, TAPS, stride=few), :]],
                axis=1,
            )
            mid[layer, o : o + 2] = pair.T.reshape(2, channels, TAPS)
        rest = bulk[layer, 5 * rows : 5 * rows + channels + few, :].astype(F32) * (1.0 / volume)
        lasts[layer] = rest[:channels, :TAPS]
        firsts[layer] = rest[channels:, :TAPS]
        if last:
            small = bulk[layer, 4 * rows : 4 * rows + 16, channels:].astype(F32) * (1.0 / volume)
            gb_first[layer : layer + 1, :] = small[0:1]
            gb_mid[layer : layer + 1, :] = small[1:2]
            gb_last[layer : layer + 1, :] = small[2:3, :2]
            if layer == 1:
                loss[...] = jnp.sum(
                    jnp.sum(small[3:6], axis=0, keepdims=True), axis=1, keepdims=True
                )
        copies += [
            pltpu.make_async_copy(
                mid.at[layer], g_mid.at[layer, pl.ds(core * few, few)], sems.at[layer * 3]
            ),
            pltpu.make_async_copy(lasts.at[layer], g_last.at[layer, core], sems.at[layer * 3 + 1]),
            pltpu.make_async_copy(
                firsts.at[layer],
                g_first.at[layer, pl.ds(pl.multiple_of(core * few, few), few)],
                sems.at[layer * 3 + 2],
            ),
        ]
        for copy in copies[-3:]:
            copy.start()
    for copy in copies:
        copy.wait()


def place_windows(refs, row, target):
    target[...] = jnp.zeros_like(target)
    for r, ref in enumerate(refs):
        target[r : r + 1, :] = ref[row : row + 1, :]


def oddness(shape, place, period):
    lane = lax.broadcasted_iota(jnp.int32, shape, 1)
    row = lax.broadcasted_iota(jnp.int32, shape, 0)
    within = lane % 128
    return ((place + row + 1 + lane // 128 + within // period + within % period) % 2).astype(F32)


def forward_kernel(period, layer, halves, ready, *refs):
    windows, refs = refs[:7], refs[7:]
    if layer == 0:
        (coords, w_first, w_mid, w_last, columns,
         field_out, state, own_out, logdet, first_out, second_out, first, stack) = refs
        field_out[...] = jnp.zeros_like(field_out)
        piece = field_out.shape[1] // halves
        for rel in range(halves):
            to = pl.multiple_of(lax.rem(coords[1] + rel, halves) * piece, 128)
            for r, ref in enumerate(windows):
                field_out[r : r + 1, pl.ds(to, piece)] = ref[:, rel * piece : (rel + 1) * piece]
    else:
        (coords, w_first, w_mid, w_last, columns,
         field_out, state, own_out, logdet, growth_out, first_out, second_out,
         first, stack) = refs
        place_windows(windows, 0, field_out)
        place_windows(windows, 1, growth_out)
    channels = w_mid.shape[0] // 9
    field = field_out[...]
    length = field.shape[1]
    frozen = oddness(field.shape, coords[0], period)
    if layer == 1:
        frozen = 1.0 - frozen
    net = frozen * field
    taps = jnp.concatenate(all_shifts(net, 1, period), axis=0).astype(BF)
    ready(w_first, columns)
    bias_first, bias_mid = columns[:channels, 0:1], columns[:channels, 1:2]
    for dest in range(5):
        part = dot(w_first[:, dest * 256 : dest * 256 + 216], taps)
        first[dest * channels : (dest + 1) * channels, :] = jnp.tanh(part + bias_first).astype(BF)
    first_out[...] = first[channels : 4 * channels, :]
    ready(w_mid)
    for dest in range(3):
        stack_planes(stack, first, channels, lambda dx, dz: (dest + dx, dz - 1))
        for at in range(0, length, 256):
            wide = dot(w_mid[...], stack[:, at : at + 256])
            wide = gather_wide(wide, channels, 1, period)
            second_out[dest * channels : (dest + 1) * channels, at : at + 256] = jnp.tanh(
                wide + bias_mid
            ).astype(BF)
    ready(w_last)
    narrow = sum(
        dot(w_last[dx], second_out[dx * channels : (dx + 1) * channels, :]) for dx in range(3)
    )
    narrow = gather_narrow(narrow, 1, period) + columns[:8, 2:3]
    growth = jnp.exp(narrow[0:1])
    mine = field[MID : MID + 1]
    still = frozen[MID : MID + 1]
    moving = 1.0 - still
    state[0:1, :] = still * mine + moving * (mine * growth + narrow[1:2])
    state[1:2, :] = growth
    own_out[...] = state[0:1, :]
    flow = moving * narrow[0:1]
    logdet[...] = sum(flow[:, at : at + 128] for at in range(0, length, 128))


def put_chunks(layout, coords, bulks, send, keep):
    halves, depth, chunk = layout
    per_core = bulks[0].shape[0] // 2
    g, c, y, z = (coords[i] for i in range(1, 5))
    for core, ref in ((c, keep), (1 - c, send)):
        at = 0
        for ry in range(2):
            for rz in range(depth):
                source = core * per_core + (
                    (g * 2 + (1 - y if ry else y)) * depth + lax.rem(z + rz, depth)
                ) * chunk
                for bulk in bulks:
                    ref[at : at + chunk, :] = bulk[pl.ds(pl.multiple_of(source, 16), chunk), :]
                    at += chunk


def output_taps(grad_output, period):
    return jnp.concatenate(all_shifts(grad_output, -1, period), axis=0).astype(BF)


def output_gradient(upstream, moving, field, grow):
    place = lax.broadcasted_iota(jnp.int32, (2 * ROWS, field.shape[1]), 0) % ROWS
    grad_scale = upstream * moving * field * grow - moving
    grad_shift = upstream * moving
    both = jnp.concatenate([grad_scale, grad_shift], axis=0)
    return jnp.where(jnp.logical_and(place >= 1, place <= 5), both, 0.0)


def second_gradient(w_last, second, taps, mids):
    channels = mids.shape[0] // 3
    for dest in range(3):
        part = dot(w_last[:, dest * 512 : dest * 512 + 432], taps)
        rows = slice(dest * channels, (dest + 1) * channels)
        wide = second[rows, :].astype(F32)
        mids[rows, :] = (part * (1.0 - wide * wide)).astype(BF)


def first_gradient(period, mids, first, w_mid, stack, grad_first):
    channels = mids.shape[0] // 3
    stack_planes(stack, mids, channels, lambda dx, dz: (2 - dx, 1 - dz))
    for at in range(0, stack.shape[1], 256):
        wide = dot(w_mid[...], stack[:, at : at + 256])
        wide = gather_wide(wide, channels, -1, period)
        seen = first[channels : 2 * channels, at : at + 256].astype(F32)
        grad_first[:, at : at + 256] = (wide * (1.0 - seen * seen)).astype(BF)


def first_weights(period, net, grad_first, pick_f):
    taps = jnp.concatenate(all_shifts(net, 1, period), axis=0).astype(BF)
    g_first = dot_nt(grad_first, taps).astype(BF)
    return dot(g_first, pick_f)


def fill_bulk(period, mids, first, second, taps, pick_l, g_first, small, stack, turned, bulk):
    channels = mids.shape[0] // 3
    few = channels // 2
    own = slice(channels, 2 * channels)
    rounded = mids[own, :].astype(F32)
    in_t = [t_shift(rounded, -dt, period) for dt in STEPS]
    for dy in range(3):
        for dt in range(3):
            turned[(dy * 3 + dt) * channels : (dy * 3 + dt + 1) * channels, :] = y_shift(
                in_t[dt], -STEPS[dy], period
            ).astype(BF)
    stack_planes(stack, first, channels, lambda dx, dz: (dx, dz - 1))
    g_mid = dot_nt(turned[...], stack[...]).astype(BF)
    per_core = bulk.shape[0] // 2
    rows = 9 * few
    g_last = dot_nt(second[own, :], taps).astype(BF)
    g_last = dot(g_last, pick_l).astype(BF)
    for core in range(2):
        base = core * per_core
        for b in range(5):
            for inner in range(9):
                at = inner * channels + core * few
                part = g_mid[at : at + few, b * 128 : (b + 1) * 128]
                if part.shape[1] < 128:
                    part = jnp.concatenate([part, jnp.zeros((few, 128 - part.shape[1]), BF)], axis=1)
                to = base + b * rows + inner * few
                bulk[to : to + few, :] = part
        at = base + 4 * rows
        bulk[at : at + 16, channels:] = small.astype(BF)
        at = base + 5 * rows
        bulk[at : at + channels, :] = g_last[:, core * 128 : (core + 1) * 128]
        bulk[at + channels : at + channels + few, :] = g_first[core * few : (core + 1) * few, :].astype(BF)
        at += channels + few
        if at < base + per_core:
            bulk[at : base + per_core, :] = jnp.zeros((base + per_core - at, 128), BF)


def bias_rows(small, grad_output, mids, grad_first):
    channels = mids.shape[0] // 3
    ones = jnp.ones((8, mids.shape[1]), BF)
    small[0:1, :] = dot_nt(ones, grad_first)[0:1]
    small[1:2, :] = dot_nt(ones, mids[channels : 2 * channels, :])[0:1]
    sums = dot_nt(ones, grad_output.astype(BF))
    small[2:3, 0:1] = sums[0:1, MID : MID + 1]
    small[2:3, 1:2] = sums[0:1, 8 + MID : 9 + MID]


def back_one_kernel(period, ready, *refs):
    windows, refs = refs[:7], refs[7:]
    (logdet0, logdet1, coords, field_in, first_in, second_in, w_last, w_mid, w_first,
     base_out, part_out, small, grad_out, mids, grad_first, field_end, growth, stack) = refs
    place_windows(windows, 0, field_end)
    place_windows(windows, 1, growth)
    frozen = 1.0 - oddness(field_in.shape, coords[0], period)
    moving = 1.0 - frozen
    field = field_end[...]
    ahead = (
        pltpu.roll(field, ROWS - 1, 0)
        + z_shift(field, 1)
        + y_shift(field, 1, period)
        + t_shift(field, 1, period)
    )
    behind = (
        pltpu.roll(field, 1, 0)
        + z_shift(field, -1)
        + y_shift(field, -1, period)
        + t_shift(field, -1, period)
    )
    squared = field * field
    density = (
        -2.0 * hopping * field * ahead + squared + quartic * (squared - 1.0) * (squared - 1.0)
    )[MID : MID + 1]
    action = sum(density[:, at : at + 128] for at in range(0, field.shape[1], 128))
    loss = jnp.sum(action - logdet0[...] - logdet1[...], axis=1, keepdims=True)
    small[...] = jnp.zeros_like(small)
    slot = lax.broadcasted_iota(jnp.int32, (1, small.shape[1]), 1) == coords[0]
    for part in range(3):
        top = loss.astype(BF).astype(F32)
        small[3 + part : 4 + part, :] = jnp.where(slot, top, 0.0)
        loss = loss - top
    place = lax.broadcasted_iota(jnp.int32, field.shape, 0)
    upstream = (
        -2.0 * hopping * (ahead + behind) + 2.0 * field + 4.0 * quartic * (squared - 1.0) * field
    )
    upstream = jnp.where(jnp.logical_and(place >= 1, place <= 5), upstream, 0.0)
    grow = growth[...]
    grad_out[...] = output_gradient(upstream, moving, field_in[...], grow)
    base_out[...] = upstream * (frozen + moving * grow)
    taps = output_taps(grad_out[...], period)
    ready(w_last, second_in)
    second_gradient(w_last, second_in, taps, mids)
    ready(w_mid, first_in)
    first_gradient(period, mids, first_in, w_mid, stack, grad_first)
    bias_rows(small, grad_out[...], mids, grad_first[...])
    ready(w_first)
    narrow = gather_narrow(dot(w_first[...], grad_first[...]), -1, period)
    for d in range(3):
        part_out[d : d + 1, :] = frozen[MID - 1 + d : MID + d] * narrow[d : d + 1]


def weights_one_kernel(period, ready, coords, field_in, first_in, second_in, grad_out, mids, grad_first, small,
                       pick_l, pick_f, bulk, stack, turned):
    taps = output_taps(grad_out[...], period)
    frozen = 1.0 - oddness(field_in.shape, coords[0], period)
    ready(first_in, second_in, pick_l, pick_f)
    g_first = first_weights(period, frozen * field_in[...], grad_first[...], pick_f[...])
    fill_bulk(
        period, mids, first_in, second_in, taps, pick_l[...], g_first, small[...], stack, turned, bulk
    )


def back_zero_kernel(period, layout, ready, *refs):
    windows, refs = refs[:7], refs[7:]
    (base_in, growth, own_in, coords, field_in, bulk_one, first_in, second_in, w_last, w_mid, w_first,
     pick_l, pick_f,
     part_low, part_mid, part_high, send, keep,
     upstream_ref, mids, stack, turned, bulk, grad_first, small) = refs
    frozen = oddness(field_in.shape, coords[0], period)
    upstream_ref[...] = base_in[...]
    for r in range(1, 6):
        upstream_ref[r : r + 1, :] += (
            windows[r - 1][2:3, :] + windows[r][1:2, :] + windows[r + 1][0:1, :]
        )
    grad_output = output_gradient(upstream_ref[...], 1.0 - frozen, field_in[...], growth[...])
    taps = output_taps(grad_output, period)
    ready(w_last, second_in)
    second_gradient(w_last, second_in, taps, mids)
    ready(w_mid, first_in)
    first_gradient(period, mids, first_in, w_mid, stack, grad_first)
    small[...] = jnp.zeros_like(small)
    bias_rows(small, grad_output, mids, grad_first[...])
    ready(w_first, pick_f, pick_l)
    g_first = first_weights(period, frozen * field_in[...], grad_first[...], pick_f[...])
    fill_bulk(
        period, mids, first_in, second_in, taps, pick_l[...], g_first, small[...], stack, turned, bulk
    )
    ready(bulk_one)
    put_chunks(layout, coords, (bulk, bulk_one), send, keep)
    narrow = gather_narrow(dot(w_first[...], grad_first[...]), -1, period)
    base = upstream_ref[...] * (frozen + (1.0 - frozen) * growth[...])
    for d in range(3):
        row = frozen[MID - 1 + d : MID + d] * narrow[d : d + 1]
        if d == 1:
            row = row + base[MID : MID + 1]
        if d == 1:
            part_mid[0:1, :] = row
        else:
            (part_low if d == 0 else part_high)[...] = row
    part_mid[1:2, :] = own_in[...]


def force_kernel(ready, coords, above, middle, below, out):
    piece = out.shape[1]
    lanes = pl.ds(pl.multiple_of(coords[1] * piece, 128), piece)
    out[0:1, :] = above[:, lanes] + middle[0:1, lanes] + below[:, lanes]
    out[1:2, :] = middle[1:2, lanes]


def stage(jobs, after=()):
    arrays, outs, plan = [], [], []
    for kind, parts, group in jobs:
        first = len(arrays)
        arrays += group
        rows = group[0].shape[0]
        if kind == "split":
            sizes = [rows // parts] * parts
        elif kind == "sum":
            sizes = [rows]
        else:
            sizes = [sum(a.shape[0] for a in group)]
        plan.append((kind, first, len(group), len(outs), sizes))
        outs += [shape((n, 128), BF) for n in sizes]
    waits = len(after)

    def body(_, *refs):
        ins, results = refs[: len(arrays)], refs[len(arrays) + waits :]
        for kind, first, many, out, sizes in plan:
            group = ins[first : first + many]
            if kind == "join":
                at = 0
                for ref in group:
                    results[out][at : at + ref.shape[0], :] = ref[...]
                    at += ref.shape[0]
                continue
            at = 0
            for i, n in enumerate(sizes):
                results[out + i][...] = sum(ref[at : at + n, :].astype(F32) for ref in group).astype(BF)
                at += n

    got = kernel_call(body, outs, [], [*arrays, *after], 1_000_000, loose=after, vmem=12, bytes_moved=500_000)
    groups, at = [], 0
    for _, _, _, _, sizes in plan:
        groups.append(list(got[at : at + len(sizes)]))
        at += len(sizes)
    return groups


SMEM = pl.BlockSpec(memory_space=pltpu.SMEM)
VMEM = pl.BlockSpec(memory_space=pltpu.VMEM)
HBM = pl.BlockSpec(memory_space=pltpu.HBM)


def kernel_call(body, outs, scratch, args, flops, small=None, late=(), loose=(), hbm_outs=0, aliases=None,
                vmem=VMEM_MB, bytes_moved=4_000_000):
    late = [id(a) for a in late]
    loose = [id(a) for a in loose]
    spec = lambda a: SMEM if a is small else HBM if id(a) in late or id(a) in loose else VMEM
    where = [i for i, a in enumerate(args) if id(a) in late]
    many, extra = len(args), len(where)

    def whole(*refs):
        refs = list(refs)
        ins, rest = refs[:many], refs[many:]
        if extra:
            held, sems = rest[len(rest) - extra - 1 : -1], rest[-1]
            rest = rest[: len(rest) - extra - 1]
        waits = {}
        for n, i in enumerate(where):
            copy = pltpu.make_async_copy(ins[i], held[n], sems.at[n])
            copy.start()
            waits[id(held[n])] = copy
            ins[i] = held[n]

        def ready(*wanted):
            for ref in wanted:
                copy = waits.pop(id(ref), None)
                if copy is not None:
                    copy.wait()

        body(ready, *ins, *rest)
        for copy in waits.values():
            copy.wait()

    held = [pltpu.VMEM(args[i].shape, args[i].dtype) for i in where]
    if extra:
        held.append(pltpu.SemaphoreType.DMA((extra,)))
    return pl.pallas_call(
        whole,
        out_shape=tuple(outs),
        in_specs=[spec(a) for a in args],
        out_specs=tuple([VMEM] * (len(outs) - hbm_outs) + [HBM] * hbm_outs),
        scratch_shapes=[*scratch, *held],
        input_output_aliases=aliases or {},
        compiler_params=pltpu.CompilerParams(vmem_limit_bytes=vmem * 2**20),
        cost_estimate=pl.CostEstimate(flops=flops, bytes_accessed=bytes_moved, transcendentals=0),
    )(*args)


def shape(dims, dtype=F32):
    return jax.ShapeDtypeStruct(dims, dtype)


def forward(period, layer, windows, coords, weights, channels, halves):
    length = windows[0].shape[1]
    outs = [
        shape((ROWS, length)),
        shape((2, length)),
        shape((1, length)),
        shape((1, 128)),
    ]
    if layer == 1:
        outs.append(shape((ROWS, length)))
    args = [*windows, coords, *weights]
    outs += [shape((3 * channels, length), BF)] * 2
    scratch = [
        pltpu.VMEM((5 * channels, length), BF),
        pltpu.VMEM((9 * channels, length), BF),
    ]
    body = functools.partial(forward_kernel, period, layer, halves)
    flops = 3 * 2 * TAPS * channels * channels * length
    return kernel_call(body, outs, scratch, args, flops, coords)


def pack(params, picks):
    channels = params[0].shape[1]
    outs = [
        shape((9 * channels, 9 * channels), BF),
        shape((channels, 5 * 256), BF),
        shape((3, 216, channels), BF),
        shape((channels, 3 * 512), BF),
        shape((216, channels), BF),
        shape((9 * channels, 9 * channels), BF),
        shape((128, 8)),
    ]
    many = len(outs)

    def body(ready, *refs):
        ins, rest = refs[:8], refs[8:]
        for layer in range(2):
            pack_kernel(layer, ready, *ins, *rest[layer * many : (layer + 1) * many], *rest[2 * many :])

    scratch = [pltpu.VMEM((TAPS * channels, channels), F32), pltpu.VMEM((8, 128), F32)]
    args = [*params, *picks]
    got = kernel_call(body, outs * 2, scratch, args, 1_000_000_000)
    return got[:many], got[many:]


def unpack(last, layout, volume, coords, pieces, channels, before):
    halves, depth, chunk = layout
    few = channels // 2
    arrays = [
        shape((2, channels, channels, TAPS)),
        shape((2, 2, channels, TAPS)),
        shape((2, channels, TAPS)),
    ]
    scratch = [
        pltpu.VMEM((2, 2 * halves * depth * chunk, 128), BF),
        pltpu.VMEM((TAPS * few, channels), F32),
        pltpu.VMEM((2, few, channels, TAPS), F32),
        pltpu.VMEM((2, channels, TAPS), F32),
        pltpu.VMEM((2, few, TAPS), F32),
        pltpu.SemaphoreType.DMA((6,)),
    ]
    body = functools.partial(unpack_kernel, layout, volume, last)
    if not last:
        return kernel_call(
            body, arrays, scratch, [coords, pieces], 1_000_000_000, coords, hbm_outs=3
        )
    extra = [shape((2, channels)), shape((2, channels)), shape((2, 2)), shape((1, 1))]

    def reordered(ready, coords, pieces, *refs):
        before, outs, rest = refs[:3], refs[3:10], refs[10:]
        body(ready, coords, pieces, *before, *outs[4:], *outs[:4], *rest)

    got = kernel_call(
        reordered, extra + arrays, scratch, [coords, pieces, *before], 1_000_000_000, coords,
        loose=before, hbm_outs=3, aliases={2: 4, 3: 5, 4: 6},
    )
    return [*got[4:], *got[:4]]


def permuters(count, halves, depth):
    xy = lambda fn: [(fn(a), a) for a in range(count)]

    def core(v):
        return lax.ppermute(v, "xy", xy(lambda a: a ^ 1))

    def y(v):
        return lax.ppermute(v, "xy", xy(lambda a: a ^ 2))

    def scatter(pieces):
        return [
            lax.ppermute(pieces[s], "xy", xy(lambda a, s=s: (a - 4 * s) % count))
            for s in range(1, depth)
        ]

    def gather(v):
        return [lax.ppermute(v, "xy", xy(lambda a, s=s: (a + 4 * s) % count)) for s in range(1, depth)]

    def square(v):
        out = []
        for rg in range(halves):
            for ry in range(2):
                if rg or ry:
                    pairs = [
                        ((a ^ (2 * ry)) * halves + (j + rg) % halves, a * halves + j)
                        for a in range(count)
                        for j in range(halves)
                    ]
                    out.append(lax.ppermute(v, ("xy", "gz"), pairs))
        return out

    return core, y, scatter, gather, square


def per_device(noise, w_first, b_first, w_mid, b_mid, w_last, b_last):
    period = noise.shape[3]
    count = lax.axis_size("xy")
    halves = lax.axis_size("gz")
    channels = w_mid.shape[2]
    order = ring_order(count)
    places = np.argsort(np.array(order))
    volume = float(noise.size * count * halves)
    index = lax.axis_index("xy")
    depth = count // 4
    coords = jnp.stack(
        [
            jnp.asarray(places, jnp.int32)[index],
            lax.axis_index("gz"),
            index % 2,
            index // 2 % 2,
            index // 4,
        ]
    ).astype(jnp.int32)
    need = 45 * channels // 2 + channels + channels // 2
    chunk = -(-need // (2 * halves * depth * 16)) * 16
    layout = (halves, depth, chunk)

    def step(values, offset):
        return lax.ppermute(
            values, "xy", [(order[(p + offset) % count], order[p]) for p in range(count)]
        )

    flat = noise.reshape(1, -1)
    whole = [
        lax.ppermute(
            flat,
            ("xy", "gz"),
            [
                (p * halves + (j + rel) % halves, order[p] * halves + j)
                for p in range(count)
                for j in range(halves)
            ],
        )
        for rel in range(halves)
    ]
    whole = jnp.concatenate(whole, axis=1)

    params = [
        w_mid.transpose(0, 2, 3, 1),
        w_first.transpose(0, 2, 3, 1).reshape(2, channels, TAPS),
        w_last.transpose(0, 2, 3, 1),
        b_first,
        b_mid,
        b_last,
    ]
    back = spread_last_back()
    tall = np.concatenate([spread_last().reshape(6 * 216, TAPS), spread_first_back()], axis=0)
    picks = [
        jnp.asarray(np.concatenate([spread_first(), back[0], back[1]], axis=1), BF),
        jnp.asarray(np.pad(tall, ((0, 0), (0, 128 - TAPS))), BF),
    ]
    pick_l, pick_f = jnp.asarray(pick_last(), BF), jnp.asarray(pick_first(), BF)
    packed = pack(params, picks)
    ahead_weights = [(p[1], p[0], p[2], p[6]) for p in packed]
    back_weights = [(p[3], p[5], p[4]) for p in packed]

    def exchange(values):
        return [values if m == 0 else step(values, m) for m in range(-3, 4)]

    field0, state, _, logdet0, first0, second0 = forward(
        period, 0, exchange(whole), coords, ahead_weights[0], channels, halves
    )
    field1, state, own, logdet1, growth0, first1, second1 = forward(
        period, 1, exchange(state), coords, ahead_weights[1], channels, halves
    )
    core, cross, scatter, gather, square = permuters(count, halves, depth)
    length = field0.shape[1]
    full = shape((ROWS, length))
    planes = shape((3 * channels, length), BF)
    wide = pltpu.VMEM((9 * channels, length), BF)
    bulk = (4 * halves * depth * chunk, 128)
    part = 4 * depth * chunk
    flops = 2 * TAPS * channels * channels * length

    weights = back_weights[1]
    base, parts, small, grad_out, mids, grad_first = kernel_call(
        functools.partial(back_one_kernel, period),
        [full, shape((3, length)), shape((16, channels)), shape((2 * ROWS, length)), planes,
         shape((channels, length), BF)],
        [pltpu.VMEM((ROWS, length), F32), pltpu.VMEM((ROWS, length), F32), wide],
        [*exchange(state), logdet0, logdet1, coords, field1, first1, second1, *weights],
        flops, coords,
    )
    (bulk1,) = kernel_call(
        functools.partial(weights_one_kernel, period),
        [shape(bulk, BF)], [wide, wide],
        [coords, field1, first1, second1, grad_out, mids, grad_first, small, pick_l, pick_f],
        flops, coords,
    )

    weights = back_weights[0]
    low, middle, high, send, keep = kernel_call(
        functools.partial(back_zero_kernel, period, layout),
        [shape((1, length)), shape((2, length)), shape((1, length))]
        + [shape((part, 128), BF)] * 2,
        [pltpu.VMEM((ROWS, length), F32), pltpu.VMEM((3 * channels, length), BF), wide, wide,
         pltpu.VMEM(bulk, BF), pltpu.VMEM((channels, length), BF),
         pltpu.VMEM((16, channels), F32)],
        [*exchange(parts), base, growth0, own, coords, field0, bulk1, first0, second0, *weights,
         pick_l, pick_f],
        2 * flops, coords,
    )

    ((stay, away),) = stage([("split", 2, [keep, core(send)])])
    crossed = cross(away)
    (force,) = kernel_call(
        force_kernel, [shape((2, length // halves))], [],
        [coords, step(low, 1), middle, step(high, -1)], 1000, coords, bytes_moved=1000,
    )
    (pieces,) = stage([("split", depth, [stay, crossed])], after=(force,))
    force = lax.ppermute(force, "xy", [(order[p], p) for p in range(count)])
    ((total,),) = stage([("sum", 1, [pieces[0], *scatter(pieces)])], after=(force,))
    ((line,),) = stage([("join", 1, [total, *gather(total)])])
    ((mine,),) = stage([("join", 1, [line, *square(line)])])
    other = core(mine)
    outs = unpack(False, layout, volume, coords, mine, channels, [])
    g_mid, g_last, g_first, gb_first, gb_mid, gb_last, loss = unpack(
        True, layout, volume, coords, other, channels, list(outs)
    )

    return (
        force[1:2].reshape(noise.shape),
        force[0:1].reshape(noise.shape),
        loss.reshape(()),
        g_first.reshape(2, channels, 1, TAPS).transpose(0, 3, 1, 2),
        gb_first,
        g_mid.transpose(0, 3, 1, 2),
        gb_mid,
        g_last.transpose(0, 3, 1, 2),
        gb_last,
    )


def solution(mesh):
    return jax.shard_map(
        per_device,
        mesh=mesh,
        in_specs=(P("xy", "gz", None, None), P(), P(), P(), P(), P(), P()),
        out_specs=(
            P("xy", "gz", None, None),
            P("xy", "gz", None, None),
            P(),
            P(),
            P(),
            P(),
            P(),
            P(),
            P(),
        ),
        check_vma=False,
    )
```

```python
import functools

import jax
import jax.numpy as jnp
import numpy as np
from jax import lax
from jax.experimental import pallas as pl
from jax.experimental.pallas import tpu as pltpu
from jax.sharding import PartitionSpec as P

hopping = 0.3
quartic = 0.05

STEPS = (-1, 0, 1)
ROWS = 8
MID = 3
BF = jnp.bfloat16
F32 = jnp.float32
TAPS = 81
VMEM_MB = 20


def ring_order(count):
    if count % 4:
        return list(range(count))
    depth = count // 4
    chips = [(z, 0) for z in range(depth)] + [(z, 1) for z in reversed(range(depth))]
    order = []
    for place, (z, y) in enumerate(chips):
        cores = (0, 1) if place % 2 == 0 else (1, 0)
        order += [z * 4 + y * 2 + core for core in cores]
    return order


def spread_first():
    out = np.zeros((81, 5, 256), np.float32)
    for tap in range(81):
        dx, rest = divmod(tap, 27)
        for dest in range(5):
            out[tap, dest, rest * ROWS + dest + dx] = 1
    return out.reshape(81, 5 * 256)


def spread_last():
    out = np.zeros((3, 2, 216, 81), np.float32)
    for tap in range(81):
        dx, rest = divmod(tap, 27)
        for o in range(2):
            out[dx, o, rest * 8 + o, tap] = 1
    return out


def spread_last_back():
    out = np.zeros((2, 81, 3, 512), np.float32)
    for tap in range(81):
        dx, rest = divmod(tap, 27)
        for o in range(2):
            for dest in range(3):
                out[o, tap, dest, rest * 16 + o * ROWS + 2 + dest - (dx - 1)] = 1
    return out.reshape(2, 81, 3 * 512)


def spread_first_back():
    out = np.zeros((216, 81), np.float32)
    for tap in range(81):
        dx, rest = divmod(tap, 27)
        out[rest * 8 + dx, tap] = 1
    return out


def pick_last():
    out = np.zeros((432, 2, 128), np.float32)
    for tap in range(81):
        dx, rest = divmod(tap, 27)
        for o in range(2):
            out[rest * 16 + o * ROWS + MID - (dx - 1), o, tap] = 1
    return out.reshape(432, 256)


def pick_first():
    out = np.zeros((216, 128), np.float32)
    for tap in range(81):
        dx, rest = divmod(tap, 27)
        out[rest * ROWS + MID + dx - 1, tap] = 1
    return out


def z_shift(values, dz):
    length = values.shape[1]
    return values if dz == 0 else pltpu.roll(values, (-dz * 128) % length, 1)


def by_plane(values, fn):
    parts = [fn(values[:, at : at + 128]) for at in range(0, values.shape[1], 128)]
    return parts[0] if len(parts) == 1 else jnp.concatenate(parts, axis=1)


def y_shift(values, dy, period):
    if dy == 0:
        return values
    return by_plane(values, lambda v: pltpu.roll(v, (-dy * period) % 128, 1))


def t_shift(values, dt, period):
    if dt == 0:
        return values

    def one(v):
        place = lax.broadcasted_iota(jnp.int32, v.shape, 1) % period
        main = pltpu.roll(v, (-dt) % 128, 1)
        wrap = pltpu.roll(v, (dt * (period - 1)) % 128, 1)
        return jnp.where(place == (period - 1 if dt == 1 else 0), wrap, main)

    return by_plane(values, one)


def all_shifts(values, sign, period):
    in_t = [t_shift(values, sign * dt, period) for dt in STEPS]
    in_y = [[y_shift(v, sign * dy, period) for v in in_t] for dy in STEPS]
    return [z_shift(in_y[dy][dt], sign * dz) for dz in STEPS for dy in range(3) for dt in range(3)]


def gather_narrow(values, sign, period):
    block = lambda k: values[k * 8 : k * 8 + 8]
    total = None
    for dt in range(3):
        over_y = None
        for dy in range(3):
            over_z = sum(z_shift(block(dz * 9 + dy * 3 + dt), sign * (dz - 1)) for dz in range(3))
            over_z = y_shift(over_z, sign * (dy - 1), period)
            over_y = over_z if over_y is None else over_y + over_z
        over_y = t_shift(over_y, sign * (dt - 1), period)
        total = over_y if total is None else total + over_y
    return total


def gather_wide(values, channels, sign, period):
    block = lambda k: values[k * channels : (k + 1) * channels]
    total = None
    for dt in range(3):
        over_y = None
        for dy in range(3):
            part = y_shift(block(dy * 3 + dt), sign * (dy - 1), period)
            over_y = part if over_y is None else over_y + part
        over_y = t_shift(over_y, sign * (dt - 1), period)
        total = over_y if total is None else total + over_y
    return total


def dot(a, b):
    return jnp.dot(a, b, preferred_element_type=F32)


def dot_nt(a, b):
    return lax.dot_general(a, b, (((1,), (1,)), ((), ())), preferred_element_type=F32)


def stack_planes(stack, planes, channels, order):
    length = stack.shape[1]
    for dx in range(3):
        for dz in range(3):
            plane, step = order(dx, dz)
            rows = pl.ds((dx * 3 + dz) * channels, channels)
            source = planes[plane * channels : (plane + 1) * channels, :]
            if step == 0:
                stack[rows, :] = source
            elif step == 1:
                stack[rows, : length - 128] = source[:, 128:]
                stack[rows, length - 128 :] = source[:, :128]
            else:
                stack[rows, 128:] = source[:, : length - 128]
                stack[rows, :128] = source[:, length - 128 :]


def identity(n):
    row = lax.broadcasted_iota(jnp.int32, (n, n), 0)
    return (row == lax.broadcasted_iota(jnp.int32, (n, n), 1)).astype(F32).astype(BF)


def pack_kernel(layer, ready, w_mid, w_first, w_last, biases, lanes, rows_81,
                matrix, first, narrow, last_back, first_back, turned, columns, taps, rows):
    channels = w_mid.shape[1]
    few = channels // 2
    for o in range(few):
        pair = jnp.concatenate([w_mid[layer, o], w_mid[layer, o + few]], axis=0)
        taps[pl.ds(o, TAPS, stride=few), :] = dot_nt(identity(TAPS), pair)

    def block(tap):
        both = taps[tap * few : (tap + 1) * few, :]
        return jnp.concatenate([both[:, :channels], both[:, channels:]], axis=0)

    for inner in range(9):
        at = pl.ds(inner * channels, channels)
        for outer in range(0, 9, 2):
            low = block(outer * 9 + inner)
            if outer < 8:
                high = block(outer * 9 + 9 + inner)
                wide = slice(outer * channels, (outer + 2) * channels)
                matrix[at, wide] = jnp.concatenate([low, high], axis=1).astype(BF)
            else:
                matrix[at, outer * channels :] = low.astype(BF)
    for inner in range(9):
        at = pl.ds(inner * channels, channels)
        for outer in range(0, 9, 2):
            if outer < 8:
                wide = slice(outer * channels, (outer + 2) * channels)
                both = dot_nt(identity(2 * channels), matrix[at, wide])
                turned[at, wide] = jnp.concatenate([both[:channels], both[channels:]], axis=1).astype(BF)
            else:
                turned[at, outer * channels :] = dot_nt(
                    identity(channels), matrix[at, outer * channels :]
                ).astype(BF)
    wf = w_first[layer]
    first[...] = dot(wf, lanes[:, : 5 * 256]).astype(BF)
    first_back[...] = dot_nt(rows_81[6 * 216 : 7 * 216, :TAPS], wf).astype(BF)
    for dx in range(3):
        narrow[dx] = sum(
            dot_nt(rows_81[(dx * 2 + o) * 216 : (dx * 2 + o + 1) * 216, :TAPS], w_last[layer, o])
            for o in range(2)
        ).astype(BF)
    last_back[...] = sum(
        dot(w_last[layer, o], lanes[:, 5 * 256 + o * 1536 : 5 * 256 + (o + 1) * 1536]) for o in range(2)
    ).astype(BF)
    rows[...] = jnp.zeros_like(rows)
    rows[0:3, :channels] = biases[3 * layer : 3 * layer + 3, :]
    columns[...] = rows[...].T


def unpack_kernel(layout, volume, last, ready, coords, pieces, *refs):
    if last:
        refs = refs[3:]
        g_mid, g_last, g_first, gb_first, gb_mid, gb_last, loss = refs[:7]
        bulk, taps, mid, lasts, firsts, sems = refs[7:]
    else:
        g_mid, g_last, g_first = refs[:3]
        bulk, taps, mid, lasts, firsts, sems = refs[3:]
    channels = g_mid.shape[2]
    few = channels // 2
    halves, depth, chunk = layout
    g, y, z = coords[1], coords[3], coords[4]
    core = 1 - coords[2] if last else coords[2]
    per_layer = 2 * halves * depth * chunk
    at = 0
    for rg in range(halves):
        for ry in range(2):
            for rz in range(depth):
                to = ((lax.rem(g + rg, halves) * 2 + (1 - y if ry else y)) * depth
                      + lax.rem(z + rz, depth)) * chunk
                for layer in range(2):
                    bulk[layer, pl.ds(pl.multiple_of(to, 16), chunk), :] = pieces[at : at + chunk, :]
                    at += chunk
    rows, pairs = 9 * few, few // 2
    copies = []
    for layer in range(2):
        for tap in range(TAPS):
            outer, inner = divmod(tap, 9)
            start = (outer // 2) * rows + inner * few
            low = (outer % 2) * channels
            both = bulk[layer, start : start + few, low : low + channels].astype(F32)
            taps[tap * pairs : (tap + 1) * pairs, :channels] = both[:pairs]
            taps[tap * pairs : (tap + 1) * pairs, channels:] = both[pairs:]
        for o in range(pairs):
            pair = taps[pl.ds(o, TAPS, stride=pairs), :].astype(BF)
            pair = dot_nt(identity(2 * channels), pair) * (1.0 / volume)
            mid[layer, o] = pair[:channels]
            mid[layer, o + pairs] = pair[channels:]
        rest = bulk[layer, 5 * rows : 5 * rows + channels + few, :].astype(F32) * (1.0 / volume)
        lasts[layer] = rest[:channels, :TAPS]
        firsts[layer] = rest[channels:, :TAPS]
        if last:
            small = bulk[layer, 4 * rows : 4 * rows + 16, channels:].astype(F32) * (1.0 / volume)
            gb_first[layer : layer + 1, :] = small[0:1]
            gb_mid[layer : layer + 1, :] = small[1:2]
            gb_last[layer : layer + 1, :] = small[2:3, :2]
            if layer == 1:
                loss[...] = jnp.sum(
                    jnp.sum(small[3:6], axis=0, keepdims=True), axis=1, keepdims=True
                )
        copies += [
            pltpu.make_async_copy(
                mid.at[layer], g_mid.at[layer, pl.ds(core * few, few)], sems.at[layer * 3]
            ),
            pltpu.make_async_copy(lasts.at[layer], g_last.at[layer, core], sems.at[layer * 3 + 1]),
            pltpu.make_async_copy(
                firsts.at[layer],
                g_first.at[layer, pl.ds(pl.multiple_of(core * few, few), few)],
                sems.at[layer * 3 + 2],
            ),
        ]
        for copy in copies[-3:]:
            copy.start()
    for copy in copies:
        copy.wait()


def place_windows(refs, row, target):
    target[...] = jnp.zeros_like(target)
    for r, ref in enumerate(refs):
        target[r : r + 1, :] = ref[row : row + 1, :]


def oddness(shape, place, period):
    lane = lax.broadcasted_iota(jnp.int32, shape, 1)
    row = lax.broadcasted_iota(jnp.int32, shape, 0)
    within = lane % 128
    return ((place + row + 1 + lane // 128 + within // period + within % period) % 2).astype(F32)


def forward_kernel(period, layer, halves, ready, *refs):
    windows, refs = refs[:7], refs[7:]
    if layer == 0:
        (coords, w_first, w_mid, w_last, columns,
         field_out, state, own_out, logdet, first_out, second_out, first, stack) = refs
        field_out[...] = jnp.zeros_like(field_out)
        piece = field_out.shape[1] // halves
        for rel in range(halves):
            to = pl.multiple_of(lax.rem(coords[1] + rel, halves) * piece, 128)
            for r, ref in enumerate(windows):
                field_out[r : r + 1, pl.ds(to, piece)] = ref[:, rel * piece : (rel + 1) * piece]
    else:
        (coords, w_first, w_mid, w_last, columns,
         field_out, state, own_out, logdet, growth_out, first_out, second_out,
         first, stack) = refs
        place_windows(windows, 0, field_out)
        place_windows(windows, 1, growth_out)
    channels = w_mid.shape[0] // 9
    field = field_out[...]
    length = field.shape[1]
    frozen = oddness(field.shape, coords[0], period)
    if layer == 1:
        frozen = 1.0 - frozen
    net = frozen * field
    taps = jnp.concatenate(all_shifts(net, 1, period), axis=0).astype(BF)
    ready(w_first, columns)
    bias_first, bias_mid = columns[:channels, 0:1], columns[:channels, 1:2]
    for dest in range(5):
        part = dot(w_first[:, dest * 256 : dest * 256 + 216], taps)
        first[dest * channels : (dest + 1) * channels, :] = jnp.tanh(part + bias_first).astype(BF)
    first_out[...] = first[channels : 4 * channels, :]
    ready(w_mid)
    for dest in range(3):
        stack_planes(stack, first, channels, lambda dx, dz: (dest + dx, dz - 1))
        for at in range(0, length, 256):
            wide = dot(w_mid[...], stack[:, at : at + 256])
            wide = gather_wide(wide, channels, 1, period)
            second_out[dest * channels : (dest + 1) * channels, at : at + 256] = jnp.tanh(
                wide + bias_mid
            ).astype(BF)
    ready(w_last)
    narrow = sum(
        dot(w_last[dx], second_out[dx * channels : (dx + 1) * channels, :]) for dx in range(3)
    )
    narrow = gather_narrow(narrow, 1, period) + columns[:8, 2:3]
    growth = jnp.exp(narrow[0:1])
    mine = field[MID : MID + 1]
    still = frozen[MID : MID + 1]
    moving = 1.0 - still
    state[0:1, :] = still * mine + moving * (mine * growth + narrow[1:2])
    state[1:2, :] = growth
    own_out[...] = state[0:1, :]
    flow = moving * narrow[0:1]
    logdet[...] = sum(flow[:, at : at + 128] for at in range(0, length, 128))


def put_chunks(layout, coords, bulks, send, keep):
    halves, depth, chunk = layout
    per_core = bulks[0].shape[0] // 2
    g, c, y, z = (coords[i] for i in range(1, 5))
    for core, ref in ((c, keep), (1 - c, send)):
        at = 0
        for ry in range(2):
            for rz in range(depth):
                source = core * per_core + (
                    (g * 2 + (1 - y if ry else y)) * depth + lax.rem(z + rz, depth)
                ) * chunk
                for bulk in bulks:
                    ref[at : at + chunk, :] = bulk[pl.ds(pl.multiple_of(source, 16), chunk), :]
                    at += chunk


def output_taps(grad_output, period):
    return jnp.concatenate(all_shifts(grad_output, -1, period), axis=0).astype(BF)


def output_gradient(upstream, moving, field, grow):
    place = lax.broadcasted_iota(jnp.int32, (2 * ROWS, field.shape[1]), 0) % ROWS
    grad_scale = upstream * moving * field * grow - moving
    grad_shift = upstream * moving
    both = jnp.concatenate([grad_scale, grad_shift], axis=0)
    return jnp.where(jnp.logical_and(place >= 1, place <= 5), both, 0.0)


def second_gradient(w_last, second, taps, mids):
    channels = mids.shape[0] // 3
    for dest in range(3):
        part = dot(w_last[:, dest * 512 : dest * 512 + 432], taps)
        rows = slice(dest * channels, (dest + 1) * channels)
        wide = second[rows, :].astype(F32)
        mids[rows, :] = (part * (1.0 - wide * wide)).astype(BF)


def first_gradient(period, mids, first, w_mid, stack, grad_first):
    channels = mids.shape[0] // 3
    stack_planes(stack, mids, channels, lambda dx, dz: (2 - dx, 1 - dz))
    for at in range(0, stack.shape[1], 256):
        wide = dot(w_mid[...], stack[:, at : at + 256])
        wide = gather_wide(wide, channels, -1, period)
        seen = first[channels : 2 * channels, at : at + 256].astype(F32)
        grad_first[:, at : at + 256] = (wide * (1.0 - seen * seen)).astype(BF)


def first_weights(period, net, grad_first, pick_f):
    taps = jnp.concatenate(all_shifts(net, 1, period), axis=0).astype(BF)
    g_first = dot_nt(grad_first, taps).astype(BF)
    return dot(g_first, pick_f)


def fill_bulk(period, mids, first, second, taps, pick_l, g_first, small, stack, turned, bulk):
    channels = mids.shape[0] // 3
    few = channels // 2
    own = slice(channels, 2 * channels)
    rounded = mids[own, :].astype(F32)
    in_t = [t_shift(rounded, -dt, period) for dt in STEPS]
    for dy in range(3):
        for dt in range(3):
            turned[(dy * 3 + dt) * channels : (dy * 3 + dt + 1) * channels, :] = y_shift(
                in_t[dt], -STEPS[dy], period
            ).astype(BF)
    stack_planes(stack, first, channels, lambda dx, dz: (dx, dz - 1))
    g_mid = dot_nt(turned[...], stack[...]).astype(BF)
    per_core = bulk.shape[0] // 2
    rows = 9 * few
    g_last = dot_nt(second[own, :], taps).astype(BF)
    g_last = dot(g_last, pick_l).astype(BF)
    for core in range(2):
        base = core * per_core
        for b in range(5):
            for inner in range(9):
                at = inner * channels + core * few
                part = g_mid[at : at + few, b * 128 : (b + 1) * 128]
                if part.shape[1] < 128:
                    part = jnp.concatenate([part, jnp.zeros((few, 128 - part.shape[1]), BF)], axis=1)
                to = base + b * rows + inner * few
                bulk[to : to + few, :] = part
        at = base + 4 * rows
        bulk[at : at + 16, channels:] = small.astype(BF)
        at = base + 5 * rows
        bulk[at : at + channels, :] = g_last[:, core * 128 : (core + 1) * 128]
        bulk[at + channels : at + channels + few, :] = g_first[core * few : (core + 1) * few, :].astype(BF)
        at += channels + few
        if at < base + per_core:
            bulk[at : base + per_core, :] = jnp.zeros((base + per_core - at, 128), BF)


def bias_rows(small, grad_output, mids, grad_first):
    channels = mids.shape[0] // 3
    ones = jnp.ones((8, mids.shape[1]), BF)
    small[0:1, :] = dot_nt(ones, grad_first)[0:1]
    small[1:2, :] = dot_nt(ones, mids[channels : 2 * channels, :])[0:1]
    sums = dot_nt(ones, grad_output.astype(BF))
    small[2:3, 0:1] = sums[0:1, MID : MID + 1]
    small[2:3, 1:2] = sums[0:1, 8 + MID : 9 + MID]


def back_one_kernel(period, ready, *refs):
    windows, refs = refs[:7], refs[7:]
    (logdet0, logdet1, coords, field_in, first_in, second_in, w_last, w_mid, w_first,
     base_out, part_out, small, grad_out, mids, grad_first, field_end, growth, stack) = refs
    place_windows(windows, 0, field_end)
    place_windows(windows, 1, growth)
    frozen = 1.0 - oddness(field_in.shape, coords[0], period)
    moving = 1.0 - frozen
    field = field_end[...]
    ahead = (
        pltpu.roll(field, ROWS - 1, 0)
        + z_shift(field, 1)
        + y_shift(field, 1, period)
        + t_shift(field, 1, period)
    )
    behind = (
        pltpu.roll(field, 1, 0)
        + z_shift(field, -1)
        + y_shift(field, -1, period)
        + t_shift(field, -1, period)
    )
    squared = field * field
    density = (
        -2.0 * hopping * field * ahead + squared + quartic * (squared - 1.0) * (squared - 1.0)
    )[MID : MID + 1]
    action = sum(density[:, at : at + 128] for at in range(0, field.shape[1], 128))
    loss = jnp.sum(action - logdet0[...] - logdet1[...], axis=1, keepdims=True)
    small[...] = jnp.zeros_like(small)
    slot = lax.broadcasted_iota(jnp.int32, (1, small.shape[1]), 1) == coords[0]
    for part in range(3):
        top = loss.astype(BF).astype(F32)
        small[3 + part : 4 + part, :] = jnp.where(slot, top, 0.0)
        loss = loss - top
    place = lax.broadcasted_iota(jnp.int32, field.shape, 0)
    upstream = (
        -2.0 * hopping * (ahead + behind) + 2.0 * field + 4.0 * quartic * (squared - 1.0) * field
    )
    upstream = jnp.where(jnp.logical_and(place >= 1, place <= 5), upstream, 0.0)
    grow = growth[...]
    grad_out[...] = output_gradient(upstream, moving, field_in[...], grow)
    base_out[...] = upstream * (frozen + moving * grow)
    taps = output_taps(grad_out[...], period)
    ready(w_last, second_in)
    second_gradient(w_last, second_in, taps, mids)
    ready(w_mid, first_in)
    first_gradient(period, mids, first_in, w_mid, stack, grad_first)
    bias_rows(small, grad_out[...], mids, grad_first[...])
    ready(w_first)
    narrow = gather_narrow(dot(w_first[...], grad_first[...]), -1, period)
    for d in range(3):
        part_out[d : d + 1, :] = frozen[MID - 1 + d : MID + d] * narrow[d : d + 1]


def weights_one_kernel(period, ready, coords, field_in, first_in, second_in, grad_out, mids, grad_first, small,
                       pick_l, pick_f, bulk, stack, turned):
    taps = output_taps(grad_out[...], period)
    frozen = 1.0 - oddness(field_in.shape, coords[0], period)
    ready(first_in, second_in, pick_l, pick_f)
    g_first = first_weights(period, frozen * field_in[...], grad_first[...], pick_f[...])
    fill_bulk(
        period, mids, first_in, second_in, taps, pick_l[...], g_first, small[...], stack, turned, bulk
    )


def back_zero_kernel(period, layout, ready, *refs):
    windows, refs = refs[:7], refs[7:]
    (base_in, growth, own_in, coords, field_in, bulk_one, first_in, second_in, w_last, w_mid, w_first,
     pick_l, pick_f,
     part_low, part_mid, part_high, send, keep,
     upstream_ref, mids, stack, turned, bulk, grad_first, small) = refs
    frozen = oddness(field_in.shape, coords[0], period)
    upstream_ref[...] = base_in[...]
    for r in range(1, 6):
        upstream_ref[r : r + 1, :] += (
            windows[r - 1][2:3, :] + windows[r][1:2, :] + windows[r + 1][0:1, :]
        )
    grad_output = output_gradient(upstream_ref[...], 1.0 - frozen, field_in[...], growth[...])
    taps = output_taps(grad_output, period)
    ready(w_last, second_in)
    second_gradient(w_last, second_in, taps, mids)
    ready(w_mid, first_in)
    first_gradient(period, mids, first_in, w_mid, stack, grad_first)
    small[...] = jnp.zeros_like(small)
    bias_rows(small, grad_output, mids, grad_first[...])
    ready(w_first, pick_f, pick_l)
    g_first = first_weights(period, frozen * field_in[...], grad_first[...], pick_f[...])
    fill_bulk(
        period, mids, first_in, second_in, taps, pick_l[...], g_first, small[...], stack, turned, bulk
    )
    ready(bulk_one)
    put_chunks(layout, coords, (bulk, bulk_one), send, keep)
    narrow = gather_narrow(dot(w_first[...], grad_first[...]), -1, period)
    base = upstream_ref[...] * (frozen + (1.0 - frozen) * growth[...])
    for d in range(3):
        row = frozen[MID - 1 + d : MID + d] * narrow[d : d + 1]
        if d == 1:
            row = row + base[MID : MID + 1]
        if d == 1:
            part_mid[0:1, :] = row
        else:
            (part_low if d == 0 else part_high)[...] = row
    part_mid[1:2, :] = own_in[...]


def force_kernel(ready, coords, above, middle, below, out):
    piece = out.shape[1]
    lanes = pl.ds(pl.multiple_of(coords[1] * piece, 128), piece)
    out[0:1, :] = above[:, lanes] + middle[0:1, lanes] + below[:, lanes]
    out[1:2, :] = middle[1:2, lanes]


def stage(jobs, after=()):
    arrays, outs, plan = [], [], []
    for kind, parts, group in jobs:
        first = len(arrays)
        arrays += group
        rows = group[0].shape[0]
        if kind == "split":
            sizes = [rows // parts] * parts
        elif kind == "sum":
            sizes = [rows]
        else:
            sizes = [sum(a.shape[0] for a in group)]
        plan.append((kind, first, len(group), len(outs), sizes))
        outs += [shape((n, 128), BF) for n in sizes]
    waits = len(after)

    def body(_, *refs):
        ins, results = refs[: len(arrays)], refs[len(arrays) + waits :]
        for kind, first, many, out, sizes in plan:
            group = ins[first : first + many]
            if kind == "join":
                at = 0
                for ref in group:
                    results[out][at : at + ref.shape[0], :] = ref[...]
                    at += ref.shape[0]
                continue
            at = 0
            for i, n in enumerate(sizes):
                results[out + i][...] = sum(ref[at : at + n, :].astype(F32) for ref in group).astype(BF)
                at += n

    got = kernel_call(body, outs, [], [*arrays, *after], 1_000_000, loose=after, vmem=12, bytes_moved=500_000)
    groups, at = [], 0
    for _, _, _, _, sizes in plan:
        groups.append(list(got[at : at + len(sizes)]))
        at += len(sizes)
    return groups


SMEM = pl.BlockSpec(memory_space=pltpu.SMEM)
VMEM = pl.BlockSpec(memory_space=pltpu.VMEM)
HBM = pl.BlockSpec(memory_space=pltpu.HBM)


HERE = "here"


def locate():
    index = lax.axis_index("xy")
    depth = lax.axis_size("xy") // 4
    core, y, z = index % 2, index // 2 % 2, index // 4
    chip = jnp.where(y == 0, z, 2 * depth - 1 - z)
    place = 2 * chip + jnp.where(chip % 2 == 0, core, 1 - core)
    return place, lax.axis_index("gz"), core, y, z


def kernel_call(body, outs, scratch, args, flops, late=(), loose=(), hbm_outs=0, aliases=None,
                vmem=VMEM_MB, bytes_moved=4_000_000):
    here = next((i for i, a in enumerate(args) if a is HERE), None)
    args = [a for a in args if a is not HERE]
    late = [id(a) for a in late]
    loose = [id(a) for a in loose]
    spec = lambda a: HBM if id(a) in late or id(a) in loose else VMEM
    where = [i for i, a in enumerate(args) if id(a) in late]
    many, extra = len(args), len(where)

    def whole(*refs):
        refs = list(refs)
        ins, rest = refs[:many], refs[many:]
        if extra:
            held, sems = rest[len(rest) - extra - 1 : -1], rest[-1]
            rest = rest[: len(rest) - extra - 1]
        waits = {}
        for n, i in enumerate(where):
            copy = pltpu.make_async_copy(ins[i], held[n], sems.at[n])
            copy.start()
            waits[id(held[n])] = copy
            ins[i] = held[n]

        def ready(*wanted):
            for ref in wanted:
                copy = waits.pop(id(ref), None)
                if copy is not None:
                    copy.wait()

        if here is not None:
            ins.insert(here, locate())
        body(ready, *ins, *rest)
        for copy in waits.values():
            copy.wait()

    held = [pltpu.VMEM(args[i].shape, args[i].dtype) for i in where]
    if extra:
        held.append(pltpu.SemaphoreType.DMA((extra,)))
    return pl.pallas_call(
        whole,
        out_shape=tuple(outs),
        in_specs=[spec(a) for a in args],
        out_specs=tuple([VMEM] * (len(outs) - hbm_outs) + [HBM] * hbm_outs),
        scratch_shapes=[*scratch, *held],
        input_output_aliases=aliases or {},
        compiler_params=pltpu.CompilerParams(vmem_limit_bytes=vmem * 2**20),
        cost_estimate=pl.CostEstimate(flops=flops, bytes_accessed=bytes_moved, transcendentals=0),
    )(*args)


def shape(dims, dtype=F32):
    return jax.ShapeDtypeStruct(dims, dtype)


def forward(period, layer, windows, coords, weights, channels, halves):
    length = windows[0].shape[1]
    outs = [
        shape((ROWS, length)),
        shape((2, length)),
        shape((1, length)),
        shape((1, 128)),
    ]
    if layer == 1:
        outs.append(shape((ROWS, length)))
    args = [*windows, coords, *weights]
    outs += [shape((3 * channels, length), BF)] * 2
    scratch = [
        pltpu.VMEM((5 * channels, length), BF),
        pltpu.VMEM((9 * channels, length), BF),
    ]
    body = functools.partial(forward_kernel, period, layer, halves)
    flops = 3 * 2 * TAPS * channels * channels * length
    return kernel_call(body, outs, scratch, args, flops)


def pack(params, picks):
    channels = params[0].shape[1]
    outs = [
        shape((9 * channels, 9 * channels), BF),
        shape((channels, 5 * 256), BF),
        shape((3, 216, channels), BF),
        shape((channels, 3 * 512), BF),
        shape((216, channels), BF),
        shape((9 * channels, 9 * channels), BF),
        shape((128, 8)),
    ]
    many = len(outs)

    def body(ready, *refs):
        ins, rest = refs[:6], refs[6:]
        for layer in range(2):
            pack_kernel(layer, ready, *ins, *rest[layer * many : (layer + 1) * many], *rest[2 * many :])

    scratch = [pltpu.VMEM((TAPS * channels // 2, 2 * channels), F32), pltpu.VMEM((8, 128), F32)]
    args = [*params, *picks]
    got = kernel_call(body, outs * 2, scratch, args, 1_000_000_000)
    return got[:many], got[many:]


def unpack(last, layout, volume, coords, pieces, channels, before):
    halves, depth, chunk = layout
    few = channels // 2
    arrays = [
        shape((2, channels, channels, TAPS)),
        shape((2, 2, channels, TAPS)),
        shape((2, channels, TAPS)),
    ]
    scratch = [
        pltpu.VMEM((2, 2 * halves * depth * chunk, 128), BF),
        pltpu.VMEM((TAPS * few // 2, 2 * channels), F32),
        pltpu.VMEM((2, few, channels, TAPS), F32),
        pltpu.VMEM((2, channels, TAPS), F32),
        pltpu.VMEM((2, few, TAPS), F32),
        pltpu.SemaphoreType.DMA((6,)),
    ]
    body = functools.partial(unpack_kernel, layout, volume, last)
    if not last:
        return kernel_call(
            body, arrays, scratch, [coords, pieces], 1_000_000_000, hbm_outs=3
        )
    extra = [shape((2, channels)), shape((2, channels)), shape((2, 2)), shape((1, 1))]

    def reordered(ready, coords, pieces, *refs):
        before, outs, rest = refs[:3], refs[3:10], refs[10:]
        body(ready, coords, pieces, *before, *outs[4:], *outs[:4], *rest)

    got = kernel_call(
        reordered, extra + arrays, scratch, [coords, pieces, *before], 1_000_000_000,
        loose=before, hbm_outs=3, aliases={1: 4, 2: 5, 3: 6},
    )
    return [*got[4:], *got[:4]]


def permuters(count, halves, depth):
    xy = lambda fn: [(fn(a), a) for a in range(count)]

    def core(v):
        return lax.ppermute(v, "xy", xy(lambda a: a ^ 1))

    def y(v):
        return lax.ppermute(v, "xy", xy(lambda a: a ^ 2))

    def scatter(pieces):
        return [
            lax.ppermute(pieces[s], "xy", xy(lambda a, s=s: (a - 4 * s) % count))
            for s in range(1, depth)
        ]

    def gather(v):
        return [lax.ppermute(v, "xy", xy(lambda a, s=s: (a + 4 * s) % count)) for s in range(1, depth)]

    def square(v):
        out = []
        for rg in range(halves):
            for ry in range(2):
                if rg or ry:
                    pairs = [
                        ((a ^ (2 * ry)) * halves + (j + rg) % halves, a * halves + j)
                        for a in range(count)
                        for j in range(halves)
                    ]
                    out.append(lax.ppermute(v, ("xy", "gz"), pairs))
        return out

    return core, y, scatter, gather, square


def per_device(noise, w_first, b_first, w_mid, b_mid, w_last, b_last):
    period = noise.shape[3]
    count = lax.axis_size("xy")
    halves = lax.axis_size("gz")
    channels = w_mid.shape[2]
    order = ring_order(count)
    volume = float(noise.size * count * halves)
    depth = count // 4
    coords = HERE
    need = 45 * channels // 2 + channels + channels // 2
    chunk = -(-need // (2 * halves * depth * 16)) * 16
    layout = (halves, depth, chunk)

    def step(values, offset):
        return lax.ppermute(
            values, "xy", [(order[(p + offset) % count], order[p]) for p in range(count)]
        )

    flat = noise.reshape(1, -1)
    whole = [
        lax.ppermute(
            flat,
            ("xy", "gz"),
            [
                (p * halves + (j + rel) % halves, order[p] * halves + j)
                for p in range(count)
                for j in range(halves)
            ],
        )
        for rel in range(halves)
    ]
    params = [
        w_mid.transpose(0, 2, 3, 1),
        w_first.transpose(0, 2, 3, 1).reshape(2, channels, TAPS),
        w_last.transpose(0, 2, 3, 1),
        jnp.stack([b_first, b_mid, jnp.pad(b_last, ((0, 0), (0, channels - 2)))], axis=1).reshape(6, channels),
    ]
    back = spread_last_back()
    tall = np.concatenate([spread_last().reshape(6 * 216, TAPS), spread_first_back()], axis=0)
    picks = [
        jnp.asarray(np.concatenate([spread_first(), back[0], back[1]], axis=1), BF),
        jnp.asarray(np.pad(tall, ((0, 0), (0, 128 - TAPS))), BF),
    ]
    pick_l, pick_f = jnp.asarray(pick_last(), BF), jnp.asarray(pick_first(), BF)
    packed = pack(params, picks)
    ahead_weights = [(p[1], p[0], p[2], p[6]) for p in packed]
    back_weights = [(p[3], p[5], p[4]) for p in packed]

    def join(ready, *refs):
        piece = refs[0].shape[1]
        for rel in range(halves):
            refs[-1][:, rel * piece : (rel + 1) * piece] = refs[rel][...]

    waits = (packed[1][5],)
    (whole,) = kernel_call(
        join, [shape((1, flat.shape[1] * halves))], [], [*whole, *waits], 1000, loose=waits, bytes_moved=1000
    )

    def exchange(values):
        return [values if m == 0 else step(values, m) for m in range(-3, 4)]

    field0, state, _, logdet0, first0, second0 = forward(
        period, 0, exchange(whole), coords, ahead_weights[0], channels, halves
    )
    field1, state, own, logdet1, growth0, first1, second1 = forward(
        period, 1, exchange(state), coords, ahead_weights[1], channels, halves
    )
    core, cross, scatter, gather, square = permuters(count, halves, depth)
    length = field0.shape[1]
    full = shape((ROWS, length))
    planes = shape((3 * channels, length), BF)
    wide = pltpu.VMEM((9 * channels, length), BF)
    bulk = (4 * halves * depth * chunk, 128)
    part = 4 * depth * chunk
    flops = 2 * TAPS * channels * channels * length

    weights = back_weights[1]
    base, parts, small, grad_out, mids, grad_first = kernel_call(
        functools.partial(back_one_kernel, period),
        [full, shape((3, length)), shape((16, channels)), shape((2 * ROWS, length)), planes,
         shape((channels, length), BF)],
        [pltpu.VMEM((ROWS, length), F32), pltpu.VMEM((ROWS, length), F32), wide],
        [*exchange(state), logdet0, logdet1, coords, field1, first1, second1, *weights],
        flops,
    )
    (bulk1,) = kernel_call(
        functools.partial(weights_one_kernel, period),
        [shape(bulk, BF)], [wide, wide],
        [coords, field1, first1, second1, grad_out, mids, grad_first, small, pick_l, pick_f],
        flops,
    )

    weights = back_weights[0]
    low, middle, high, send, keep = kernel_call(
        functools.partial(back_zero_kernel, period, layout),
        [shape((1, length)), shape((2, length)), shape((1, length))]
        + [shape((part, 128), BF)] * 2,
        [pltpu.VMEM((ROWS, length), F32), pltpu.VMEM((3 * channels, length), BF), wide, wide,
         pltpu.VMEM(bulk, BF), pltpu.VMEM((channels, length), BF),
         pltpu.VMEM((16, channels), F32)],
        [*exchange(parts), base, growth0, own, coords, field0, bulk1, first0, second0, *weights,
         pick_l, pick_f],
        2 * flops,
    )

    ((stay, away),) = stage([("split", 2, [keep, core(send)])])
    crossed = cross(away)
    (force,) = kernel_call(
        force_kernel, [shape((2, length // halves))], [],
        [coords, step(low, 1), middle, step(high, -1)], 1000, bytes_moved=1000,
    )
    (pieces,) = stage([("split", depth, [stay, crossed])], after=(force,))
    ((total,),) = stage([("sum", 1, [pieces[0], *scatter(pieces)])])
    ((line,),) = stage([("join", 1, [total, *gather(total)])])
    ((mine,),) = stage([("join", 1, [line, *square(line)])])
    other = core(mine)
    force = lax.ppermute(force, "xy", [(order[p], p) for p in range(count)])
    outs = unpack(False, layout, volume, coords, mine, channels, [])
    g_mid, g_last, g_first, gb_first, gb_mid, gb_last, loss = unpack(
        True, layout, volume, coords, other, channels, list(outs)
    )

    return (
        force[1:2].reshape(noise.shape),
        force[0:1].reshape(noise.shape),
        loss.reshape(()),
        g_first.reshape(2, channels, 1, TAPS).transpose(0, 3, 1, 2),
        gb_first,
        g_mid.transpose(0, 3, 1, 2),
        gb_mid,
        g_last.transpose(0, 3, 1, 2),
        gb_last,
    )


def solution(mesh):
    return jax.shard_map(
        per_device,
        mesh=mesh,
        in_specs=(P("xy", "gz", None, None), P(), P(), P(), P(), P(), P()),
        out_specs=(
            P("xy", "gz", None, None),
            P("xy", "gz", None, None),
            P(),
            P(),
            P(),
            P(),
            P(),
            P(),
            P(),
        ),
        check_vma=False,
    )
```

```python
import functools

import jax
import jax.numpy as jnp
import numpy as np
from jax import lax
from jax.experimental import pallas as pl
from jax.experimental.pallas import tpu as pltpu
from jax.sharding import PartitionSpec as P

hopping = 0.3
quartic = 0.05

STEPS = (-1, 0, 1)
ROWS = 8
MID = 3
BF = jnp.bfloat16
F32 = jnp.float32
TAPS = 81
VMEM_MB = 20


def ring_order(count):
    if count % 4:
        return list(range(count))
    depth = count // 4
    chips = [(z, 0) for z in range(depth)] + [(z, 1) for z in reversed(range(depth))]
    order = []
    for place, (z, y) in enumerate(chips):
        cores = (0, 1) if place % 2 == 0 else (1, 0)
        order += [z * 4 + y * 2 + core for core in cores]
    return order


def spread_first():
    out = np.zeros((81, 5, 256), np.float32)
    for tap in range(81):
        dx, rest = divmod(tap, 27)
        for dest in range(5):
            out[tap, dest, rest * ROWS + dest + dx] = 1
    return out.reshape(81, 5 * 256)


def spread_last():
    out = np.zeros((3, 2, 216, 81), np.float32)
    for tap in range(81):
        dx, rest = divmod(tap, 27)
        for o in range(2):
            out[dx, o, rest * 8 + o, tap] = 1
    return out


def spread_last_back():
    out = np.zeros((2, 81, 3, 512), np.float32)
    for tap in range(81):
        dx, rest = divmod(tap, 27)
        for o in range(2):
            for dest in range(3):
                out[o, tap, dest, rest * 16 + o * ROWS + 2 + dest - (dx - 1)] = 1
    return out.reshape(2, 81, 3 * 512)


def spread_first_back():
    out = np.zeros((216, 81), np.float32)
    for tap in range(81):
        dx, rest = divmod(tap, 27)
        out[rest * 8 + dx, tap] = 1
    return out


def pick_last():
    out = np.zeros((432, 2, 128), np.float32)
    for tap in range(81):
        dx, rest = divmod(tap, 27)
        for o in range(2):
            out[rest * 16 + o * ROWS + MID - (dx - 1), o, tap] = 1
    return out.reshape(432, 256)


def pick_first():
    out = np.zeros((216, 128), np.float32)
    for tap in range(81):
        dx, rest = divmod(tap, 27)
        out[rest * ROWS + MID + dx - 1, tap] = 1
    return out


def z_shift(values, dz):
    length = values.shape[1]
    return values if dz == 0 else pltpu.roll(values, (-dz * 128) % length, 1)


def by_plane(values, fn):
    parts = [fn(values[:, at : at + 128]) for at in range(0, values.shape[1], 128)]
    return parts[0] if len(parts) == 1 else jnp.concatenate(parts, axis=1)


def y_shift(values, dy, period):
    if dy == 0:
        return values
    return by_plane(values, lambda v: pltpu.roll(v, (-dy * period) % 128, 1))


def t_shift(values, dt, period):
    if dt == 0:
        return values

    def one(v):
        place = lax.broadcasted_iota(jnp.int32, v.shape, 1) % period
        main = pltpu.roll(v, (-dt) % 128, 1)
        wrap = pltpu.roll(v, (dt * (period - 1)) % 128, 1)
        return jnp.where(place == (period - 1 if dt == 1 else 0), wrap, main)

    return by_plane(values, one)


def all_shifts(values, sign, period):
    in_t = [t_shift(values, sign * dt, period) for dt in STEPS]
    in_y = [[y_shift(v, sign * dy, period) for v in in_t] for dy in STEPS]
    return [z_shift(in_y[dy][dt], sign * dz) for dz in STEPS for dy in range(3) for dt in range(3)]


def gather_narrow(values, sign, period):
    block = lambda k: values[k * 8 : k * 8 + 8]
    total = None
    for dt in range(3):
        over_y = None
        for dy in range(3):
            over_z = sum(z_shift(block(dz * 9 + dy * 3 + dt), sign * (dz - 1)) for dz in range(3))
            over_z = y_shift(over_z, sign * (dy - 1), period)
            over_y = over_z if over_y is None else over_y + over_z
        over_y = t_shift(over_y, sign * (dt - 1), period)
        total = over_y if total is None else total + over_y
    return total


def gather_wide(values, channels, sign, period):
    block = lambda k: values[k * channels : (k + 1) * channels]
    total = None
    for dt in range(3):
        over_y = None
        for dy in range(3):
            part = y_shift(block(dy * 3 + dt), sign * (dy - 1), period)
            over_y = part if over_y is None else over_y + part
        over_y = t_shift(over_y, sign * (dt - 1), period)
        total = over_y if total is None else total + over_y
    return total


def dot(a, b):
    return jnp.dot(a, b, preferred_element_type=F32)


def dot_nt(a, b):
    return lax.dot_general(a, b, (((1,), (1,)), ((), ())), preferred_element_type=F32)


def stack_planes(stack, planes, channels, order):
    length = stack.shape[1]
    for dx in range(3):
        for dz in range(3):
            plane, step = order(dx, dz)
            rows = pl.ds((dx * 3 + dz) * channels, channels)
            source = planes[plane * channels : (plane + 1) * channels, :]
            if step == 0:
                stack[rows, :] = source
            elif step == 1:
                stack[rows, : length - 128] = source[:, 128:]
                stack[rows, length - 128 :] = source[:, :128]
            else:
                stack[rows, 128:] = source[:, : length - 128]
                stack[rows, :128] = source[:, length - 128 :]


def identity(n):
    row = lax.broadcasted_iota(jnp.int32, (n, n), 0)
    return (row == lax.broadcasted_iota(jnp.int32, (n, n), 1)).astype(F32).astype(BF)


def pack_ahead_kernel(layer, ready, w_mid, w_first, w_last, biases, lanes, spread_rows, *refs):
    matrix, first, narrow, columns, taps, rows = refs[-6:]
    channels = w_mid.shape[1]
    few = channels // 2
    for o in range(few):
        pair = jnp.concatenate([w_mid[layer, o], w_mid[layer, o + few]], axis=0)
        taps[pl.ds(o, TAPS, stride=few), :] = dot_nt(identity(TAPS), pair)

    def block(tap):
        both = taps[tap * few : (tap + 1) * few, :]
        return jnp.concatenate([both[:, :channels], both[:, channels:]], axis=0)

    for inner in range(9):
        at = pl.ds(inner * channels, channels)
        for outer in range(0, 9, 2):
            low = block(outer * 9 + inner)
            if outer < 8:
                high = block(outer * 9 + 9 + inner)
                wide = slice(outer * channels, (outer + 2) * channels)
                matrix[at, wide] = jnp.concatenate([low, high], axis=1).astype(BF)
            else:
                matrix[at, outer * channels :] = low.astype(BF)
    first[...] = dot(w_first[layer], lanes[...]).astype(BF)
    for dx in range(3):
        narrow[dx] = sum(
            dot_nt(spread_rows[(dx * 2 + o) * 216 : (dx * 2 + o + 1) * 216, :TAPS], w_last[layer, o])
            for o in range(2)
        ).astype(BF)
    rows[...] = jnp.zeros_like(rows)
    rows[0:3, :channels] = biases[3 * layer : 3 * layer + 3, :]
    columns[...] = rows[...].T


def pack_back_kernel(ready, matrix_zero, matrix_one, w_first, w_last, lanes, spread_rows, *refs):
    outs = refs[-6:]
    channels = w_first.shape[1]
    for layer, matrix in ((0, matrix_zero), (1, matrix_one)):
        last_back, turned, first_back = outs[3 * layer : 3 * layer + 3]
        for inner in range(9):
            at = pl.ds(inner * channels, channels)
            for outer in range(0, 9, 2):
                end = min(outer + 2, 9) * channels
                both = dot_nt(identity(end - outer * channels), matrix[at, outer * channels : end])
                if outer < 8:
                    both = jnp.concatenate([both[:channels], both[channels:]], axis=1)
                turned[at, outer * channels : end] = both.astype(BF)
        first_back[...] = dot_nt(spread_rows[:, :TAPS], w_first[layer]).astype(BF)
        last_back[...] = sum(
            dot(w_last[layer, o], lanes[:, o * 1536 : (o + 1) * 1536]) for o in range(2)
        ).astype(BF)


def unpack_kernel(layout, volume, last, ready, coords, pieces, *refs):
    if last:
        force_in, refs = refs[0], refs[4:]
        g_mid, g_last, g_first, gb_first, gb_mid, gb_last, loss, sample, force = refs[:9]
        bulk, taps, mid, lasts, firsts, sems = refs[9:]
        period = force.shape[3]
        for row, target in ((0, force), (1, sample)):
            for k in range(target.shape[1] * target.shape[2]):
                target[0, k // target.shape[2], k % target.shape[2] : k % target.shape[2] + 1, :] = (
                    force_in[row : row + 1, k * period : (k + 1) * period]
                )
    else:
        g_mid, g_last, g_first = refs[:3]
        bulk, taps, mid, lasts, firsts, sems = refs[3:]
    channels = g_mid.shape[2]
    few = channels // 2
    halves, depth, chunk = layout
    g, y, z = coords[1], coords[3], coords[4]
    core = 1 - coords[2] if last else coords[2]
    per_layer = 2 * halves * depth * chunk
    at = 0
    for rg in range(halves):
        for ry in range(2):
            for rz in range(depth):
                to = ((lax.rem(g + rg, halves) * 2 + (1 - y if ry else y)) * depth
                      + (z ^ rz)) * chunk
                for layer in range(2):
                    bulk[layer, pl.ds(pl.multiple_of(to, 16), chunk), :] = pieces[at : at + chunk, :]
                    at += chunk
    rows, pairs = 9 * few, few // 2
    copies = []
    for layer in range(2):
        for tap in range(TAPS):
            outer, inner = divmod(tap, 9)
            start = (outer // 2) * rows + inner * few
            low = (outer % 2) * channels
            both = bulk[layer, start : start + few, low : low + channels].astype(F32)
            taps[tap * pairs : (tap + 1) * pairs, :channels] = both[:pairs]
            taps[tap * pairs : (tap + 1) * pairs, channels:] = both[pairs:]
        for o in range(pairs):
            pair = taps[pl.ds(o, TAPS, stride=pairs), :].astype(BF)
            pair = dot_nt(identity(2 * channels), pair) * (1.0 / volume)
            mid[layer, o] = pair[:channels]
            mid[layer, o + pairs] = pair[channels:]
        rest = bulk[layer, 5 * rows : 5 * rows + channels + few, :].astype(F32) * (1.0 / volume)
        lasts[layer] = rest[:channels, :TAPS]
        firsts[layer] = rest[channels:, :TAPS]
        if last:
            small = bulk[layer, 4 * rows : 4 * rows + 16, channels:].astype(F32) * (1.0 / volume)
            gb_first[layer : layer + 1, :] = small[0:1]
            gb_mid[layer : layer + 1, :] = small[1:2]
            gb_last[layer : layer + 1, :] = small[2:3, :2]
            if layer == 1:
                loss[...] = jnp.sum(
                    jnp.sum(small[3:6], axis=0, keepdims=True), axis=1, keepdims=True
                )
        copies += [
            pltpu.make_async_copy(
                mid.at[layer], g_mid.at[layer, pl.ds(core * few, few)], sems.at[layer * 3]
            ),
            pltpu.make_async_copy(lasts.at[layer], g_last.at[layer, core], sems.at[layer * 3 + 1]),
            pltpu.make_async_copy(
                firsts.at[layer],
                g_first.at[layer, pl.ds(pl.multiple_of(core * few, few), few)],
                sems.at[layer * 3 + 2],
            ),
        ]
        for copy in copies[-3:]:
            copy.start()
    for copy in copies:
        copy.wait()


def place_windows(refs, row, target):
    target[...] = jnp.zeros_like(target)
    for r, ref in enumerate(refs):
        target[r : r + 1, :] = ref[row : row + 1, :]


def oddness(shape, place, period):
    lane = lax.broadcasted_iota(jnp.int32, shape, 1)
    row = lax.broadcasted_iota(jnp.int32, shape, 0)
    within = lane % 128
    return ((place + row + 1 + lane // 128 + within // period + within % period) % 2).astype(F32)


def forward_kernel(period, layer, halves, ready, *refs):
    windows, refs = refs[:7], refs[7:]
    if layer == 0:
        (coords, w_first, w_mid, w_last, columns,
         field_out, state, own_out, logdet, first_out, second_out, first, stack) = refs
        field_out[...] = jnp.zeros_like(field_out)
        piece = field_out.shape[1] // halves
        for rel in range(halves):
            to = pl.multiple_of(lax.rem(coords[1] + rel, halves) * piece, 128)
            for r, ref in enumerate(windows):
                field_out[r : r + 1, pl.ds(to, piece)] = ref[:, rel * piece : (rel + 1) * piece]
    else:
        (coords, w_first, w_mid, w_last, columns,
         field_out, state, own_out, logdet, growth_out, first_out, second_out,
         first, stack) = refs
        place_windows(windows, 0, field_out)
        place_windows(windows, 1, growth_out)
    channels = w_mid.shape[0] // 9
    field = field_out[...]
    length = field.shape[1]
    frozen = oddness(field.shape, coords[0], period)
    if layer == 1:
        frozen = 1.0 - frozen
    net = frozen * field
    taps = jnp.concatenate(all_shifts(net, 1, period), axis=0).astype(BF)
    ready(w_first, columns)
    bias_first, bias_mid = columns[:channels, 0:1], columns[:channels, 1:2]
    for dest in range(5):
        part = dot(w_first[:, dest * 256 : dest * 256 + 216], taps)
        first[dest * channels : (dest + 1) * channels, :] = jnp.tanh(part + bias_first).astype(BF)
    first_out[...] = first[channels : 4 * channels, :]
    ready(w_mid)
    for dest in range(3):
        stack_planes(stack, first, channels, lambda dx, dz: (dest + dx, dz - 1))
        for at in range(0, length, 256):
            wide = dot(w_mid[...], stack[:, at : at + 256])
            wide = gather_wide(wide, channels, 1, period)
            second_out[dest * channels : (dest + 1) * channels, at : at + 256] = jnp.tanh(
                wide + bias_mid
            ).astype(BF)
    ready(w_last)
    narrow = sum(
        dot(w_last[dx], second_out[dx * channels : (dx + 1) * channels, :]) for dx in range(3)
    )
    narrow = gather_narrow(narrow, 1, period) + columns[:8, 2:3]
    growth = jnp.exp(narrow[0:1])
    mine = field[MID : MID + 1]
    still = frozen[MID : MID + 1]
    moving = 1.0 - still
    state[0:1, :] = still * mine + moving * (mine * growth + narrow[1:2])
    state[1:2, :] = growth
    own_out[...] = state[0:1, :]
    flow = moving * narrow[0:1]
    logdet[...] = sum(flow[:, at : at + 128] for at in range(0, length, 128))


def put_chunks(layout, coords, bulks, send, keep):
    halves, depth, chunk = layout
    per_core = bulks[0].shape[0] // 2
    g, c, y, z = (coords[i] for i in range(1, 5))
    for core, ref in ((c, keep), (1 - c, send)):
        at = 0
        for ry in range(2):
            for rz in range(depth):
                source = core * per_core + (
                    (g * 2 + (1 - y if ry else y)) * depth + (z ^ rz)
                ) * chunk
                for bulk in bulks:
                    ref[at : at + chunk, :] = bulk[pl.ds(pl.multiple_of(source, 16), chunk), :]
                    at += chunk


def output_taps(grad_output, period):
    return jnp.concatenate(all_shifts(grad_output, -1, period), axis=0).astype(BF)


def output_gradient(upstream, moving, field, grow):
    place = lax.broadcasted_iota(jnp.int32, (2 * ROWS, field.shape[1]), 0) % ROWS
    grad_scale = upstream * moving * field * grow - moving
    grad_shift = upstream * moving
    both = jnp.concatenate([grad_scale, grad_shift], axis=0)
    return jnp.where(jnp.logical_and(place >= 1, place <= 5), both, 0.0)


def second_gradient(w_last, second, taps, mids):
    channels = mids.shape[0] // 3
    for dest in range(3):
        part = dot(w_last[:, dest * 512 : dest * 512 + 432], taps)
        rows = slice(dest * channels, (dest + 1) * channels)
        wide = second[rows, :].astype(F32)
        mids[rows, :] = (part * (1.0 - wide * wide)).astype(BF)


def first_gradient(period, mids, first, w_mid, stack, grad_first):
    channels = mids.shape[0] // 3
    stack_planes(stack, mids, channels, lambda dx, dz: (2 - dx, 1 - dz))
    for at in range(0, stack.shape[1], 256):
        wide = dot(w_mid[...], stack[:, at : at + 256])
        wide = gather_wide(wide, channels, -1, period)
        seen = first[channels : 2 * channels, at : at + 256].astype(F32)
        grad_first[:, at : at + 256] = (wide * (1.0 - seen * seen)).astype(BF)


def first_weights(period, net, grad_first, pick_f):
    taps = jnp.concatenate(all_shifts(net, 1, period), axis=0).astype(BF)
    g_first = dot_nt(grad_first, taps).astype(BF)
    return dot(g_first, pick_f)


def fill_bulk(period, mids, first, second, taps, pick_l, g_first, small, stack, turned, bulk):
    channels = mids.shape[0] // 3
    few = channels // 2
    own = slice(channels, 2 * channels)
    rounded = mids[own, :].astype(F32)
    in_t = [t_shift(rounded, -dt, period) for dt in STEPS]
    for dy in range(3):
        for dt in range(3):
            turned[(dy * 3 + dt) * channels : (dy * 3 + dt + 1) * channels, :] = y_shift(
                in_t[dt], -STEPS[dy], period
            ).astype(BF)
    stack_planes(stack, first, channels, lambda dx, dz: (dx, dz - 1))
    g_mid = dot_nt(turned[...], stack[...]).astype(BF)
    per_core = bulk.shape[0] // 2
    rows = 9 * few
    g_last = dot_nt(second[own, :], taps).astype(BF)
    g_last = dot(g_last, pick_l).astype(BF)
    for core in range(2):
        base = core * per_core
        for b in range(5):
            for inner in range(9):
                at = inner * channels + core * few
                part = g_mid[at : at + few, b * 128 : (b + 1) * 128]
                if part.shape[1] < 128:
                    part = jnp.concatenate([part, jnp.zeros((few, 128 - part.shape[1]), BF)], axis=1)
                to = base + b * rows + inner * few
                bulk[to : to + few, :] = part
        at = base + 4 * rows
        bulk[at : at + 16, channels:] = small.astype(BF)
        at = base + 5 * rows
        bulk[at : at + channels, :] = g_last[:, core * 128 : (core + 1) * 128]
        bulk[at + channels : at + channels + few, :] = g_first[core * few : (core + 1) * few, :].astype(BF)
        at += channels + few
        if at < base + per_core:
            bulk[at : base + per_core, :] = jnp.zeros((base + per_core - at, 128), BF)


def bias_rows(small, grad_output, mids, grad_first):
    channels = mids.shape[0] // 3
    ones = jnp.ones((8, mids.shape[1]), BF)
    small[0:1, :] = dot_nt(ones, grad_first)[0:1]
    small[1:2, :] = dot_nt(ones, mids[channels : 2 * channels, :])[0:1]
    sums = dot_nt(ones, grad_output.astype(BF))
    small[2:3, 0:1] = sums[0:1, MID : MID + 1]
    small[2:3, 1:2] = sums[0:1, 8 + MID : 9 + MID]


def back_one_kernel(period, ready, *refs):
    windows, refs = refs[:7], refs[7:]
    (logdet0, logdet1, coords, field_in, first_in, second_in, w_last, w_mid, w_first,
     base_out, part_out, small, grad_out, mids, grad_first, field_end, growth, stack) = refs
    place_windows(windows, 0, field_end)
    place_windows(windows, 1, growth)
    frozen = 1.0 - oddness(field_in.shape, coords[0], period)
    moving = 1.0 - frozen
    field = field_end[...]
    ahead = (
        pltpu.roll(field, ROWS - 1, 0)
        + z_shift(field, 1)
        + y_shift(field, 1, period)
        + t_shift(field, 1, period)
    )
    behind = (
        pltpu.roll(field, 1, 0)
        + z_shift(field, -1)
        + y_shift(field, -1, period)
        + t_shift(field, -1, period)
    )
    squared = field * field
    density = (
        -2.0 * hopping * field * ahead + squared + quartic * (squared - 1.0) * (squared - 1.0)
    )[MID : MID + 1]
    action = sum(density[:, at : at + 128] for at in range(0, field.shape[1], 128))
    loss = jnp.sum(action - logdet0[...] - logdet1[...], axis=1, keepdims=True)
    small[...] = jnp.zeros_like(small)
    slot = lax.broadcasted_iota(jnp.int32, (1, small.shape[1]), 1) == coords[0]
    for part in range(3):
        top = loss.astype(BF).astype(F32)
        small[3 + part : 4 + part, :] = jnp.where(slot, top, 0.0)
        loss = loss - top
    place = lax.broadcasted_iota(jnp.int32, field.shape, 0)
    upstream = (
        -2.0 * hopping * (ahead + behind) + 2.0 * field + 4.0 * quartic * (squared - 1.0) * field
    )
    upstream = jnp.where(jnp.logical_and(place >= 1, place <= 5), upstream, 0.0)
    grow = growth[...]
    grad_out[...] = output_gradient(upstream, moving, field_in[...], grow)
    base_out[...] = upstream * (frozen + moving * grow)
    taps = output_taps(grad_out[...], period)
    ready(w_last, second_in)
    second_gradient(w_last, second_in, taps, mids)
    ready(w_mid, first_in)
    first_gradient(period, mids, first_in, w_mid, stack, grad_first)
    bias_rows(small, grad_out[...], mids, grad_first[...])
    ready(w_first)
    narrow = gather_narrow(dot(w_first[...], grad_first[...]), -1, period)
    for d in range(3):
        part_out[d : d + 1, :] = frozen[MID - 1 + d : MID + d] * narrow[d : d + 1]


def weights_one_kernel(period, ready, coords, field_in, first_in, second_in, grad_out, mids, grad_first, small,
                       pick_l, pick_f, bulk, stack, turned):
    taps = output_taps(grad_out[...], period)
    frozen = 1.0 - oddness(field_in.shape, coords[0], period)
    ready(first_in, second_in, pick_l, pick_f)
    g_first = first_weights(period, frozen * field_in[...], grad_first[...], pick_f[...])
    fill_bulk(
        period, mids, first_in, second_in, taps, pick_l[...], g_first, small[...], stack, turned, bulk
    )


def back_zero_kernel(period, layout, ready, *refs):
    windows, refs = refs[:7], refs[7:]
    (base_in, growth, own_in, coords, field_in, bulk_one, first_in, second_in, w_last, w_mid, w_first,
     pick_l, pick_f,
     part_low, part_mid, part_high, send, keep,
     upstream_ref, mids, stack, turned, bulk, grad_first, small) = refs
    frozen = oddness(field_in.shape, coords[0], period)
    upstream_ref[...] = base_in[...]
    for r in range(1, 6):
        upstream_ref[r : r + 1, :] += (
            windows[r - 1][2:3, :] + windows[r][1:2, :] + windows[r + 1][0:1, :]
        )
    grad_output = output_gradient(upstream_ref[...], 1.0 - frozen, field_in[...], growth[...])
    taps = output_taps(grad_output, period)
    ready(w_last, second_in)
    second_gradient(w_last, second_in, taps, mids)
    ready(w_mid, first_in)
    first_gradient(period, mids, first_in, w_mid, stack, grad_first)
    small[...] = jnp.zeros_like(small)
    bias_rows(small, grad_output, mids, grad_first[...])
    ready(w_first, pick_f, pick_l)
    g_first = first_weights(period, frozen * field_in[...], grad_first[...], pick_f[...])
    fill_bulk(
        period, mids, first_in, second_in, taps, pick_l[...], g_first, small[...], stack, turned, bulk
    )
    ready(bulk_one)
    put_chunks(layout, coords, (bulk, bulk_one), send, keep)
    narrow = gather_narrow(dot(w_first[...], grad_first[...]), -1, period)
    base = upstream_ref[...] * (frozen + (1.0 - frozen) * growth[...])
    for d in range(3):
        row = frozen[MID - 1 + d : MID + d] * narrow[d : d + 1]
        if d == 1:
            row = row + base[MID : MID + 1]
        if d == 1:
            part_mid[0:1, :] = row
        else:
            (part_low if d == 0 else part_high)[...] = row
    part_mid[1:2, :] = own_in[...]


def force_kernel(ready, coords, above, middle, below, out):
    piece = out.shape[1]
    lanes = pl.ds(pl.multiple_of(coords[1] * piece, 128), piece)
    out[0:1, :] = above[:, lanes] + middle[0:1, lanes] + below[:, lanes]
    out[1:2, :] = middle[1:2, lanes]


def stage(jobs, after=()):
    arrays, outs, plan = [], [], []
    for kind, parts, group in jobs:
        first = len(arrays)
        arrays += group
        rows = group[0].shape[0]
        if kind == "split":
            sizes = [rows // parts] * parts
        elif kind == "sum":
            sizes = [rows]
        else:
            sizes = [sum(a.shape[0] for a in group)]
        plan.append((kind, first, len(group), len(outs), sizes))
        outs += [shape((n, 128), BF) for n in sizes]
    waits = len(after)

    def body(_, *refs):
        ins, results = refs[: len(arrays)], refs[len(arrays) + waits :]
        for kind, first, many, out, sizes in plan:
            group = ins[first : first + many]
            if kind == "join":
                at = 0
                for ref in group:
                    results[out][at : at + ref.shape[0], :] = ref[...]
                    at += ref.shape[0]
                continue
            at = 0
            for i, n in enumerate(sizes):
                results[out + i][...] = sum(ref[at : at + n, :].astype(F32) for ref in group).astype(BF)
                at += n

    got = kernel_call(body, outs, [], [*arrays, *after], 1_000_000, loose=after, vmem=12, bytes_moved=500_000)
    groups, at = [], 0
    for _, _, _, _, sizes in plan:
        groups.append(list(got[at : at + len(sizes)]))
        at += len(sizes)
    return groups


SMEM = pl.BlockSpec(memory_space=pltpu.SMEM)
VMEM = pl.BlockSpec(memory_space=pltpu.VMEM)
HBM = pl.BlockSpec(memory_space=pltpu.HBM)


HERE = "here"


def locate():
    index = lax.axis_index("xy")
    depth = lax.axis_size("xy") // 4
    core, y, z = index % 2, index // 2 % 2, index // 4
    chip = jnp.where(y == 0, z, 2 * depth - 1 - z)
    place = 2 * chip + jnp.where(chip % 2 == 0, core, 1 - core)
    return place, lax.axis_index("gz"), core, y, z


def kernel_call(body, outs, scratch, args, flops, late=(), loose=(), hbm_outs=0, aliases=None,
                vmem=VMEM_MB, bytes_moved=4_000_000):
    here = next((i for i, a in enumerate(args) if a is HERE), None)
    args = [a for a in args if a is not HERE]
    late = [id(a) for a in late]
    loose = [id(a) for a in loose]
    spec = lambda a: HBM if id(a) in late or id(a) in loose else VMEM
    where = [i for i, a in enumerate(args) if id(a) in late]
    many, extra = len(args), len(where)

    def whole(*refs):
        refs = list(refs)
        ins, rest = refs[:many], refs[many:]
        if extra:
            held, sems = rest[len(rest) - extra - 1 : -1], rest[-1]
            rest = rest[: len(rest) - extra - 1]
        waits = {}
        for n, i in enumerate(where):
            copy = pltpu.make_async_copy(ins[i], held[n], sems.at[n])
            copy.start()
            waits[id(held[n])] = copy
            ins[i] = held[n]

        def ready(*wanted):
            for ref in wanted:
                copy = waits.pop(id(ref), None)
                if copy is not None:
                    copy.wait()

        if here is not None:
            ins.insert(here, locate())
        body(ready, *ins, *rest)
        for copy in waits.values():
            copy.wait()

    held = [pltpu.VMEM(args[i].shape, args[i].dtype) for i in where]
    if extra:
        held.append(pltpu.SemaphoreType.DMA((extra,)))
    return pl.pallas_call(
        whole,
        out_shape=tuple(outs),
        in_specs=[spec(a) for a in args],
        out_specs=tuple([VMEM] * (len(outs) - hbm_outs) + [HBM] * hbm_outs),
        scratch_shapes=[*scratch, *held],
        input_output_aliases=aliases or {},
        compiler_params=pltpu.CompilerParams(vmem_limit_bytes=vmem * 2**20),
        cost_estimate=pl.CostEstimate(flops=flops, bytes_accessed=bytes_moved, transcendentals=0),
    )(*args)


def shape(dims, dtype=F32):
    return jax.ShapeDtypeStruct(dims, dtype)


def forward(period, layer, windows, coords, weights, channels, halves):
    length = windows[0].shape[1]
    outs = [
        shape((ROWS, length)),
        shape((2, length)),
        shape((1, length)),
        shape((1, 128)),
    ]
    if layer == 1:
        outs.append(shape((ROWS, length)))
    args = [*windows, coords, *weights]
    outs += [shape((3 * channels, length), BF)] * 2
    scratch = [
        pltpu.VMEM((5 * channels, length), BF),
        pltpu.VMEM((9 * channels, length), BF),
    ]
    body = functools.partial(forward_kernel, period, layer, halves)
    flops = 3 * 2 * TAPS * channels * channels * length
    return kernel_call(body, outs, scratch, args, flops)


def pack_ahead(layer, params, picks, after=()):
    channels = params[0].shape[1]
    outs = [
        shape((9 * channels, 9 * channels), BF),
        shape((channels, 5 * 256), BF),
        shape((3, 216, channels), BF),
        shape((128, 8)),
    ]
    scratch = [pltpu.VMEM((TAPS * channels // 2, 2 * channels), F32), pltpu.VMEM((8, 128), F32)]
    body = functools.partial(pack_ahead_kernel, layer)
    return kernel_call(body, outs, scratch, [*params, *picks, *after], 1_000_000_000, loose=after)


def pack_back(matrices, narrow, picks, after):
    channels = narrow[0].shape[1]
    outs = [
        shape((channels, 3 * 512), BF),
        shape((9 * channels, 9 * channels), BF),
        shape((216, channels), BF),
    ]
    got = kernel_call(
        pack_back_kernel, outs * 2, [], [*matrices, *narrow, *picks, *after], 1_000_000_000, loose=after
    )
    return got[:3], got[3:]


def unpack(last, layout, volume, coords, pieces, channels, before, force=None, block=None):
    halves, depth, chunk = layout
    few = channels // 2
    arrays = [
        shape((2, channels, channels, TAPS)),
        shape((2, 2, channels, TAPS)),
        shape((2, channels, TAPS)),
    ]
    scratch = [
        pltpu.VMEM((2, 2 * halves * depth * chunk, 128), BF),
        pltpu.VMEM((TAPS * few // 2, 2 * channels), F32),
        pltpu.VMEM((2, few, channels, TAPS), F32),
        pltpu.VMEM((2, channels, TAPS), F32),
        pltpu.VMEM((2, few, TAPS), F32),
        pltpu.SemaphoreType.DMA((6,)),
    ]
    body = functools.partial(unpack_kernel, layout, volume, last)
    if not last:
        return kernel_call(
            body, arrays, scratch, [coords, pieces], 1_000_000_000, hbm_outs=3
        )
    extra = [shape((2, channels)), shape((2, channels)), shape((2, 2)), shape((1, 1)), shape(block), shape(block)]
    new = len(extra)

    def reordered(ready, coords, pieces, *refs):
        ins, outs, rest = refs[:4], refs[4 : 7 + new], refs[7 + new :]
        body(ready, coords, pieces, *ins, *outs[new:], *outs[:new], *rest)

    got = kernel_call(
        reordered, extra + arrays, scratch, [coords, pieces, force, *before], 1_000_000_000,
        loose=before, hbm_outs=3, aliases={2 + i: new + i for i in range(3)},
    )
    return [*got[new:], *got[:new]]


def permuters(count, halves, depth):
    xy = lambda fn: [(fn(a), a) for a in range(count)]

    def core(v):
        return lax.ppermute(v, "xy", xy(lambda a: a ^ 1))

    def y(v):
        return lax.ppermute(v, "xy", xy(lambda a: a ^ 2))

    def scatter(pieces):
        return [lax.ppermute(pieces[s], "xy", xy(lambda a, s=s: a ^ (4 * s))) for s in range(1, depth)]

    def gather(v):
        return [lax.ppermute(v, "xy", xy(lambda a, s=s: a ^ (4 * s))) for s in range(1, depth)]

    def square(v):
        out = []
        for rg in range(halves):
            for ry in range(2):
                if rg or ry:
                    pairs = [
                        ((a ^ (2 * ry)) * halves + (j + rg) % halves, a * halves + j)
                        for a in range(count)
                        for j in range(halves)
                    ]
                    out.append(lax.ppermute(v, ("xy", "gz"), pairs))
        return out

    return core, y, scatter, gather, square


def per_device(noise, w_first, b_first, w_mid, b_mid, w_last, b_last):
    period = noise.shape[3]
    count = lax.axis_size("xy")
    halves = lax.axis_size("gz")
    channels = w_mid.shape[2]
    order = ring_order(count)
    volume = float(noise.size * count * halves)
    depth = count // 4
    coords = HERE
    need = 45 * channels // 2 + channels + channels // 2
    chunk = -(-need // (2 * halves * depth * 16)) * 16
    layout = (halves, depth, chunk)

    def step(values, offset):
        return lax.ppermute(
            values, "xy", [(order[(p + offset) % count], order[p]) for p in range(count)]
        )

    whole = [
        lax.ppermute(
            noise,
            ("xy", "gz"),
            [
                (p * halves + (j + rel) % halves, order[p] * halves + j)
                for p in range(count)
                for j in range(halves)
            ],
        )
        for rel in range(halves)
    ]
    params = [
        w_mid.transpose(0, 2, 3, 1),
        w_first.transpose(0, 2, 3, 1).reshape(2, channels, TAPS),
        w_last.transpose(0, 2, 3, 1),
        jnp.stack([b_first, b_mid, jnp.pad(b_last, ((0, 0), (0, channels - 2)))], axis=1).reshape(6, channels),
    ]
    back = spread_last_back()
    pad = ((0, 0), (0, 128 - TAPS))
    picks = [
        jnp.asarray(spread_first(), BF),
        jnp.asarray(np.pad(spread_last().reshape(6 * 216, TAPS), pad), BF),
    ]
    back_picks = [
        jnp.asarray(np.concatenate([back[0], back[1]], axis=1), BF),
        jnp.asarray(np.pad(spread_first_back(), pad), BF),
    ]
    pick_l, pick_f = jnp.asarray(pick_last(), BF), jnp.asarray(pick_first(), BF)
    packed = [pack_ahead(0, params, picks)]

    def join(ready, *refs):
        rows = noise.shape[1] * noise.shape[2]
        for rel in range(halves):
            for k in range(rows):
                at = (rel * rows + k) * period
                y = k % noise.shape[2]
                refs[-1][:, at : at + period] = refs[rel][0, k // noise.shape[2], y : y + 1, :]

    waits = (packed[0][0],)
    (whole,) = kernel_call(
        join, [shape((1, noise.size * halves))], [], [*whole, *waits], 1000, loose=waits, bytes_moved=1000
    )

    def exchange(values):
        return [values if m == 0 else step(values, m) for m in range(-3, 4)]

    order_weights = lambda p: (p[1], p[0], p[2], p[3])
    field0, state, _, logdet0, first0, second0 = forward(
        period, 0, exchange(whole), coords, order_weights(packed[0]), channels, halves
    )
    packed.append(pack_ahead(1, params, picks, (logdet0,)))
    field1, state, own, logdet1, growth0, first1, second1 = forward(
        period, 1, exchange(state), coords, order_weights(packed[1]), channels, halves
    )
    back_weights = pack_back([p[0] for p in packed], params[1:3], back_picks, (logdet1,))
    core, cross, scatter, gather, square = permuters(count, halves, depth)
    length = field0.shape[1]
    full = shape((ROWS, length))
    planes = shape((3 * channels, length), BF)
    wide = pltpu.VMEM((9 * channels, length), BF)
    bulk = (4 * halves * depth * chunk, 128)
    part = 4 * depth * chunk
    flops = 2 * TAPS * channels * channels * length

    weights = back_weights[1]
    base, parts, small, grad_out, mids, grad_first = kernel_call(
        functools.partial(back_one_kernel, period),
        [full, shape((3, length)), shape((16, channels)), shape((2 * ROWS, length)), planes,
         shape((channels, length), BF)],
        [pltpu.VMEM((ROWS, length), F32), pltpu.VMEM((ROWS, length), F32), wide],
        [*exchange(state), logdet0, logdet1, coords, field1, first1, second1, *weights],
        flops,
    )
    (bulk1,) = kernel_call(
        functools.partial(weights_one_kernel, period),
        [shape(bulk, BF)], [wide, wide],
        [coords, field1, first1, second1, grad_out, mids, grad_first, small, pick_l, pick_f],
        flops,
    )

    weights = back_weights[0]
    low, middle, high, send, keep = kernel_call(
        functools.partial(back_zero_kernel, period, layout),
        [shape((1, length)), shape((2, length)), shape((1, length))]
        + [shape((part, 128), BF)] * 2,
        [pltpu.VMEM((ROWS, length), F32), pltpu.VMEM((3 * channels, length), BF), wide, wide,
         pltpu.VMEM(bulk, BF), pltpu.VMEM((channels, length), BF),
         pltpu.VMEM((16, channels), F32)],
        [*exchange(parts), base, growth0, own, coords, field0, bulk1, first0, second0, *weights,
         pick_l, pick_f],
        2 * flops,
    )

    ((stay, away),) = stage([("split", 2, [keep, core(send)])])
    crossed = cross(away)
    (force,) = kernel_call(
        force_kernel, [shape((2, length // halves))], [],
        [coords, step(low, 1), middle, step(high, -1)], 1000, bytes_moved=1000,
    )
    (pieces,) = stage([("split", depth, [stay, crossed])], after=(force,))
    ((total,),) = stage([("sum", 1, [pieces[0], *scatter(pieces)])])
    ((line,),) = stage([("join", 1, [total, *gather(total)])])
    ((mine,),) = stage([("join", 1, [line, *square(line)])])
    other = core(mine)
    force = lax.ppermute(force, "xy", [(order[p], p) for p in range(count)])
    outs = unpack(False, layout, volume, coords, mine, channels, [])
    g_mid, g_last, g_first, gb_first, gb_mid, gb_last, loss, sample, force = unpack(
        True, layout, volume, coords, other, channels, list(outs), force, noise.shape
    )

    return (
        sample,
        force,
        loss.reshape(()),
        g_first.reshape(2, channels, 1, TAPS).transpose(0, 3, 1, 2),
        gb_first,
        g_mid.transpose(0, 3, 1, 2),
        gb_mid,
        g_last.transpose(0, 3, 1, 2),
        gb_last,
    )


def solution(mesh):
    return jax.shard_map(
        per_device,
        mesh=mesh,
        in_specs=(P("xy", "gz", None, None), P(), P(), P(), P(), P(), P()),
        out_specs=(
            P("xy", "gz", None, None),
            P("xy", "gz", None, None),
            P(),
            P(),
            P(),
            P(),
            P(),
            P(),
            P(),
        ),
        check_vma=False,
    )
```

```python
import functools

import jax
import jax.numpy as jnp
import numpy as np
from jax import lax
from jax.experimental import pallas as pl
from jax.experimental.pallas import tpu as pltpu
from jax.sharding import PartitionSpec as P

hopping = 0.3
quartic = 0.05

STEPS = (-1, 0, 1)
ROWS = 8
MID = 3
BF = jnp.bfloat16
F32 = jnp.float32
TAPS = 81
VMEM_MB = 20
CHUNK = 512


def ring_order(count):
    if count % 4:
        return list(range(count))
    depth = count // 4
    chips = [(z, 0) for z in range(depth)] + [(z, 1) for z in reversed(range(depth))]
    order = []
    for place, (z, y) in enumerate(chips):
        cores = (0, 1) if place % 2 == 0 else (1, 0)
        order += [z * 4 + y * 2 + core for core in cores]
    return order


def spread_last_back():
    out = np.zeros((2, 81, 3, 512), np.float32)
    for tap in range(81):
        dx, rest = divmod(tap, 27)
        for o in range(2):
            for dest in range(3):
                out[o, tap, dest, rest * 16 + o * ROWS + 2 + dest - (dx - 1)] = 1
    return out.reshape(2, 81, 3 * 512)


def spread_first_back():
    out = np.zeros((216, 81), np.float32)
    for tap in range(81):
        dx, rest = divmod(tap, 27)
        out[rest * 8 + dx, tap] = 1
    return out


def pick_last():
    out = np.zeros((432, 2, 128), np.float32)
    for tap in range(81):
        dx, rest = divmod(tap, 27)
        for o in range(2):
            out[rest * 16 + o * ROWS + MID - (dx - 1), o, tap] = 1
    return out.reshape(432, 256)


def pick_first():
    out = np.zeros((216, 128), np.float32)
    for tap in range(81):
        dx, rest = divmod(tap, 27)
        out[rest * ROWS + MID + dx - 1, tap] = 1
    return out


def z_shift(values, dz):
    length = values.shape[1]
    return values if dz == 0 else pltpu.roll(values, (-dz * 128) % length, 1)


def by_plane(values, fn):
    parts = [fn(values[:, at : at + 128]) for at in range(0, values.shape[1], 128)]
    return parts[0] if len(parts) == 1 else jnp.concatenate(parts, axis=1)


def y_shift(values, dy, period):
    if dy == 0:
        return values
    return by_plane(values, lambda v: pltpu.roll(v, (-dy * period) % 128, 1))


def t_shift(values, dt, period):
    if dt == 0:
        return values

    def one(v):
        place = lax.broadcasted_iota(jnp.int32, v.shape, 1) % period
        main = pltpu.roll(v, (-dt) % 128, 1)
        wrap = pltpu.roll(v, (dt * (period - 1)) % 128, 1)
        return jnp.where(place == (period - 1 if dt == 1 else 0), wrap, main)

    return by_plane(values, one)


def all_shifts(values, sign, period):
    in_t = [t_shift(values, sign * dt, period) for dt in STEPS]
    in_y = [[y_shift(v, sign * dy, period) for v in in_t] for dy in STEPS]
    return [z_shift(in_y[dy][dt], sign * dz) for dz in STEPS for dy in range(3) for dt in range(3)]


def gather_narrow(values, sign, period):
    block = lambda k: values[k * 8 : k * 8 + 8]
    total = None
    for dt in range(3):
        over_y = None
        for dy in range(3):
            over_z = sum(z_shift(block(dz * 9 + dy * 3 + dt), sign * (dz - 1)) for dz in range(3))
            over_z = y_shift(over_z, sign * (dy - 1), period)
            over_y = over_z if over_y is None else over_y + over_z
        over_y = t_shift(over_y, sign * (dt - 1), period)
        total = over_y if total is None else total + over_y
    return total


def gather_wide(values, channels, sign, period):
    block = lambda k: values[k * channels : (k + 1) * channels]
    total = None
    for dt in range(3):
        over_y = None
        for dy in range(3):
            part = y_shift(block(dy * 3 + dt), sign * (dy - 1), period)
            over_y = part if over_y is None else over_y + part
        over_y = t_shift(over_y, sign * (dt - 1), period)
        total = over_y if total is None else total + over_y
    return total


def dot(a, b):
    return jnp.dot(a, b, preferred_element_type=F32)


def dot_nt(a, b):
    return lax.dot_general(a, b, (((1,), (1,)), ((), ())), preferred_element_type=F32)


def stack_planes(stack, planes, channels, order):
    length = stack.shape[1]
    for dx in range(3):
        for dz in range(3):
            plane, step = order(dx, dz)
            rows = pl.ds((dx * 3 + dz) * channels, channels)
            source = planes[plane * channels : (plane + 1) * channels, :]
            if step == 0:
                stack[rows, :] = source
            elif step == 1:
                stack[rows, : length - 128] = source[:, 128:]
                stack[rows, length - 128 :] = source[:, :128]
            else:
                stack[rows, 128:] = source[:, : length - 128]
                stack[rows, :128] = source[:, length - 128 :]


def identity(n):
    row = lax.broadcasted_iota(jnp.int32, (n, n), 0)
    return (row == lax.broadcasted_iota(jnp.int32, (n, n), 1)).astype(F32).astype(BF)


def pack_ahead_kernel(layer, ready, w_mid, *refs):
    matrix, taps = refs[-2:]
    channels = w_mid.shape[1]
    few = channels // 2
    for o in range(few):
        pair = jnp.concatenate([w_mid[layer, o], w_mid[layer, o + few]], axis=0)
        taps[pl.ds(o, TAPS, stride=few), :] = dot_nt(identity(TAPS), pair)

    def block(tap):
        both = taps[tap * few : (tap + 1) * few, :]
        return jnp.concatenate([both[:, :channels], both[:, channels:]], axis=0)

    for inner in range(9):
        at = pl.ds(inner * channels, channels)
        for outer in range(0, 9, 2):
            low = block(outer * 9 + inner)
            if outer < 8:
                high = block(outer * 9 + 9 + inner)
                wide = slice(outer * channels, (outer + 2) * channels)
                matrix[at, wide] = jnp.concatenate([low, high], axis=1).astype(BF)
            else:
                matrix[at, outer * channels :] = low.astype(BF)


def pack_narrow_kernel(ready, w_first, w_last, biases, *refs):
    outs, rows = refs[-7:-1], refs[-1]
    channels = w_first.shape[1]
    tap = lax.broadcasted_iota(jnp.int32, (TAPS, 256), 0)
    column = lax.broadcasted_iota(jnp.int32, (TAPS, 256), 1)
    for dest in range(5):
        dx = column % ROWS - dest
        hit = jnp.logical_and(tap == dx * 27 + column // ROWS, jnp.logical_and(dx >= 0, dx <= 2))
        hit = jnp.logical_and(hit, column < 27 * ROWS).astype(F32).astype(BF)
        for layer in range(2):
            outs[3 * layer][:, dest * 256 : (dest + 1) * 256] = dot(w_first[layer], hit).astype(BF)
    row = lax.broadcasted_iota(jnp.int32, (216, TAPS), 0)
    tap = lax.broadcasted_iota(jnp.int32, (216, TAPS), 1)
    for dx in range(3):
        hit = tap == dx * 27 + row // 8
        hits = [jnp.logical_and(hit, row % 8 == o).astype(F32).astype(BF) for o in range(2)]
        for layer in range(2):
            outs[3 * layer + 1][dx] = sum(dot_nt(hits[o], w_last[layer, o]) for o in range(2)).astype(BF)
    for layer in range(2):
        rows[...] = jnp.zeros_like(rows)
        rows[0:3, :channels] = biases[3 * layer : 3 * layer + 3, :]
        outs[3 * layer + 2][...] = rows[...].T


def pack_back_kernel(ready, matrix_zero, matrix_one, w_first, w_last, lanes, spread_rows, *refs):
    outs = refs[-6:]
    channels = w_first.shape[1]
    for layer, matrix in ((0, matrix_zero), (1, matrix_one)):
        last_back, turned, first_back = outs[3 * layer : 3 * layer + 3]
        for inner in range(9):
            at = pl.ds(inner * channels, channels)
            for outer in range(0, 9, 2):
                end = min(outer + 2, 9) * channels
                both = dot_nt(identity(end - outer * channels), matrix[at, outer * channels : end])
                if outer < 8:
                    both = jnp.concatenate([both[:channels], both[channels:]], axis=1)
                turned[at, outer * channels : end] = both.astype(BF)
        first_back[...] = dot_nt(spread_rows[:, :TAPS], w_first[layer]).astype(BF)
        last_back[...] = sum(
            dot(w_last[layer, o], lanes[:, o * 1536 : (o + 1) * 1536]) for o in range(2)
        ).astype(BF)


def unpack_kernel(layout, volume, last, ready, coords, pieces, *refs):
    if last:
        force_in, refs = refs[0], refs[4:]
        g_mid, g_last, g_first, gb_first, gb_mid, gb_last, loss, sample, force = refs[:9]
        bulk, taps, mid, lasts, firsts, sems = refs[9:]
        period = force.shape[3]
        for row, target in ((0, force), (1, sample)):
            for k in range(target.shape[1] * target.shape[2]):
                target[0, k // target.shape[2], k % target.shape[2] : k % target.shape[2] + 1, :] = (
                    force_in[row : row + 1, k * period : (k + 1) * period]
                )
    else:
        g_mid, g_last, g_first = refs[:3]
        bulk, taps, mid, lasts, firsts, sems = refs[3:]
    channels = g_mid.shape[2]
    few = channels // 2
    halves, depth, chunk = layout
    g, y, z = coords[1], coords[3], coords[4]
    core = 1 - coords[2] if last else coords[2]
    per_layer = 2 * halves * depth * chunk
    at = 0
    for rg in range(halves):
        for ry in range(2):
            for rz in range(depth):
                to = ((lax.rem(g + rg, halves) * 2 + (1 - y if ry else y)) * depth
                      + (z ^ rz)) * chunk
                for layer in range(2):
                    bulk[layer, pl.ds(pl.multiple_of(to, 16), chunk), :] = pieces[at : at + chunk, :]
                    at += chunk
    rows, pairs = 9 * few, few // 2
    copies = []
    for layer in range(2):
        for tap in range(TAPS):
            outer, inner = divmod(tap, 9)
            start = (outer // 2) * rows + inner * few
            low = (outer % 2) * channels
            both = bulk[layer, start : start + few, low : low + channels].astype(F32)
            taps[tap * pairs : (tap + 1) * pairs, :channels] = both[:pairs]
            taps[tap * pairs : (tap + 1) * pairs, channels:] = both[pairs:]
        for o in range(pairs):
            pair = taps[pl.ds(o, TAPS, stride=pairs), :].astype(BF)
            pair = dot_nt(identity(2 * channels), pair) * (1.0 / volume)
            mid[layer, o] = pair[:channels]
            mid[layer, o + pairs] = pair[channels:]
        rest = bulk[layer, 5 * rows : 5 * rows + channels + few, :].astype(F32) * (1.0 / volume)
        lasts[layer] = rest[:channels, :TAPS]
        firsts[layer] = rest[channels:, :TAPS]
        if last:
            small = bulk[layer, 4 * rows : 4 * rows + 16, channels:].astype(F32) * (1.0 / volume)
            gb_first[layer : layer + 1, :] = small[0:1]
            gb_mid[layer : layer + 1, :] = small[1:2]
            gb_last[layer : layer + 1, :] = small[2:3, :2]
            if layer == 1:
                loss[...] = jnp.sum(
                    jnp.sum(small[3:6], axis=0, keepdims=True), axis=1, keepdims=True
                )
        copies += [
            pltpu.make_async_copy(
                mid.at[layer], g_mid.at[layer, pl.ds(core * few, few)], sems.at[layer * 3]
            ),
            pltpu.make_async_copy(lasts.at[layer], g_last.at[layer, core], sems.at[layer * 3 + 1]),
            pltpu.make_async_copy(
                firsts.at[layer],
                g_first.at[layer, pl.ds(pl.multiple_of(core * few, few), few)],
                sems.at[layer * 3 + 2],
            ),
        ]
        for copy in copies[-3:]:
            copy.start()
    for copy in copies:
        copy.wait()


def place_windows(refs, row, target):
    target[...] = jnp.zeros_like(target)
    for r, ref in enumerate(refs):
        target[r : r + 1, :] = ref[row : row + 1, :]


def oddness(shape, place, period):
    lane = lax.broadcasted_iota(jnp.int32, shape, 1)
    row = lax.broadcasted_iota(jnp.int32, shape, 0)
    within = lane % 128
    return ((place + row + 1 + lane // 128 + within // period + within % period) % 2).astype(F32)


def forward_kernel(period, layer, halves, ready, *refs):
    windows, refs = refs[:7], refs[7:]
    if layer == 0:
        (coords, w_first, w_mid, w_last, columns,
         field_out, state, own_out, logdet, first_out, second_out, first, stack) = refs
        place_windows(windows, 0, field_out)
    else:
        (coords, w_first, w_mid, w_last, columns,
         field_out, state, own_out, logdet, growth_out, first_out, second_out,
         first, stack) = refs
        place_windows(windows, 0, field_out)
        place_windows(windows, 1, growth_out)
    channels = w_mid.shape[0] // 9
    field = field_out[...]
    length = field.shape[1]
    frozen = oddness(field.shape, coords[0], period)
    if layer == 1:
        frozen = 1.0 - frozen
    net = frozen * field
    taps = jnp.concatenate(all_shifts(net, 1, period), axis=0).astype(BF)
    ready(w_first, columns)
    bias_first, bias_mid = columns[:channels, 0:1], columns[:channels, 1:2]
    for dest in range(5):
        part = dot(w_first[:, dest * 256 : dest * 256 + 216], taps)
        first[dest * channels : (dest + 1) * channels, :] = jnp.tanh(part + bias_first).astype(BF)
    first_out[...] = first[channels : 4 * channels, :]
    ready(w_mid)
    for dest in range(3):
        stack_planes(stack, first, channels, lambda dx, dz: (dest + dx, dz - 1))
        for at in range(0, length, CHUNK):
            wide = dot(w_mid[...], stack[:, at : at + CHUNK])
            wide = gather_wide(wide, channels, 1, period)
            second_out[dest * channels : (dest + 1) * channels, at : at + CHUNK] = jnp.tanh(
                wide + bias_mid
            ).astype(BF)
    ready(w_last)
    narrow = sum(
        dot(w_last[dx], second_out[dx * channels : (dx + 1) * channels, :]) for dx in range(3)
    )
    narrow = gather_narrow(narrow, 1, period) + columns[:8, 2:3]
    growth = jnp.exp(narrow[0:1])
    mine = field[MID : MID + 1]
    still = frozen[MID : MID + 1]
    moving = 1.0 - still
    state[0:1, :] = still * mine + moving * (mine * growth + narrow[1:2])
    state[1:2, :] = growth
    own_out[...] = state[0:1, :]
    flow = moving * narrow[0:1]
    logdet[...] = sum(flow[:, at : at + 128] for at in range(0, length, 128))


def put_chunks(layout, coords, bulks, send, keep):
    halves, depth, chunk = layout
    per_core = bulks[0].shape[0] // 2
    g, c, y, z = (coords[i] for i in range(1, 5))
    for core, ref in ((c, keep), (1 - c, send)):
        at = 0
        for ry in range(2):
            for rz in range(depth):
                source = core * per_core + (
                    (g * 2 + (1 - y if ry else y)) * depth + (z ^ rz)
                ) * chunk
                for bulk in bulks:
                    ref[at : at + chunk, :] = bulk[pl.ds(pl.multiple_of(source, 16), chunk), :]
                    at += chunk


def output_taps(grad_output, period):
    return jnp.concatenate(all_shifts(grad_output, -1, period), axis=0).astype(BF)


def output_gradient(upstream, moving, field, grow):
    place = lax.broadcasted_iota(jnp.int32, (2 * ROWS, field.shape[1]), 0) % ROWS
    grad_scale = upstream * moving * field * grow - moving
    grad_shift = upstream * moving
    both = jnp.concatenate([grad_scale, grad_shift], axis=0)
    return jnp.where(jnp.logical_and(place >= 1, place <= 5), both, 0.0)


def second_gradient(w_last, second, taps, mids):
    channels = mids.shape[0] // 3
    for dest in range(3):
        part = dot(w_last[:, dest * 512 : dest * 512 + 432], taps)
        rows = slice(dest * channels, (dest + 1) * channels)
        wide = second[rows, :].astype(F32)
        mids[rows, :] = (part * (1.0 - wide * wide)).astype(BF)


def first_gradient(period, mids, first, w_mid, stack, grad_first):
    channels = mids.shape[0] // 3
    stack_planes(stack, mids, channels, lambda dx, dz: (2 - dx, 1 - dz))
    for at in range(0, stack.shape[1], CHUNK):
        wide = dot(w_mid[...], stack[:, at : at + CHUNK])
        wide = gather_wide(wide, channels, -1, period)
        seen = first[channels : 2 * channels, at : at + CHUNK].astype(F32)
        grad_first[:, at : at + CHUNK] = (wide * (1.0 - seen * seen)).astype(BF)


def first_weights(period, net, grad_first, pick_f):
    taps = jnp.concatenate(all_shifts(net, 1, period), axis=0).astype(BF)
    g_first = dot_nt(grad_first, taps).astype(BF)
    return dot(g_first, pick_f)


def fill_bulk(period, mids, first, second, taps, pick_l, g_first, small, stack, turned, bulk):
    channels = mids.shape[0] // 3
    few = channels // 2
    own = slice(channels, 2 * channels)
    rounded = mids[own, :].astype(F32)
    in_t = [t_shift(rounded, -dt, period) for dt in STEPS]
    for dy in range(3):
        for dt in range(3):
            turned[(dy * 3 + dt) * channels : (dy * 3 + dt + 1) * channels, :] = y_shift(
                in_t[dt], -STEPS[dy], period
            ).astype(BF)
    stack_planes(stack, first, channels, lambda dx, dz: (dx, dz - 1))
    g_mid = dot_nt(turned[...], stack[...]).astype(BF)
    per_core = bulk.shape[0] // 2
    rows = 9 * few
    g_last = dot_nt(second[own, :], taps).astype(BF)
    g_last = dot(g_last, pick_l).astype(BF)
    for core in range(2):
        base = core * per_core
        for b in range(5):
            for inner in range(9):
                at = inner * channels + core * few
                part = g_mid[at : at + few, b * 128 : (b + 1) * 128]
                if part.shape[1] < 128:
                    part = jnp.concatenate([part, jnp.zeros((few, 128 - part.shape[1]), BF)], axis=1)
                to = base + b * rows + inner * few
                bulk[to : to + few, :] = part
        at = base + 4 * rows
        bulk[at : at + 16, channels:] = small.astype(BF)
        at = base + 5 * rows
        bulk[at : at + channels, :] = g_last[:, core * 128 : (core + 1) * 128]
        bulk[at + channels : at + channels + few, :] = g_first[core * few : (core + 1) * few, :].astype(BF)
        at += channels + few
        if at < base + per_core:
            bulk[at : base + per_core, :] = jnp.zeros((base + per_core - at, 128), BF)


def bias_rows(small, grad_output, mids, grad_first):
    channels = mids.shape[0] // 3
    ones = jnp.ones((8, mids.shape[1]), BF)
    small[0:1, :] = dot_nt(ones, grad_first)[0:1]
    small[1:2, :] = dot_nt(ones, mids[channels : 2 * channels, :])[0:1]
    sums = dot_nt(ones, grad_output.astype(BF))
    small[2:3, 0:1] = sums[0:1, MID : MID + 1]
    small[2:3, 1:2] = sums[0:1, 8 + MID : 9 + MID]


def back_one_kernel(period, ready, *refs):
    windows, refs = refs[:7], refs[7:]
    (logdet0, logdet1, coords, field_in, first_in, second_in, w_last, w_mid, w_first,
     base_out, part_out, small, grad_out, mids, grad_first, field_end, growth, stack) = refs
    place_windows(windows, 0, field_end)
    place_windows(windows, 1, growth)
    frozen = 1.0 - oddness(field_in.shape, coords[0], period)
    moving = 1.0 - frozen
    field = field_end[...]
    ahead = (
        pltpu.roll(field, ROWS - 1, 0)
        + z_shift(field, 1)
        + y_shift(field, 1, period)
        + t_shift(field, 1, period)
    )
    behind = (
        pltpu.roll(field, 1, 0)
        + z_shift(field, -1)
        + y_shift(field, -1, period)
        + t_shift(field, -1, period)
    )
    squared = field * field
    density = (
        -2.0 * hopping * field * ahead + squared + quartic * (squared - 1.0) * (squared - 1.0)
    )[MID : MID + 1]
    action = sum(density[:, at : at + 128] for at in range(0, field.shape[1], 128))
    loss = jnp.sum(action - logdet0[...] - logdet1[...], axis=1, keepdims=True)
    small[...] = jnp.zeros_like(small)
    slot = lax.broadcasted_iota(jnp.int32, (1, small.shape[1]), 1) == coords[0]
    for part in range(3):
        top = loss.astype(BF).astype(F32)
        small[3 + part : 4 + part, :] = jnp.where(slot, top, 0.0)
        loss = loss - top
    place = lax.broadcasted_iota(jnp.int32, field.shape, 0)
    upstream = (
        -2.0 * hopping * (ahead + behind) + 2.0 * field + 4.0 * quartic * (squared - 1.0) * field
    )
    upstream = jnp.where(jnp.logical_and(place >= 1, place <= 5), upstream, 0.0)
    grow = growth[...]
    grad_out[...] = output_gradient(upstream, moving, field_in[...], grow)
    base_out[...] = upstream * (frozen + moving * grow)
    taps = output_taps(grad_out[...], period)
    ready(w_last, second_in)
    second_gradient(w_last, second_in, taps, mids)
    ready(w_mid, first_in)
    first_gradient(period, mids, first_in, w_mid, stack, grad_first)
    bias_rows(small, grad_out[...], mids, grad_first[...])
    ready(w_first)
    narrow = gather_narrow(dot(w_first[...], grad_first[...]), -1, period)
    for d in range(3):
        part_out[d : d + 1, :] = frozen[MID - 1 + d : MID + d] * narrow[d : d + 1]


def weights_one_kernel(period, ready, coords, field_in, first_in, second_in, grad_out, mids, grad_first, small,
                       pick_l, pick_f, bulk, stack, turned):
    taps = output_taps(grad_out[...], period)
    frozen = 1.0 - oddness(field_in.shape, coords[0], period)
    ready(first_in, second_in, pick_l, pick_f)
    g_first = first_weights(period, frozen * field_in[...], grad_first[...], pick_f[...])
    fill_bulk(
        period, mids, first_in, second_in, taps, pick_l[...], g_first, small[...], stack, turned, bulk
    )


def back_zero_kernel(period, layout, ready, *refs):
    windows, refs = refs[:7], refs[7:]
    (base_in, growth, own_in, coords, field_in, bulk_one, first_in, second_in, w_last, w_mid, w_first,
     pick_l, pick_f,
     part_low, part_mid, part_high, send, keep,
     upstream_ref, mids, stack, turned, bulk, grad_first, small) = refs
    frozen = oddness(field_in.shape, coords[0], period)
    upstream_ref[...] = base_in[...]
    for r in range(1, 6):
        upstream_ref[r : r + 1, :] += (
            windows[r - 1][2:3, :] + windows[r][1:2, :] + windows[r + 1][0:1, :]
        )
    grad_output = output_gradient(upstream_ref[...], 1.0 - frozen, field_in[...], growth[...])
    taps = output_taps(grad_output, period)
    ready(w_last, second_in)
    second_gradient(w_last, second_in, taps, mids)
    ready(w_mid, first_in)
    first_gradient(period, mids, first_in, w_mid, stack, grad_first)
    small[...] = jnp.zeros_like(small)
    bias_rows(small, grad_output, mids, grad_first[...])
    ready(w_first, pick_f, pick_l)
    g_first = first_weights(period, frozen * field_in[...], grad_first[...], pick_f[...])
    fill_bulk(
        period, mids, first_in, second_in, taps, pick_l[...], g_first, small[...], stack, turned, bulk
    )
    ready(bulk_one)
    put_chunks(layout, coords, (bulk, bulk_one), send, keep)
    narrow = gather_narrow(dot(w_first[...], grad_first[...]), -1, period)
    base = upstream_ref[...] * (frozen + (1.0 - frozen) * growth[...])
    for d in range(3):
        row = frozen[MID - 1 + d : MID + d] * narrow[d : d + 1]
        if d == 1:
            row = row + base[MID : MID + 1]
        if d == 1:
            part_mid[0:1, :] = row
        else:
            (part_low if d == 0 else part_high)[...] = row
    part_mid[1:2, :] = own_in[...]


def force_kernel(ready, coords, above, middle, below, out):
    piece = out.shape[1]
    lanes = pl.ds(pl.multiple_of(coords[1] * piece, 128), piece)
    out[0:1, :] = above[:, lanes] + middle[0:1, lanes] + below[:, lanes]
    out[1:2, :] = middle[1:2, lanes]


def stage(jobs, after=()):
    arrays, outs, plan = [], [], []
    for kind, parts, group in jobs:
        first = len(arrays)
        arrays += group
        rows = group[0].shape[0]
        if kind == "split":
            sizes = [rows // parts] * parts
        elif kind == "sum":
            sizes = [rows]
        else:
            sizes = [sum(a.shape[0] for a in group)]
        plan.append((kind, first, len(group), len(outs), sizes))
        outs += [shape((n, 128), BF) for n in sizes]
    waits = len(after)

    def body(_, *refs):
        ins, results = refs[: len(arrays)], refs[len(arrays) + waits :]
        for kind, first, many, out, sizes in plan:
            group = ins[first : first + many]
            if kind == "join":
                at = 0
                for ref in group:
                    results[out][at : at + ref.shape[0], :] = ref[...]
                    at += ref.shape[0]
                continue
            at = 0
            for i, n in enumerate(sizes):
                results[out + i][...] = sum(ref[at : at + n, :].astype(F32) for ref in group).astype(BF)
                at += n

    got = kernel_call(body, outs, [], [*arrays, *after], 1_000_000, loose=after, vmem=12, bytes_moved=500_000)
    groups, at = [], 0
    for _, _, _, _, sizes in plan:
        groups.append(list(got[at : at + len(sizes)]))
        at += len(sizes)
    return groups


SMEM = pl.BlockSpec(memory_space=pltpu.SMEM)
VMEM = pl.BlockSpec(memory_space=pltpu.VMEM)
HBM = pl.BlockSpec(memory_space=pltpu.HBM)


HERE = "here"


def locate():
    index = lax.axis_index("xy")
    depth = lax.axis_size("xy") // 4
    core, y, z = index % 2, index // 2 % 2, index // 4
    chip = jnp.where(y == 0, z, 2 * depth - 1 - z)
    place = 2 * chip + jnp.where(chip % 2 == 0, core, 1 - core)
    return place, lax.axis_index("gz"), core, y, z


def kernel_call(body, outs, scratch, args, flops, late=(), loose=(), hbm_outs=0, aliases=None,
                vmem=VMEM_MB, bytes_moved=4_000_000):
    here = next((i for i, a in enumerate(args) if a is HERE), None)
    args = [a for a in args if a is not HERE]
    late = [id(a) for a in late]
    loose = [id(a) for a in loose]
    spec = lambda a: HBM if id(a) in late or id(a) in loose else VMEM
    where = [i for i, a in enumerate(args) if id(a) in late]
    many, extra = len(args), len(where)

    def whole(*refs):
        refs = list(refs)
        ins, rest = refs[:many], refs[many:]
        if extra:
            held, sems = rest[len(rest) - extra - 1 : -1], rest[-1]
            rest = rest[: len(rest) - extra - 1]
        waits = {}
        for n, i in enumerate(where):
            copy = pltpu.make_async_copy(ins[i], held[n], sems.at[n])
            copy.start()
            waits[id(held[n])] = copy
            ins[i] = held[n]

        def ready(*wanted):
            for ref in wanted:
                copy = waits.pop(id(ref), None)
                if copy is not None:
                    copy.wait()

        if here is not None:
            ins.insert(here, locate())
        body(ready, *ins, *rest)
        for copy in waits.values():
            copy.wait()

    held = [pltpu.VMEM(args[i].shape, args[i].dtype) for i in where]
    if extra:
        held.append(pltpu.SemaphoreType.DMA((extra,)))
    return pl.pallas_call(
        whole,
        out_shape=tuple(outs),
        in_specs=[spec(a) for a in args],
        out_specs=tuple([VMEM] * (len(outs) - hbm_outs) + [HBM] * hbm_outs),
        scratch_shapes=[*scratch, *held],
        input_output_aliases=aliases or {},
        compiler_params=pltpu.CompilerParams(vmem_limit_bytes=vmem * 2**20),
        cost_estimate=pl.CostEstimate(flops=flops, bytes_accessed=bytes_moved, transcendentals=0),
    )(*args)


def shape(dims, dtype=F32):
    return jax.ShapeDtypeStruct(dims, dtype)


def forward(period, layer, windows, coords, weights, channels, halves):
    length = windows[0].shape[1]
    outs = [
        shape((ROWS, length)),
        shape((2, length)),
        shape((1, length)),
        shape((1, 128)),
    ]
    if layer == 1:
        outs.append(shape((ROWS, length)))
    args = [*windows, coords, *weights]
    outs += [shape((3 * channels, length), BF)] * 2
    scratch = [
        pltpu.VMEM((5 * channels, length), BF),
        pltpu.VMEM((9 * channels, length), BF),
    ]
    body = functools.partial(forward_kernel, period, layer, halves)
    flops = 3 * 2 * TAPS * channels * channels * length
    return kernel_call(body, outs, scratch, args, flops)


def pack_ahead(layer, w_mid, after=()):
    channels = w_mid.shape[1]
    outs = [shape((9 * channels, 9 * channels), BF)]
    scratch = [pltpu.VMEM((TAPS * channels // 2, 2 * channels), F32)]
    body = functools.partial(pack_ahead_kernel, layer)
    return kernel_call(body, outs, scratch, [w_mid, *after], 1_000_000_000, loose=after)[0]


def pack_narrow(params, after):
    channels = params[0].shape[1]
    outs = [shape((channels, 5 * 256), BF), shape((3, 216, channels), BF), shape((128, 8))]
    scratch = [pltpu.VMEM((8, 128), F32)]
    got = kernel_call(
        pack_narrow_kernel, outs * 2, scratch, [*params, *after], 1_000_000_000, loose=after
    )
    return got[:3], got[3:]


def pack_back(matrices, narrow, picks, after):
    channels = narrow[0].shape[1]
    outs = [
        shape((channels, 3 * 512), BF),
        shape((9 * channels, 9 * channels), BF),
        shape((216, channels), BF),
    ]
    got = kernel_call(
        pack_back_kernel, outs * 2, [], [*matrices, *narrow, *picks, *after], 1_000_000_000, loose=after
    )
    return got[:3], got[3:]


def unpack(last, layout, volume, coords, pieces, channels, before, force=None, block=None):
    halves, depth, chunk = layout
    few = channels // 2
    arrays = [
        shape((2, channels, channels, TAPS)),
        shape((2, 2, channels, TAPS)),
        shape((2, channels, TAPS)),
    ]
    scratch = [
        pltpu.VMEM((2, 2 * halves * depth * chunk, 128), BF),
        pltpu.VMEM((TAPS * few // 2, 2 * channels), F32),
        pltpu.VMEM((2, few, channels, TAPS), F32),
        pltpu.VMEM((2, channels, TAPS), F32),
        pltpu.VMEM((2, few, TAPS), F32),
        pltpu.SemaphoreType.DMA((6,)),
    ]
    body = functools.partial(unpack_kernel, layout, volume, last)
    if not last:
        return kernel_call(
            body, arrays, scratch, [coords, pieces], 1_000_000_000, hbm_outs=3
        )
    extra = [shape((2, channels)), shape((2, channels)), shape((2, 2)), shape((1, 1)), shape(block), shape(block)]
    new = len(extra)

    def reordered(ready, coords, pieces, *refs):
        ins, outs, rest = refs[:4], refs[4 : 7 + new], refs[7 + new :]
        body(ready, coords, pieces, *ins, *outs[new:], *outs[:new], *rest)

    got = kernel_call(
        reordered, extra + arrays, scratch, [coords, pieces, force, *before], 1_000_000_000,
        loose=before, hbm_outs=3, aliases={2 + i: new + i for i in range(3)},
    )
    return [*got[new:], *got[:new]]


def permuters(count, halves, depth):
    xy = lambda fn: [(fn(a), a) for a in range(count)]

    def core(v):
        return lax.ppermute(v, "xy", xy(lambda a: a ^ 1))

    def y(v):
        return lax.ppermute(v, "xy", xy(lambda a: a ^ 2))

    def scatter(pieces):
        return [lax.ppermute(pieces[s], "xy", xy(lambda a, s=s: a ^ (4 * s))) for s in range(1, depth)]

    def gather(v):
        return [lax.ppermute(v, "xy", xy(lambda a, s=s: a ^ (4 * s))) for s in range(1, depth)]

    def square(v):
        out = []
        for rg in range(halves):
            for ry in range(2):
                if rg or ry:
                    pairs = [
                        ((a ^ (2 * ry)) * halves + (j + rg) % halves, a * halves + j)
                        for a in range(count)
                        for j in range(halves)
                    ]
                    out.append(lax.ppermute(v, ("xy", "gz"), pairs))
        return out

    return core, y, scatter, gather, square


def per_device(noise, w_first, b_first, w_mid, b_mid, w_last, b_last):
    period = noise.shape[3]
    count = lax.axis_size("xy")
    halves = lax.axis_size("gz")
    channels = w_mid.shape[2]
    order = ring_order(count)
    volume = float(noise.size * count * halves)
    depth = count // 4
    coords = HERE
    need = 45 * channels // 2 + channels + channels // 2
    chunk = -(-need // (2 * halves * depth * 16)) * 16
    layout = (halves, depth, chunk)

    def step(values, offset):
        return lax.ppermute(
            values, "xy", [(order[(p + offset) % count], order[p]) for p in range(count)]
        )

    whole = [
        lax.ppermute(
            noise,
            ("xy", "gz"),
            [
                (p * halves + (j + rel) % halves, order[p] * halves + j)
                for p in range(count)
                for j in range(halves)
            ],
        )
        for rel in range(halves)
    ]
    params = [
        w_mid.transpose(0, 2, 3, 1),
        w_first.transpose(0, 2, 3, 1).reshape(2, channels, TAPS),
        w_last.transpose(0, 2, 3, 1),
        jnp.stack([b_first, b_mid, jnp.pad(b_last, ((0, 0), (0, channels - 2)))], axis=1).reshape(6, channels),
    ]
    back = spread_last_back()
    pad = ((0, 0), (0, 128 - TAPS))
    back_picks = [
        jnp.asarray(np.concatenate([back[0], back[1]], axis=1), BF),
        jnp.asarray(np.pad(spread_first_back(), pad), BF),
    ]
    pick_l, pick_f = jnp.asarray(pick_last(), BF), jnp.asarray(pick_first(), BF)
    matrices = [pack_ahead(0, params[0])]

    def join(ready, here, *refs):
        out, held = refs[-2:]
        rows = noise.shape[1] * noise.shape[2]
        piece = rows * period
        for rel in range(halves):
            for k in range(rows):
                y = k % noise.shape[2]
                held[:, k * period : (k + 1) * period] = refs[rel][0, k // noise.shape[2], y : y + 1, :]
            to = pl.multiple_of(lax.rem(here[1] + rel, halves) * piece, 128)
            out[:, pl.ds(to, piece)] = held[...]

    waits = (matrices[0],)
    (whole,) = kernel_call(
        join, [shape((1, noise.size * halves))], [pltpu.VMEM((1, noise.size), F32)],
        [HERE, *whole, *waits], 1000, loose=waits, bytes_moved=1000,
    )
    narrow = pack_narrow(params[1:], (whole,))

    def exchange(values):
        return [values if m == 0 else step(values, m) for m in range(-3, 4)]

    field0, state, _, logdet0, first0, second0 = forward(
        period, 0, exchange(whole), coords, (narrow[0][0], matrices[0], *narrow[0][1:]), channels, halves
    )
    matrices.append(pack_ahead(1, params[0], (logdet0,)))
    field1, state, own, logdet1, growth0, first1, second1 = forward(
        period, 1, exchange(state), coords, (narrow[1][0], matrices[1], *narrow[1][1:]), channels, halves
    )
    back_weights = pack_back(matrices, params[1:3], back_picks, (logdet1,))
    core, cross, scatter, gather, square = permuters(count, halves, depth)
    length = field0.shape[1]
    full = shape((ROWS, length))
    planes = shape((3 * channels, length), BF)
    wide = pltpu.VMEM((9 * channels, length), BF)
    bulk = (4 * halves * depth * chunk, 128)
    part = 4 * depth * chunk
    flops = 2 * TAPS * channels * channels * length

    weights = back_weights[1]
    base, parts, small, grad_out, mids, grad_first = kernel_call(
        functools.partial(back_one_kernel, period),
        [full, shape((3, length)), shape((16, channels)), shape((2 * ROWS, length)), planes,
         shape((channels, length), BF)],
        [pltpu.VMEM((ROWS, length), F32), pltpu.VMEM((ROWS, length), F32), wide],
        [*exchange(state), logdet0, logdet1, coords, field1, first1, second1, *weights],
        flops,
    )
    (bulk1,) = kernel_call(
        functools.partial(weights_one_kernel, period),
        [shape(bulk, BF)], [wide, wide],
        [coords, field1, first1, second1, grad_out, mids, grad_first, small, pick_l, pick_f],
        flops,
    )

    weights = back_weights[0]
    low, middle, high, send, keep = kernel_call(
        functools.partial(back_zero_kernel, period, layout),
        [shape((1, length)), shape((2, length)), shape((1, length))]
        + [shape((part, 128), BF)] * 2,
        [pltpu.VMEM((ROWS, length), F32), pltpu.VMEM((3 * channels, length), BF), wide, wide,
         pltpu.VMEM(bulk, BF), pltpu.VMEM((channels, length), BF),
         pltpu.VMEM((16, channels), F32)],
        [*exchange(parts), base, growth0, own, coords, field0, bulk1, first0, second0, *weights,
         pick_l, pick_f],
        2 * flops,
    )

    ((stay, away),) = stage([("split", 2, [keep, core(send)])])
    crossed = cross(away)
    (force,) = kernel_call(
        force_kernel, [shape((2, length // halves))], [],
        [coords, step(low, 1), middle, step(high, -1)], 1000, bytes_moved=1000,
    )
    (pieces,) = stage([("split", depth, [stay, crossed])], after=(force,))
    ((total,),) = stage([("sum", 1, [pieces[0], *scatter(pieces)])])
    ((line,),) = stage([("join", 1, [total, *gather(total)])])
    ((mine,),) = stage([("join", 1, [line, *square(line)])])
    other = core(mine)
    force = lax.ppermute(force, "xy", [(order[p], p) for p in range(count)])
    outs = unpack(False, layout, volume, coords, mine, channels, [])
    g_mid, g_last, g_first, gb_first, gb_mid, gb_last, loss, sample, force = unpack(
        True, layout, volume, coords, other, channels, list(outs), force, noise.shape
    )

    return (
        sample,
        force,
        loss.reshape(()),
        g_first.reshape(2, channels, 1, TAPS).transpose(0, 3, 1, 2),
        gb_first,
        g_mid.transpose(0, 3, 1, 2),
        gb_mid,
        g_last.transpose(0, 3, 1, 2),
        gb_last,
    )


def solution(mesh):
    return jax.shard_map(
        per_device,
        mesh=mesh,
        in_specs=(P("xy", "gz", None, None), P(), P(), P(), P(), P(), P()),
        out_specs=(
            P("xy", "gz", None, None),
            P("xy", "gz", None, None),
            P(),
            P(),
            P(),
            P(),
            P(),
            P(),
            P(),
        ),
        check_vma=False,
    )
```

```python
import functools

import jax
import jax.numpy as jnp
import numpy as np
from jax import lax
from jax.experimental import pallas as pl
from jax.experimental.pallas import tpu as pltpu
from jax.sharding import PartitionSpec as P

hopping = 0.3
quartic = 0.05

STEPS = (-1, 0, 1)
ROWS = 8
MID = 3
BF = jnp.bfloat16
F32 = jnp.float32
TAPS = 81
VMEM_MB = 20
CHUNK = 512


def ring_order(count):
    if count % 4:
        return list(range(count))
    depth = count // 4
    chips = [(z, 0) for z in range(depth)] + [(z, 1) for z in reversed(range(depth))]
    order = []
    for place, (z, y) in enumerate(chips):
        cores = (0, 1) if place % 2 == 0 else (1, 0)
        order += [z * 4 + y * 2 + core for core in cores]
    return order


def spread_last_back():
    out = np.zeros((2, 81, 3, 512), np.float32)
    for tap in range(81):
        dx, rest = divmod(tap, 27)
        for o in range(2):
            for dest in range(3):
                out[o, tap, dest, rest * 16 + o * ROWS + 2 + dest - (dx - 1)] = 1
    return out.reshape(2, 81, 3 * 512)


def spread_first_back():
    out = np.zeros((216, 81), np.float32)
    for tap in range(81):
        dx, rest = divmod(tap, 27)
        out[rest * 8 + dx, tap] = 1
    return out


def pick_last():
    out = np.zeros((432, 2, 128), np.float32)
    for tap in range(81):
        dx, rest = divmod(tap, 27)
        for o in range(2):
            out[rest * 16 + o * ROWS + MID - (dx - 1), o, tap] = 1
    return out.reshape(432, 256)


def pick_first():
    out = np.zeros((216, 128), np.float32)
    for tap in range(81):
        dx, rest = divmod(tap, 27)
        out[rest * ROWS + MID + dx - 1, tap] = 1
    return out


def z_shift(values, dz):
    length = values.shape[1]
    return values if dz == 0 else pltpu.roll(values, (-dz * 128) % length, 1)


def by_plane(values, fn):
    parts = [fn(values[:, at : at + 128]) for at in range(0, values.shape[1], 128)]
    return parts[0] if len(parts) == 1 else jnp.concatenate(parts, axis=1)


def y_shift(values, dy, period):
    if dy == 0:
        return values
    return by_plane(values, lambda v: pltpu.roll(v, (-dy * period) % 128, 1))


def t_shift(values, dt, period):
    if dt == 0:
        return values

    def one(v):
        place = lax.broadcasted_iota(jnp.int32, v.shape, 1) % period
        main = pltpu.roll(v, (-dt) % 128, 1)
        wrap = pltpu.roll(v, (dt * (period - 1)) % 128, 1)
        return jnp.where(place == (period - 1 if dt == 1 else 0), wrap, main)

    return by_plane(values, one)


def all_shifts(values, sign, period):
    in_t = [t_shift(values, sign * dt, period) for dt in STEPS]
    in_y = [[y_shift(v, sign * dy, period) for v in in_t] for dy in STEPS]
    return [z_shift(in_y[dy][dt], sign * dz) for dz in STEPS for dy in range(3) for dt in range(3)]


def gather_narrow(values, sign, period):
    block = lambda k: values[k * 8 : k * 8 + 8]
    total = None
    for dt in range(3):
        over_y = None
        for dy in range(3):
            over_z = sum(z_shift(block(dz * 9 + dy * 3 + dt), sign * (dz - 1)) for dz in range(3))
            over_z = y_shift(over_z, sign * (dy - 1), period)
            over_y = over_z if over_y is None else over_y + over_z
        over_y = t_shift(over_y, sign * (dt - 1), period)
        total = over_y if total is None else total + over_y
    return total


def gather_wide(values, channels, sign, period):
    block = lambda k: values[k * channels : (k + 1) * channels]
    total = None
    for dt in range(3):
        over_y = None
        for dy in range(3):
            part = y_shift(block(dy * 3 + dt), sign * (dy - 1), period)
            over_y = part if over_y is None else over_y + part
        over_y = t_shift(over_y, sign * (dt - 1), period)
        total = over_y if total is None else total + over_y
    return total


def dot(a, b):
    return jnp.dot(a, b, preferred_element_type=F32)


def dot_nt(a, b):
    return lax.dot_general(a, b, (((1,), (1,)), ((), ())), preferred_element_type=F32)


def stack_planes(stack, planes, channels, order):
    length = stack.shape[1]
    for dx in range(3):
        for dz in range(3):
            plane, step = order(dx, dz)
            rows = pl.ds((dx * 3 + dz) * channels, channels)
            source = planes[plane * channels : (plane + 1) * channels, :]
            if step == 0:
                stack[rows, :] = source
            elif step == 1:
                stack[rows, : length - 128] = source[:, 128:]
                stack[rows, length - 128 :] = source[:, :128]
            else:
                stack[rows, 128:] = source[:, : length - 128]
                stack[rows, :128] = source[:, length - 128 :]


def identity(n):
    row = lax.broadcasted_iota(jnp.int32, (n, n), 0)
    return (row == lax.broadcasted_iota(jnp.int32, (n, n), 1)).astype(F32).astype(BF)


def pack_ahead_kernel(layer, ready, w_mid, *refs):
    matrix, taps = refs[-2:]
    channels = w_mid.shape[1]
    few = channels // 2
    for o in range(few):
        pair = jnp.concatenate([w_mid[layer, o], w_mid[layer, o + few]], axis=0)
        taps[pl.ds(o, TAPS, stride=few), :] = dot_nt(identity(TAPS), pair)

    def block(tap):
        both = taps[tap * few : (tap + 1) * few, :]
        return jnp.concatenate([both[:, :channels], both[:, channels:]], axis=0)

    for inner in range(9):
        at = pl.ds(inner * channels, channels)
        for outer in range(0, 9, 2):
            low = block(outer * 9 + inner)
            if outer < 8:
                high = block(outer * 9 + 9 + inner)
                wide = slice(outer * channels, (outer + 2) * channels)
                matrix[at, wide] = jnp.concatenate([low, high], axis=1).astype(BF)
            else:
                matrix[at, outer * channels :] = low.astype(BF)


def pack_narrow_kernel(ready, w_first, w_last, biases, *refs):
    outs, rows = refs[-7:-1], refs[-1]
    channels = w_first.shape[1]
    tap = lax.broadcasted_iota(jnp.int32, (TAPS, 256), 0)
    column = lax.broadcasted_iota(jnp.int32, (TAPS, 256), 1)
    for dest in range(5):
        dx = column % ROWS - dest
        hit = jnp.logical_and(tap == dx * 27 + column // ROWS, jnp.logical_and(dx >= 0, dx <= 2))
        hit = jnp.logical_and(hit, column < 27 * ROWS).astype(F32).astype(BF)
        for layer in range(2):
            outs[3 * layer][:, dest * 256 : (dest + 1) * 256] = dot(w_first[layer], hit).astype(BF)
    row = lax.broadcasted_iota(jnp.int32, (216, TAPS), 0)
    tap = lax.broadcasted_iota(jnp.int32, (216, TAPS), 1)
    for dx in range(3):
        hit = tap == dx * 27 + row // 8
        hits = [jnp.logical_and(hit, row % 8 == o).astype(F32).astype(BF) for o in range(2)]
        for layer in range(2):
            outs[3 * layer + 1][dx] = sum(dot_nt(hits[o], w_last[layer, o]) for o in range(2)).astype(BF)
    for layer in range(2):
        rows[...] = jnp.zeros_like(rows)
        rows[0:3, :channels] = biases[3 * layer : 3 * layer + 3, :]
        outs[3 * layer + 2][...] = rows[...].T


def pack_back_kernel(ready, matrix_zero, matrix_one, w_first, w_last, lanes, spread_rows, *refs):
    outs = refs[-6:]
    channels = w_first.shape[1]
    for layer, matrix in ((0, matrix_zero), (1, matrix_one)):
        last_back, turned, first_back = outs[3 * layer : 3 * layer + 3]
        for inner in range(9):
            at = pl.ds(inner * channels, channels)
            for outer in range(0, 9, 2):
                end = min(outer + 2, 9) * channels
                both = dot_nt(identity(end - outer * channels), matrix[at, outer * channels : end])
                if outer < 8:
                    both = jnp.concatenate([both[:channels], both[channels:]], axis=1)
                turned[at, outer * channels : end] = both.astype(BF)
        first_back[...] = dot_nt(spread_rows[:, :TAPS], w_first[layer]).astype(BF)
        last_back[...] = sum(
            dot(w_last[layer, o], lanes[:, o * 1536 : (o + 1) * 1536]) for o in range(2)
        ).astype(BF)


def unpack_kernel(layout, volume, last, ready, coords, pieces, *refs):
    if last:
        force_in, refs = refs[0], refs[4:]
        g_mid, g_last, g_first, gb_first, gb_mid, gb_last, loss, sample, force = refs[:9]
        bulk, taps, mid, lasts, firsts, sems = refs[9:]
        period = force.shape[3]
        for row, target in ((0, force), (1, sample)):
            for k in range(target.shape[1] * target.shape[2]):
                target[0, k // target.shape[2], k % target.shape[2] : k % target.shape[2] + 1, :] = (
                    force_in[row : row + 1, k * period : (k + 1) * period]
                )
    else:
        g_mid, g_last, g_first = refs[:3]
        bulk, taps, mid, lasts, firsts, sems = refs[3:]
    channels = g_mid.shape[2]
    few = channels // 2
    halves, depth, chunk = layout
    g, y, z = coords[1], coords[3], coords[4]
    core = 1 - coords[2] if last else coords[2]
    per_layer = 2 * halves * depth * chunk
    at = 0
    for rg in range(halves):
        for ry in range(2):
            for rz in range(depth):
                to = ((lax.rem(g + rg, halves) * 2 + (1 - y if ry else y)) * depth
                      + (z ^ rz)) * chunk
                for layer in range(2):
                    bulk[layer, pl.ds(pl.multiple_of(to, 16), chunk), :] = pieces[at : at + chunk, :]
                    at += chunk
    rows, pairs = 9 * few, few // 2
    copies = []
    for layer in range(2):
        for tap in range(TAPS):
            outer, inner = divmod(tap, 9)
            start = (outer // 2) * rows + inner * few
            low = (outer % 2) * channels
            both = bulk[layer, start : start + few, low : low + channels].astype(F32)
            taps[tap * pairs : (tap + 1) * pairs, :channels] = both[:pairs]
            taps[tap * pairs : (tap + 1) * pairs, channels:] = both[pairs:]
        for o in range(pairs):
            pair = taps[pl.ds(o, TAPS, stride=pairs), :].astype(BF)
            pair = dot_nt(identity(2 * channels), pair) * (1.0 / volume)
            mid[layer, o] = pair[:channels]
            mid[layer, o + pairs] = pair[channels:]
        rest = bulk[layer, 5 * rows : 5 * rows + channels + few, :].astype(F32) * (1.0 / volume)
        lasts[layer] = rest[:channels, :TAPS]
        firsts[layer] = rest[channels:, :TAPS]
        if last:
            small = bulk[layer, 4 * rows : 4 * rows + 16, channels:].astype(F32) * (1.0 / volume)
            gb_first[layer : layer + 1, :] = small[0:1]
            gb_mid[layer : layer + 1, :] = small[1:2]
            gb_last[layer : layer + 1, :] = small[2:3, :2]
            if layer == 1:
                loss[...] = jnp.sum(
                    jnp.sum(small[3:6], axis=0, keepdims=True), axis=1, keepdims=True
                )
        copies += [
            pltpu.make_async_copy(
                mid.at[layer], g_mid.at[layer, pl.ds(core * few, few)], sems.at[layer * 3]
            ),
            pltpu.make_async_copy(lasts.at[layer], g_last.at[layer, core], sems.at[layer * 3 + 1]),
            pltpu.make_async_copy(
                firsts.at[layer],
                g_first.at[layer, pl.ds(pl.multiple_of(core * few, few), few)],
                sems.at[layer * 3 + 2],
            ),
        ]
        for copy in copies[-3:]:
            copy.start()
    for copy in copies:
        copy.wait()


def place_windows(refs, row, target):
    target[...] = jnp.zeros_like(target)
    for r, ref in enumerate(refs):
        target[r : r + 1, :] = ref[row : row + 1, :]


def oddness(shape, place, period):
    lane = lax.broadcasted_iota(jnp.int32, shape, 1)
    row = lax.broadcasted_iota(jnp.int32, shape, 0)
    within = lane % 128
    return ((place + row + 1 + lane // 128 + within // period + within % period) % 2).astype(F32)


def forward_kernel(period, layer, halves, ready, *refs):
    windows, refs = refs[:7], refs[7:]
    if layer == 0:
        (coords, w_first, w_mid, w_last, columns,
         field_out, state, own_out, logdet, first_out, second_out, first, stack) = refs
        place_windows(windows, 0, field_out)
    else:
        (coords, w_first, w_mid, w_last, columns,
         field_out, state, own_out, logdet, growth_out, first_out, second_out,
         first, stack) = refs
        place_windows(windows, 0, field_out)
        place_windows(windows, 1, growth_out)
    channels = w_mid.shape[0] // 9
    field = field_out[...]
    length = field.shape[1]
    frozen = oddness(field.shape, coords[0], period)
    if layer == 1:
        frozen = 1.0 - frozen
    net = frozen * field
    taps = jnp.concatenate(all_shifts(net, 1, period), axis=0).astype(BF)
    ready(w_first, columns)
    bias_first, bias_mid = columns[:channels, 0:1], columns[:channels, 1:2]
    for dest in range(5):
        part = dot(w_first[:, dest * 256 : dest * 256 + 216], taps)
        first[dest * channels : (dest + 1) * channels, :] = jnp.tanh(part + bias_first).astype(BF)
    first_out[...] = first[channels : 4 * channels, :]
    ready(w_mid)
    for dest in range(3):
        stack_planes(stack, first, channels, lambda dx, dz: (dest + dx, dz - 1))
        for at in range(0, length, CHUNK):
            wide = dot(w_mid[...], stack[:, at : at + CHUNK])
            wide = gather_wide(wide, channels, 1, period)
            second_out[dest * channels : (dest + 1) * channels, at : at + CHUNK] = jnp.tanh(
                wide + bias_mid
            ).astype(BF)
    ready(w_last)
    narrow = sum(
        dot(w_last[dx], second_out[dx * channels : (dx + 1) * channels, :]) for dx in range(3)
    )
    narrow = gather_narrow(narrow, 1, period) + columns[:8, 2:3]
    growth = jnp.exp(narrow[0:1])
    mine = field[MID : MID + 1]
    still = frozen[MID : MID + 1]
    moving = 1.0 - still
    state[0:1, :] = still * mine + moving * (mine * growth + narrow[1:2])
    state[1:2, :] = growth
    own_out[...] = state[0:1, :]
    flow = moving * narrow[0:1]
    logdet[...] = sum(flow[:, at : at + 128] for at in range(0, length, 128))


def put_chunks(layout, coords, bulks, send, keep):
    halves, depth, chunk = layout
    per_core = bulks[0].shape[0] // 2
    g, c, y, z = (coords[i] for i in range(1, 5))
    for core, ref in ((c, keep), (1 - c, send)):
        at = 0
        for ry in range(2):
            for rz in range(depth):
                source = core * per_core + (
                    (g * 2 + (1 - y if ry else y)) * depth + (z ^ rz)
                ) * chunk
                for bulk in bulks:
                    ref[at : at + chunk, :] = bulk[pl.ds(pl.multiple_of(source, 16), chunk), :]
                    at += chunk


def output_taps(grad_output, period):
    return jnp.concatenate(all_shifts(grad_output, -1, period), axis=0).astype(BF)


def output_gradient(upstream, moving, field, grow):
    place = lax.broadcasted_iota(jnp.int32, (2 * ROWS, field.shape[1]), 0) % ROWS
    grad_scale = upstream * moving * field * grow - moving
    grad_shift = upstream * moving
    both = jnp.concatenate([grad_scale, grad_shift], axis=0)
    return jnp.where(jnp.logical_and(place >= 1, place <= 5), both, 0.0)


def second_gradient(w_last, second, taps, mids):
    channels = mids.shape[0] // 3
    for dest in range(3):
        part = dot(w_last[:, dest * 512 : dest * 512 + 432], taps)
        rows = slice(dest * channels, (dest + 1) * channels)
        wide = second[rows, :].astype(F32)
        mids[rows, :] = (part * (1.0 - wide * wide)).astype(BF)


def first_gradient(period, mids, first, w_mid, stack, grad_first):
    channels = mids.shape[0] // 3
    stack_planes(stack, mids, channels, lambda dx, dz: (2 - dx, 1 - dz))
    for at in range(0, stack.shape[1], CHUNK):
        wide = dot(w_mid[...], stack[:, at : at + CHUNK])
        wide = gather_wide(wide, channels, -1, period)
        seen = first[channels : 2 * channels, at : at + CHUNK].astype(F32)
        grad_first[:, at : at + CHUNK] = (wide * (1.0 - seen * seen)).astype(BF)


def first_weights(period, net, grad_first, pick_f):
    taps = jnp.concatenate(all_shifts(net, 1, period), axis=0).astype(BF)
    g_first = dot_nt(grad_first, taps).astype(BF)
    return dot(g_first, pick_f)


def fill_bulk(period, mids, first, second, taps, pick_l, g_first, small, stack, turned, bulk):
    channels = mids.shape[0] // 3
    few = channels // 2
    own = slice(channels, 2 * channels)
    rounded = mids[own, :].astype(F32)
    in_t = [t_shift(rounded, -dt, period) for dt in STEPS]
    for dy in range(3):
        for dt in range(3):
            turned[(dy * 3 + dt) * channels : (dy * 3 + dt + 1) * channels, :] = y_shift(
                in_t[dt], -STEPS[dy], period
            ).astype(BF)
    stack_planes(stack, first, channels, lambda dx, dz: (dx, dz - 1))
    g_mid = dot_nt(turned[...], stack[...]).astype(BF)
    per_core = bulk.shape[0] // 2
    rows = 9 * few
    g_last = dot_nt(second[own, :], taps).astype(BF)
    g_last = dot(g_last, pick_l).astype(BF)
    for core in range(2):
        base = core * per_core
        for b in range(5):
            for inner in range(9):
                at = inner * channels + core * few
                part = g_mid[at : at + few, b * 128 : (b + 1) * 128]
                if part.shape[1] < 128:
                    part = jnp.concatenate([part, jnp.zeros((few, 128 - part.shape[1]), BF)], axis=1)
                to = base + b * rows + inner * few
                bulk[to : to + few, :] = part
        at = base + 4 * rows
        bulk[at : at + 16, channels:] = small.astype(BF)
        at = base + 5 * rows
        bulk[at : at + channels, :] = g_last[:, core * 128 : (core + 1) * 128]
        bulk[at + channels : at + channels + few, :] = g_first[core * few : (core + 1) * few, :].astype(BF)
        at += channels + few
        if at < base + per_core:
            bulk[at : base + per_core, :] = jnp.zeros((base + per_core - at, 128), BF)


def bias_rows(small, grad_output, mids, grad_first):
    channels = mids.shape[0] // 3
    ones = jnp.ones((8, mids.shape[1]), BF)
    small[0:1, :] = dot_nt(ones, grad_first)[0:1]
    small[1:2, :] = dot_nt(ones, mids[channels : 2 * channels, :])[0:1]
    sums = dot_nt(ones, grad_output.astype(BF))
    small[2:3, 0:1] = sums[0:1, MID : MID + 1]
    small[2:3, 1:2] = sums[0:1, 8 + MID : 9 + MID]


def back_one_kernel(period, ready, *refs):
    windows, refs = refs[:7], refs[7:]
    (logdet0, logdet1, coords, field_in, first_in, second_in, w_last, w_mid, w_first,
     base_out, part_out, small, grad_out, mids, grad_first, field_end, growth, stack) = refs
    place_windows(windows, 0, field_end)
    place_windows(windows, 1, growth)
    frozen = 1.0 - oddness(field_in.shape, coords[0], period)
    moving = 1.0 - frozen
    field = field_end[...]
    ahead = (
        pltpu.roll(field, ROWS - 1, 0)
        + z_shift(field, 1)
        + y_shift(field, 1, period)
        + t_shift(field, 1, period)
    )
    behind = (
        pltpu.roll(field, 1, 0)
        + z_shift(field, -1)
        + y_shift(field, -1, period)
        + t_shift(field, -1, period)
    )
    squared = field * field
    density = (
        -2.0 * hopping * field * ahead + squared + quartic * (squared - 1.0) * (squared - 1.0)
    )[MID : MID + 1]
    action = sum(density[:, at : at + 128] for at in range(0, field.shape[1], 128))
    loss = jnp.sum(action - logdet0[...] - logdet1[...], axis=1, keepdims=True)
    small[...] = jnp.zeros_like(small)
    slot = lax.broadcasted_iota(jnp.int32, (1, small.shape[1]), 1) == coords[0]
    for part in range(3):
        top = loss.astype(BF).astype(F32)
        small[3 + part : 4 + part, :] = jnp.where(slot, top, 0.0)
        loss = loss - top
    place = lax.broadcasted_iota(jnp.int32, field.shape, 0)
    upstream = (
        -2.0 * hopping * (ahead + behind) + 2.0 * field + 4.0 * quartic * (squared - 1.0) * field
    )
    upstream = jnp.where(jnp.logical_and(place >= 1, place <= 5), upstream, 0.0)
    grow = growth[...]
    grad_out[...] = output_gradient(upstream, moving, field_in[...], grow)
    base_out[...] = upstream * (frozen + moving * grow)
    taps = output_taps(grad_out[...], period)
    ready(w_last, second_in)
    second_gradient(w_last, second_in, taps, mids)
    ready(w_mid, first_in)
    first_gradient(period, mids, first_in, w_mid, stack, grad_first)
    bias_rows(small, grad_out[...], mids, grad_first[...])
    ready(w_first)
    narrow = gather_narrow(dot(w_first[...], grad_first[...]), -1, period)
    for d in range(3):
        part_out[d : d + 1, :] = frozen[MID - 1 + d : MID + d] * narrow[d : d + 1]


def weights_one_kernel(period, ready, coords, field_in, first_in, second_in, grad_out, mids, grad_first, small,
                       pick_l, pick_f, bulk, stack, turned):
    taps = output_taps(grad_out[...], period)
    frozen = 1.0 - oddness(field_in.shape, coords[0], period)
    ready(first_in, second_in, pick_l, pick_f)
    g_first = first_weights(period, frozen * field_in[...], grad_first[...], pick_f[...])
    fill_bulk(
        period, mids, first_in, second_in, taps, pick_l[...], g_first, small[...], stack, turned, bulk
    )


def back_zero_kernel(period, layout, ready, *refs):
    windows, refs = refs[:7], refs[7:]
    (base_in, growth, own_in, coords, field_in, bulk_one, first_in, second_in, w_last, w_mid, w_first,
     pick_l, pick_f,
     part_low, part_mid, part_high, send, keep,
     upstream_ref, mids, stack, turned, bulk, grad_first, small) = refs
    frozen = oddness(field_in.shape, coords[0], period)
    upstream_ref[...] = base_in[...]
    for r in range(1, 6):
        upstream_ref[r : r + 1, :] += (
            windows[r - 1][2:3, :] + windows[r][1:2, :] + windows[r + 1][0:1, :]
        )
    grad_output = output_gradient(upstream_ref[...], 1.0 - frozen, field_in[...], growth[...])
    taps = output_taps(grad_output, period)
    ready(w_last, second_in)
    second_gradient(w_last, second_in, taps, mids)
    ready(w_mid, first_in)
    first_gradient(period, mids, first_in, w_mid, stack, grad_first)
    small[...] = jnp.zeros_like(small)
    bias_rows(small, grad_output, mids, grad_first[...])
    ready(w_first, pick_f, pick_l)
    g_first = first_weights(period, frozen * field_in[...], grad_first[...], pick_f[...])
    fill_bulk(
        period, mids, first_in, second_in, taps, pick_l[...], g_first, small[...], stack, turned, bulk
    )
    ready(bulk_one)
    put_chunks(layout, coords, (bulk, bulk_one), send, keep)
    narrow = gather_narrow(dot(w_first[...], grad_first[...]), -1, period)
    base = upstream_ref[...] * (frozen + (1.0 - frozen) * growth[...])
    for d in range(3):
        row = frozen[MID - 1 + d : MID + d] * narrow[d : d + 1]
        if d == 1:
            row = row + base[MID : MID + 1]
        if d == 1:
            part_mid[0:1, :] = row
        else:
            (part_low if d == 0 else part_high)[...] = row
    part_mid[1:2, :] = own_in[...]


def force_kernel(ready, coords, above, middle, below, out):
    piece = out.shape[1]
    lanes = pl.ds(pl.multiple_of(coords[1] * piece, 128), piece)
    out[0:1, :] = above[:, lanes] + middle[0:1, lanes] + below[:, lanes]
    out[1:2, :] = middle[1:2, lanes]


def stage(jobs, after=()):
    arrays, outs, plan = [], [], []
    for kind, parts, group in jobs:
        first = len(arrays)
        arrays += group
        rows = group[0].shape[0]
        if kind == "split":
            sizes = [rows // parts] * parts
        elif kind == "sum":
            sizes = [rows]
        else:
            sizes = [sum(a.shape[0] for a in group)]
        plan.append((kind, first, len(group), len(outs), sizes))
        outs += [shape((n, 128), BF) for n in sizes]
    waits = len(after)

    def body(_, *refs):
        ins, results = refs[: len(arrays)], refs[len(arrays) + waits :]
        for kind, first, many, out, sizes in plan:
            group = ins[first : first + many]
            if kind == "join":
                at = 0
                for ref in group:
                    results[out][at : at + ref.shape[0], :] = ref[...]
                    at += ref.shape[0]
                continue
            at = 0
            for i, n in enumerate(sizes):
                results[out + i][...] = sum(ref[at : at + n, :].astype(F32) for ref in group).astype(BF)
                at += n

    got = kernel_call(body, outs, [], [*arrays, *after], 1_000_000, loose=after, vmem=12, bytes_moved=500_000)
    groups, at = [], 0
    for _, _, _, _, sizes in plan:
        groups.append(list(got[at : at + len(sizes)]))
        at += len(sizes)
    return groups


SMEM = pl.BlockSpec(memory_space=pltpu.SMEM)
VMEM = pl.BlockSpec(memory_space=pltpu.VMEM)
HBM = pl.BlockSpec(memory_space=pltpu.HBM)


HERE = "here"


def locate():
    index = lax.axis_index("xy")
    depth = lax.axis_size("xy") // 4
    core, y, z = index % 2, index // 2 % 2, index // 4
    chip = jnp.where(y == 0, z, 2 * depth - 1 - z)
    place = 2 * chip + jnp.where(chip % 2 == 0, core, 1 - core)
    return place, lax.axis_index("gz"), core, y, z


def kernel_call(body, outs, scratch, args, flops, late=(), loose=(), hbm_outs=0, aliases=None,
                vmem=VMEM_MB, bytes_moved=4_000_000):
    here = next((i for i, a in enumerate(args) if a is HERE), None)
    args = [a for a in args if a is not HERE]
    late = [id(a) for a in late]
    loose = [id(a) for a in loose]
    spec = lambda a: HBM if id(a) in late or id(a) in loose else VMEM
    where = [i for i, a in enumerate(args) if id(a) in late]
    many, extra = len(args), len(where)

    def whole(*refs):
        refs = list(refs)
        ins, rest = refs[:many], refs[many:]
        if extra:
            held, sems = rest[len(rest) - extra - 1 : -1], rest[-1]
            rest = rest[: len(rest) - extra - 1]
        waits = {}
        for n, i in enumerate(where):
            copy = pltpu.make_async_copy(ins[i], held[n], sems.at[n])
            copy.start()
            waits[id(held[n])] = copy
            ins[i] = held[n]

        def ready(*wanted):
            for ref in wanted:
                copy = waits.pop(id(ref), None)
                if copy is not None:
                    copy.wait()

        if here is not None:
            ins.insert(here, locate())
        body(ready, *ins, *rest)
        for copy in waits.values():
            copy.wait()

    held = [pltpu.VMEM(args[i].shape, args[i].dtype) for i in where]
    if extra:
        held.append(pltpu.SemaphoreType.DMA((extra,)))
    return pl.pallas_call(
        whole,
        out_shape=tuple(outs),
        in_specs=[spec(a) for a in args],
        out_specs=tuple([VMEM] * (len(outs) - hbm_outs) + [HBM] * hbm_outs),
        scratch_shapes=[*scratch, *held],
        input_output_aliases=aliases or {},
        compiler_params=pltpu.CompilerParams(vmem_limit_bytes=vmem * 2**20),
        cost_estimate=pl.CostEstimate(flops=flops, bytes_accessed=bytes_moved, transcendentals=0),
    )(*args)


def shape(dims, dtype=F32):
    return jax.ShapeDtypeStruct(dims, dtype)


def forward(period, layer, windows, coords, weights, channels, halves):
    length = windows[0].shape[1]
    outs = [
        shape((ROWS, length)),
        shape((2, length)),
        shape((1, length)),
        shape((1, 128)),
    ]
    if layer == 1:
        outs.append(shape((ROWS, length)))
    args = [*windows, coords, *weights]
    outs += [shape((3 * channels, length), BF)] * 2
    scratch = [
        pltpu.VMEM((5 * channels, length), BF),
        pltpu.VMEM((9 * channels, length), BF),
    ]
    body = functools.partial(forward_kernel, period, layer, halves)
    flops = 3 * 2 * TAPS * channels * channels * length
    return kernel_call(body, outs, scratch, args, flops)


def pack_ahead(layer, w_mid, after=()):
    channels = w_mid.shape[1]
    outs = [shape((9 * channels, 9 * channels), BF)]
    scratch = [pltpu.VMEM((TAPS * channels // 2, 2 * channels), F32)]
    body = functools.partial(pack_ahead_kernel, layer)
    return kernel_call(body, outs, scratch, [w_mid, *after], 1_000_000_000, loose=after)[0]


def pack_narrow(params, after):
    channels = params[0].shape[1]
    outs = [shape((channels, 5 * 256), BF), shape((3, 216, channels), BF), shape((128, 8))]
    scratch = [pltpu.VMEM((8, 128), F32)]
    got = kernel_call(
        pack_narrow_kernel, outs * 2, scratch, [*params, *after], 1_000_000_000, loose=after
    )
    return got[:3], got[3:]


def pack_back(matrices, narrow, picks, after):
    channels = narrow[0].shape[1]
    outs = [
        shape((channels, 3 * 512), BF),
        shape((9 * channels, 9 * channels), BF),
        shape((216, channels), BF),
    ]
    got = kernel_call(
        pack_back_kernel, outs * 2, [], [*matrices, *narrow, *picks, *after], 1_000_000_000, loose=after
    )
    return got[:3], got[3:]


def unpack(last, layout, volume, coords, pieces, channels, before, force=None, block=None):
    halves, depth, chunk = layout
    few = channels // 2
    arrays = [
        shape((2, channels, channels, TAPS)),
        shape((2, 2, channels, TAPS)),
        shape((2, channels, TAPS)),
    ]
    scratch = [
        pltpu.VMEM((2, 2 * halves * depth * chunk, 128), BF),
        pltpu.VMEM((TAPS * few // 2, 2 * channels), F32),
        pltpu.VMEM((2, few, channels, TAPS), F32),
        pltpu.VMEM((2, channels, TAPS), F32),
        pltpu.VMEM((2, few, TAPS), F32),
        pltpu.SemaphoreType.DMA((6,)),
    ]
    body = functools.partial(unpack_kernel, layout, volume, last)
    if not last:
        return kernel_call(
            body, arrays, scratch, [coords, pieces], 1_000_000_000, hbm_outs=3
        )
    extra = [shape((2, channels)), shape((2, channels)), shape((2, 2)), shape((1, 1)), shape(block), shape(block)]
    new = len(extra)

    def reordered(ready, coords, pieces, *refs):
        ins, outs, rest = refs[:4], refs[4 : 7 + new], refs[7 + new :]
        body(ready, coords, pieces, *ins, *outs[new:], *outs[:new], *rest)

    got = kernel_call(
        reordered, extra + arrays, scratch, [coords, pieces, force, *before], 1_000_000_000,
        loose=before, hbm_outs=3, aliases={2 + i: new + i for i in range(3)},
    )
    return [*got[new:], *got[:new]]


def permuters(count, halves, depth):
    xy = lambda fn: [(fn(a), a) for a in range(count)]

    def core(v):
        return lax.ppermute(v, "xy", xy(lambda a: a ^ 1))

    def y(v):
        return lax.ppermute(v, "xy", xy(lambda a: a ^ 2))

    def scatter(pieces):
        return [lax.ppermute(pieces[s], "xy", xy(lambda a, s=s: a ^ (4 * s))) for s in range(1, depth)]

    def gather(v):
        return [lax.ppermute(v, "xy", xy(lambda a, s=s: a ^ (4 * s))) for s in range(1, depth)]

    def square(v):
        out = []
        for rg in range(halves):
            for ry in range(2):
                if rg or ry:
                    pairs = [
                        ((a ^ (2 * ry)) * halves + (j + rg) % halves, a * halves + j)
                        for a in range(count)
                        for j in range(halves)
                    ]
                    out.append(lax.ppermute(v, ("xy", "gz"), pairs))
        return out

    return core, y, scatter, gather, square


def per_device(noise, w_first, b_first, w_mid, b_mid, w_last, b_last):
    period = noise.shape[3]
    count = lax.axis_size("xy")
    halves = lax.axis_size("gz")
    channels = w_mid.shape[2]
    order = ring_order(count)
    volume = float(noise.size * count * halves)
    depth = count // 4
    coords = HERE
    need = 45 * channels // 2 + channels + channels // 2
    chunk = -(-need // (2 * halves * depth * 16)) * 16
    layout = (halves, depth, chunk)

    def step(values, offset):
        return lax.ppermute(
            values, "xy", [(order[(p + offset) % count], order[p]) for p in range(count)]
        )

    whole = [
        lax.ppermute(
            noise,
            ("xy", "gz"),
            [
                (p * halves + (j + rel) % halves, order[p] * halves + j)
                for p in range(count)
                for j in range(halves)
            ],
        )
        for rel in range(halves)
    ]
    params = [
        w_mid.transpose(0, 2, 3, 1),
        w_first.transpose(0, 2, 3, 1).reshape(2, channels, TAPS),
        w_last.transpose(0, 2, 3, 1),
    ]
    back = spread_last_back()
    pad = ((0, 0), (0, 128 - TAPS))
    back_picks = [
        jnp.asarray(np.concatenate([back[0], back[1]], axis=1), BF),
        jnp.asarray(np.pad(spread_first_back(), pad), BF),
    ]
    pick_l, pick_f = jnp.asarray(pick_last(), BF), jnp.asarray(pick_first(), BF)
    matrices = [pack_ahead(0, params[0])]

    def join(ready, here, *refs):
        out, held = refs[-2:]
        rows = noise.shape[1] * noise.shape[2]
        piece = rows * period
        for rel in range(halves):
            for k in range(rows):
                y = k % noise.shape[2]
                held[:, k * period : (k + 1) * period] = refs[rel][0, k // noise.shape[2], y : y + 1, :]
            to = pl.multiple_of(lax.rem(here[1] + rel, halves) * piece, 128)
            out[:, pl.ds(to, piece)] = held[...]

    waits = (matrices[0],)
    (whole,) = kernel_call(
        join, [shape((1, noise.size * halves))], [pltpu.VMEM((1, noise.size), F32)],
        [HERE, *whole, *waits], 1000, loose=waits, bytes_moved=1000,
    )
    *bias, whole = lax.optimization_barrier((b_first, b_mid, b_last, whole))
    bias[2] = jnp.pad(bias[2], ((0, 0), (0, channels - 2)))
    narrow = pack_narrow([*params[1:3], jnp.stack(bias, axis=1).reshape(6, channels)], (whole,))

    def exchange(values):
        return [values if m == 0 else step(values, m) for m in range(-3, 4)]

    field0, state, _, logdet0, first0, second0 = forward(
        period, 0, exchange(whole), coords, (narrow[0][0], matrices[0], *narrow[0][1:]), channels, halves
    )
    matrices.append(pack_ahead(1, params[0], (logdet0,)))
    field1, state, own, logdet1, growth0, first1, second1 = forward(
        period, 1, exchange(state), coords, (narrow[1][0], matrices[1], *narrow[1][1:]), channels, halves
    )
    back_weights = pack_back(matrices, params[1:3], back_picks, (logdet1,))
    core, cross, scatter, gather, square = permuters(count, halves, depth)
    length = field0.shape[1]
    full = shape((ROWS, length))
    planes = shape((3 * channels, length), BF)
    wide = pltpu.VMEM((9 * channels, length), BF)
    bulk = (4 * halves * depth * chunk, 128)
    part = 4 * depth * chunk
    flops = 2 * TAPS * channels * channels * length

    weights = back_weights[1]
    base, parts, small, grad_out, mids, grad_first = kernel_call(
        functools.partial(back_one_kernel, period),
        [full, shape((3, length)), shape((16, channels)), shape((2 * ROWS, length)), planes,
         shape((channels, length), BF)],
        [pltpu.VMEM((ROWS, length), F32), pltpu.VMEM((ROWS, length), F32), wide],
        [*exchange(state), logdet0, logdet1, coords, field1, first1, second1, *weights],
        flops,
    )
    (bulk1,) = kernel_call(
        functools.partial(weights_one_kernel, period),
        [shape(bulk, BF)], [wide, wide],
        [coords, field1, first1, second1, grad_out, mids, grad_first, small, pick_l, pick_f],
        flops,
    )

    weights = back_weights[0]
    low, middle, high, send, keep = kernel_call(
        functools.partial(back_zero_kernel, period, layout),
        [shape((1, length)), shape((2, length)), shape((1, length))]
        + [shape((part, 128), BF)] * 2,
        [pltpu.VMEM((ROWS, length), F32), pltpu.VMEM((3 * channels, length), BF), wide, wide,
         pltpu.VMEM(bulk, BF), pltpu.VMEM((channels, length), BF),
         pltpu.VMEM((16, channels), F32)],
        [*exchange(parts), base, growth0, own, coords, field0, bulk1, first0, second0, *weights,
         pick_l, pick_f],
        2 * flops,
    )

    ((stay, away),) = stage([("split", 2, [keep, core(send)])])
    crossed = cross(away)
    (force,) = kernel_call(
        force_kernel, [shape((2, length // halves))], [],
        [coords, step(low, 1), middle, step(high, -1)], 1000, bytes_moved=1000,
    )
    (pieces,) = stage([("split", depth, [stay, crossed])], after=(force,))
    ((total,),) = stage([("sum", 1, [pieces[0], *scatter(pieces)])])
    ((line,),) = stage([("join", 1, [total, *gather(total)])])
    force = lax.ppermute(force, "xy", [(order[p], p) for p in range(count)])
    ((mine,),) = stage([("join", 1, [line, *square(line)])], after=(force,))
    other = core(mine)
    outs = unpack(False, layout, volume, coords, mine, channels, [])
    g_mid, g_last, g_first, gb_first, gb_mid, gb_last, loss, sample, force = unpack(
        True, layout, volume, coords, other, channels, list(outs), force, noise.shape
    )

    return (
        sample,
        force,
        loss.reshape(()),
        g_first.reshape(2, channels, 1, TAPS).transpose(0, 3, 1, 2),
        gb_first,
        g_mid.transpose(0, 3, 1, 2),
        gb_mid,
        g_last.transpose(0, 3, 1, 2),
        gb_last,
    )


def solution(mesh):
    return jax.shard_map(
        per_device,
        mesh=mesh,
        in_specs=(P("xy", "gz", None, None), P(), P(), P(), P(), P(), P()),
        out_specs=(
            P("xy", "gz", None, None),
            P("xy", "gz", None, None),
            P(),
            P(),
            P(),
            P(),
            P(),
            P(),
            P(),
        ),
        check_vma=False,
    )
```

```python
import functools

import jax
import jax.numpy as jnp
import numpy as np
from jax import lax
from jax.experimental import pallas as pl
from jax.experimental.pallas import tpu as pltpu
from jax.sharding import PartitionSpec as P

hopping = 0.3
quartic = 0.05

STEPS = (-1, 0, 1)
ROWS = 8
MID = 3
BF = jnp.bfloat16
F32 = jnp.float32
TAPS = 81
TAP_ROWS = 88
VMEM_MB = 20
CHUNK = 512


def ring_order(count):
    if count % 4:
        return list(range(count))
    depth = count // 4
    chips = [(z, 0) for z in range(depth)] + [(z, 1) for z in reversed(range(depth))]
    order = []
    for place, (z, y) in enumerate(chips):
        cores = (0, 1) if place % 2 == 0 else (1, 0)
        order += [z * 4 + y * 2 + core for core in cores]
    return order


def spread_last_back():
    out = np.zeros((2, 81, 3, 512), np.float32)
    for tap in range(81):
        dx, rest = divmod(tap, 27)
        for o in range(2):
            for dest in range(3):
                out[o, tap, dest, rest * 16 + o * ROWS + 2 + dest - (dx - 1)] = 1
    return out.reshape(2, 81, 3 * 512)


def spread_first_back():
    out = np.zeros((216, 81), np.float32)
    for tap in range(81):
        dx, rest = divmod(tap, 27)
        out[rest * 8 + dx, tap] = 1
    return out


def pick_last():
    out = np.zeros((432, 2, 128), np.float32)
    for tap in range(81):
        dx, rest = divmod(tap, 27)
        for o in range(2):
            out[rest * 16 + o * ROWS + MID - (dx - 1), o, tap] = 1
    return out.reshape(432, 256)


def pick_first():
    out = np.zeros((216, 128), np.float32)
    for tap in range(81):
        dx, rest = divmod(tap, 27)
        out[rest * ROWS + MID + dx - 1, tap] = 1
    return out


def z_shift(values, dz):
    length = values.shape[1]
    return values if dz == 0 else pltpu.roll(values, (-dz * 128) % length, 1)


def by_plane(values, fn):
    parts = [fn(values[:, at : at + 128]) for at in range(0, values.shape[1], 128)]
    return parts[0] if len(parts) == 1 else jnp.concatenate(parts, axis=1)


def y_shift(values, dy, period):
    if dy == 0:
        return values
    return by_plane(values, lambda v: pltpu.roll(v, (-dy * period) % 128, 1))


def t_shift(values, dt, period):
    if dt == 0:
        return values

    def one(v):
        place = lax.broadcasted_iota(jnp.int32, v.shape, 1) % period
        main = pltpu.roll(v, (-dt) % 128, 1)
        wrap = pltpu.roll(v, (dt * (period - 1)) % 128, 1)
        return jnp.where(place == (period - 1 if dt == 1 else 0), wrap, main)

    return by_plane(values, one)


def all_shifts(values, sign, period):
    in_t = [t_shift(values, sign * dt, period) for dt in STEPS]
    in_y = [[y_shift(v, sign * dy, period) for v in in_t] for dy in STEPS]
    return [z_shift(in_y[dy][dt], sign * dz) for dz in STEPS for dy in range(3) for dt in range(3)]


def gather_narrow(values, sign, period):
    block = lambda k: values[k * 8 : k * 8 + 8]
    total = None
    for dt in range(3):
        over_y = None
        for dy in range(3):
            over_z = sum(z_shift(block(dz * 9 + dy * 3 + dt), sign * (dz - 1)) for dz in range(3))
            over_z = y_shift(over_z, sign * (dy - 1), period)
            over_y = over_z if over_y is None else over_y + over_z
        over_y = t_shift(over_y, sign * (dt - 1), period)
        total = over_y if total is None else total + over_y
    return total


def gather_wide(values, channels, sign, period):
    block = lambda k: values[k * channels : (k + 1) * channels]
    total = None
    for dt in range(3):
        over_y = None
        for dy in range(3):
            part = y_shift(block(dy * 3 + dt), sign * (dy - 1), period)
            over_y = part if over_y is None else over_y + part
        over_y = t_shift(over_y, sign * (dt - 1), period)
        total = over_y if total is None else total + over_y
    return total


def dot(a, b):
    return jnp.dot(a, b, preferred_element_type=F32)


def dot_nt(a, b):
    return lax.dot_general(a, b, (((1,), (1,)), ((), ())), preferred_element_type=F32)


def stack_planes(stack, planes, channels, order):
    length = stack.shape[1]
    for dx in range(3):
        for dz in range(3):
            plane, step = order(dx, dz)
            rows = pl.ds((dx * 3 + dz) * channels, channels)
            source = planes[plane * channels : (plane + 1) * channels, :]
            if step == 0:
                stack[rows, :] = source
            elif step == 1:
                stack[rows, : length - 128] = source[:, 128:]
                stack[rows, length - 128 :] = source[:, :128]
            else:
                stack[rows, 128:] = source[:, : length - 128]
                stack[rows, :128] = source[:, length - 128 :]


def identity(n):
    row = lax.broadcasted_iota(jnp.int32, (n, n), 0)
    return (row == lax.broadcasted_iota(jnp.int32, (n, n), 1)).astype(F32).astype(BF)


def pack_ahead_kernel(layer, ready, w_mid, *refs):
    matrix, taps = refs[-2:]
    channels = w_mid.shape[1]
    few = channels // 2
    for o in range(few):
        pair = jnp.concatenate([w_mid[layer, o], w_mid[layer, o + few]], axis=0)
        taps[pl.ds(o, TAPS, stride=few), :] = dot_nt(identity(TAPS), pair)

    def block(tap):
        both = taps[tap * few : (tap + 1) * few, :]
        return jnp.concatenate([both[:, :channels], both[:, channels:]], axis=0)

    for inner in range(9):
        at = pl.ds(inner * channels, channels)
        for outer in range(0, 9, 2):
            low = block(outer * 9 + inner)
            if outer < 8:
                high = block(outer * 9 + 9 + inner)
                wide = slice(outer * channels, (outer + 2) * channels)
                matrix[at, wide] = jnp.concatenate([low, high], axis=1).astype(BF)
            else:
                matrix[at, outer * channels :] = low.astype(BF)


def pack_narrow_kernel(ready, w_first, w_last, biases, *refs):
    outs, rows = refs[-7:-1], refs[-1]
    channels = w_first.shape[1]
    tap = lax.broadcasted_iota(jnp.int32, (TAPS, 256), 0)
    column = lax.broadcasted_iota(jnp.int32, (TAPS, 256), 1)
    for dest in range(5):
        dx = column % ROWS - dest
        hit = jnp.logical_and(tap == dx * 27 + column // ROWS, jnp.logical_and(dx >= 0, dx <= 2))
        hit = jnp.logical_and(hit, column < 27 * ROWS).astype(F32).astype(BF)
        for layer in range(2):
            outs[3 * layer][:, dest * 256 : (dest + 1) * 256] = dot(w_first[layer], hit).astype(BF)
    row = lax.broadcasted_iota(jnp.int32, (216, TAPS), 0)
    tap = lax.broadcasted_iota(jnp.int32, (216, TAPS), 1)
    for dx in range(3):
        hit = tap == dx * 27 + row // 8
        hits = [jnp.logical_and(hit, row % 8 == o).astype(F32).astype(BF) for o in range(2)]
        for layer in range(2):
            outs[3 * layer + 1][dx] = sum(dot_nt(hits[o], w_last[layer, o]) for o in range(2)).astype(BF)
    for layer in range(2):
        rows[...] = jnp.zeros_like(rows)
        rows[0:3, :channels] = biases[3 * layer : 3 * layer + 3, :]
        outs[3 * layer + 2][...] = rows[...].T


def pack_back_kernel(ready, matrix_zero, matrix_one, w_first, w_last, lanes, spread_rows, *refs):
    outs = refs[-6:]
    channels = w_first.shape[1]
    for layer, matrix in ((0, matrix_zero), (1, matrix_one)):
        last_back, turned, first_back = outs[3 * layer : 3 * layer + 3]
        for inner in range(9):
            at = pl.ds(inner * channels, channels)
            for outer in range(0, 9, 2):
                end = min(outer + 2, 9) * channels
                both = dot_nt(identity(end - outer * channels), matrix[at, outer * channels : end])
                if outer < 8:
                    both = jnp.concatenate([both[:channels], both[channels:]], axis=1)
                turned[at, outer * channels : end] = both.astype(BF)
        first_back[...] = dot_nt(spread_rows[:, :TAPS], w_first[layer]).astype(BF)
        last_back[...] = sum(
            dot(w_last[layer, o], lanes[:, o * 1536 : (o + 1) * 1536]) for o in range(2)
        ).astype(BF)


def unpack_kernel(layout, volume, last, ready, coords, pieces, *refs):
    if last:
        force_in, refs = refs[0], refs[4:]
        g_mid, g_last, g_first, gb_first, gb_mid, gb_last, loss, sample, force = refs[:9]
        bulk, taps, mid, lasts, firsts, sems = refs[9:]
        period = force.shape[3]
        for row, target in ((0, force), (1, sample)):
            for k in range(target.shape[1] * target.shape[2]):
                target[0, k // target.shape[2], k % target.shape[2] : k % target.shape[2] + 1, :] = (
                    force_in[row : row + 1, k * period : (k + 1) * period]
                )
    else:
        g_mid, g_last, g_first = refs[:3]
        bulk, taps, mid, lasts, firsts, sems = refs[3:]
    channels = g_mid.shape[2]
    few = channels // 2
    halves, depth, chunk = layout
    g, y, z = coords[1], coords[3], coords[4]
    core = 1 - coords[2] if last else coords[2]
    per_layer = 2 * halves * depth * chunk
    at = 0
    for rg in range(halves):
        for ry in range(2):
            for rz in range(depth):
                to = ((lax.rem(g + rg, halves) * 2 + (1 - y if ry else y)) * depth
                      + (z ^ rz)) * chunk
                for layer in range(2):
                    bulk[layer, pl.ds(pl.multiple_of(to, 16), chunk), :] = pieces[at : at + chunk, :]
                    at += chunk
    rows, pairs = 9 * few, few // 2
    copies = []
    for layer in range(2):
        for tap in range(TAPS):
            outer, inner = divmod(tap, 9)
            start = (outer // 2) * rows + inner * few
            low = (outer % 2) * channels
            both = bulk[layer, start : start + few, low : low + channels].astype(F32)
            taps[tap * pairs : (tap + 1) * pairs, :channels] = both[:pairs]
            taps[tap * pairs : (tap + 1) * pairs, channels:] = both[pairs:]
        for o in range(pairs):
            pair = taps[pl.ds(o, TAPS, stride=pairs), :].astype(BF)
            pair = dot_nt(identity(2 * channels), pair) * (1.0 / volume)
            mid[layer, o] = pair[:channels]
            mid[layer, o + pairs] = pair[channels:]
        rest = bulk[layer, 5 * rows : 5 * rows + channels + few, :].astype(F32) * (1.0 / volume)
        lasts[layer] = rest[:channels, :TAPS]
        firsts[layer] = rest[channels:, :TAPS]
        if last:
            small = bulk[layer, 4 * rows : 4 * rows + 16, channels:].astype(F32) * (1.0 / volume)
            gb_first[layer : layer + 1, :] = small[0:1]
            gb_mid[layer : layer + 1, :] = small[1:2]
            gb_last[layer : layer + 1, :] = small[2:3, :2]
            if layer == 1:
                loss[...] = jnp.sum(
                    jnp.sum(small[3:6], axis=0, keepdims=True), axis=1, keepdims=True
                )
        copies += [
            pltpu.make_async_copy(
                mid.at[layer], g_mid.at[layer, pl.ds(core * few, few)], sems.at[layer * 3]
            ),
            pltpu.make_async_copy(lasts.at[layer], g_last.at[layer, core], sems.at[layer * 3 + 1]),
            pltpu.make_async_copy(
                firsts.at[layer],
                g_first.at[layer, pl.ds(pl.multiple_of(core * few, few), few)],
                sems.at[layer * 3 + 2],
            ),
        ]
        for copy in copies[-3:]:
            copy.start()
    for copy in copies:
        copy.wait()


def place_windows(refs, row, target):
    target[...] = jnp.zeros_like(target)
    for r, ref in enumerate(refs):
        target[r : r + 1, :] = ref[row : row + 1, :]


def oddness(shape, place, period):
    lane = lax.broadcasted_iota(jnp.int32, shape, 1)
    row = lax.broadcasted_iota(jnp.int32, shape, 0)
    within = lane % 128
    return ((place + row + 1 + lane // 128 + within // period + within % period) % 2).astype(F32)


def forward_kernel(period, layer, halves, ready, *refs):
    windows, refs = refs[:7], refs[7:]
    if layer == 0:
        (coords, w_first, w_mid, w_last, columns,
         field_out, state, own_out, logdet, first_out, second_out, first, stack) = refs
        place_windows(windows, 0, field_out)
    else:
        (coords, w_first, w_mid, w_last, columns,
         field_out, state, own_out, logdet, growth_out, first_out, second_out,
         first, stack) = refs
        place_windows(windows, 0, field_out)
        place_windows(windows, 1, growth_out)
    channels = w_mid.shape[0] // 9
    field = field_out[...]
    length = field.shape[1]
    frozen = oddness(field.shape, coords[0], period)
    if layer == 1:
        frozen = 1.0 - frozen
    net = frozen * field
    taps = jnp.concatenate(all_shifts(net, 1, period), axis=0).astype(BF)
    ready(w_first, columns)
    bias_first, bias_mid = columns[:channels, 0:1], columns[:channels, 1:2]
    for dest in range(5):
        part = dot(w_first[:, dest * 256 : dest * 256 + 216], taps)
        first[dest * channels : (dest + 1) * channels, :] = jnp.tanh(part + bias_first).astype(BF)
    first_out[...] = first[channels : 4 * channels, :]
    ready(w_mid)
    for dest in range(3):
        stack_planes(stack, first, channels, lambda dx, dz: (dest + dx, dz - 1))
        for at in range(0, length, CHUNK):
            wide = dot(w_mid[...], stack[:, at : at + CHUNK])
            wide = gather_wide(wide, channels, 1, period)
            second_out[dest * channels : (dest + 1) * channels, at : at + CHUNK] = jnp.tanh(
                wide + bias_mid
            ).astype(BF)
    ready(w_last)
    narrow = sum(
        dot(w_last[dx], second_out[dx * channels : (dx + 1) * channels, :]) for dx in range(3)
    )
    narrow = gather_narrow(narrow, 1, period) + columns[:8, 2:3]
    growth = jnp.exp(narrow[0:1])
    mine = field[MID : MID + 1]
    still = frozen[MID : MID + 1]
    moving = 1.0 - still
    state[0:1, :] = still * mine + moving * (mine * growth + narrow[1:2])
    state[1:2, :] = growth
    own_out[...] = state[0:1, :]
    flow = moving * narrow[0:1]
    logdet[...] = sum(flow[:, at : at + 128] for at in range(0, length, 128))


def put_chunks(layout, coords, bulks, send, keep):
    halves, depth, chunk = layout
    per_core = bulks[0].shape[0] // 2
    g, c, y, z = (coords[i] for i in range(1, 5))
    for core, ref in ((c, keep), (1 - c, send)):
        at = 0
        for ry in range(2):
            for rz in range(depth):
                source = core * per_core + (
                    (g * 2 + (1 - y if ry else y)) * depth + (z ^ rz)
                ) * chunk
                for bulk in bulks:
                    ref[at : at + chunk, :] = bulk[pl.ds(pl.multiple_of(source, 16), chunk), :]
                    at += chunk


def output_taps(grad_output, period):
    return jnp.concatenate(all_shifts(grad_output, -1, period), axis=0).astype(BF)


def output_gradient(upstream, moving, field, grow):
    place = lax.broadcasted_iota(jnp.int32, (2 * ROWS, field.shape[1]), 0) % ROWS
    grad_scale = upstream * moving * field * grow - moving
    grad_shift = upstream * moving
    both = jnp.concatenate([grad_scale, grad_shift], axis=0)
    return jnp.where(jnp.logical_and(place >= 1, place <= 5), both, 0.0)


def second_gradient(w_last, second, taps, mids):
    channels = mids.shape[0] // 3
    for dest in range(3):
        part = dot(w_last[:, dest * 512 : dest * 512 + 432], taps)
        rows = slice(dest * channels, (dest + 1) * channels)
        wide = second[rows, :].astype(F32)
        mids[rows, :] = (part * (1.0 - wide * wide)).astype(BF)


def first_gradient(period, mids, first, w_mid, stack, grad_first):
    channels = mids.shape[0] // 3
    stack_planes(stack, mids, channels, lambda dx, dz: (2 - dx, 1 - dz))
    for at in range(0, stack.shape[1], CHUNK):
        wide = dot(w_mid[...], stack[:, at : at + CHUNK])
        wide = gather_wide(wide, channels, -1, period)
        seen = first[channels : 2 * channels, at : at + CHUNK].astype(F32)
        grad_first[:, at : at + CHUNK] = (wide * (1.0 - seen * seen)).astype(BF)


def first_weights(period, net, grad_first, pick_f):
    taps = jnp.concatenate(all_shifts(net, 1, period), axis=0).astype(BF)
    g_first = dot_nt(grad_first, taps).astype(BF)
    return dot(g_first, pick_f)


def fill_bulk(period, mids, first, second, taps, pick_l, g_first, small, stack, turned, bulk):
    channels = mids.shape[0] // 3
    few = channels // 2
    own = slice(channels, 2 * channels)
    rounded = mids[own, :].astype(F32)
    in_t = [t_shift(rounded, -dt, period) for dt in STEPS]
    for dy in range(3):
        for dt in range(3):
            turned[(dy * 3 + dt) * channels : (dy * 3 + dt + 1) * channels, :] = y_shift(
                in_t[dt], -STEPS[dy], period
            ).astype(BF)
    stack_planes(stack, first, channels, lambda dx, dz: (dx, dz - 1))
    g_mid = dot_nt(turned[...], stack[...]).astype(BF)
    per_core = bulk.shape[0] // 2
    rows = 9 * few
    g_last = dot_nt(second[own, :], taps).astype(BF)
    g_last = dot(g_last, pick_l).astype(BF)
    for core in range(2):
        base = core * per_core
        for b in range(5):
            for inner in range(9):
                at = inner * channels + core * few
                part = g_mid[at : at + few, b * 128 : (b + 1) * 128]
                if part.shape[1] < 128:
                    part = jnp.concatenate([part, jnp.zeros((few, 128 - part.shape[1]), BF)], axis=1)
                to = base + b * rows + inner * few
                bulk[to : to + few, :] = part
        at = base + 4 * rows
        bulk[at : at + 16, channels:] = small.astype(BF)
        at = base + 5 * rows
        bulk[at : at + channels, :] = g_last[:, core * 128 : (core + 1) * 128]
        bulk[at + channels : at + channels + few, :] = g_first[core * few : (core + 1) * few, :].astype(BF)
        at += channels + few
        if at < base + per_core:
            bulk[at : base + per_core, :] = jnp.zeros((base + per_core - at, 128), BF)


def bias_rows(small, grad_output, mids, grad_first):
    channels = mids.shape[0] // 3
    ones = jnp.ones((8, mids.shape[1]), BF)
    small[0:1, :] = dot_nt(ones, grad_first)[0:1]
    small[1:2, :] = dot_nt(ones, mids[channels : 2 * channels, :])[0:1]
    sums = dot_nt(ones, grad_output.astype(BF))
    small[2:3, 0:1] = sums[0:1, MID : MID + 1]
    small[2:3, 1:2] = sums[0:1, 8 + MID : 9 + MID]


def back_one_kernel(period, ready, *refs):
    windows, refs = refs[:7], refs[7:]
    (logdet0, logdet1, coords, field_in, first_in, second_in, w_last, w_mid, w_first,
     base_out, part_out, small, grad_out, mids, grad_first, field_end, growth, stack) = refs
    place_windows(windows, 0, field_end)
    place_windows(windows, 1, growth)
    frozen = 1.0 - oddness(field_in.shape, coords[0], period)
    moving = 1.0 - frozen
    field = field_end[...]
    ahead = (
        pltpu.roll(field, ROWS - 1, 0)
        + z_shift(field, 1)
        + y_shift(field, 1, period)
        + t_shift(field, 1, period)
    )
    behind = (
        pltpu.roll(field, 1, 0)
        + z_shift(field, -1)
        + y_shift(field, -1, period)
        + t_shift(field, -1, period)
    )
    squared = field * field
    density = (
        -2.0 * hopping * field * ahead + squared + quartic * (squared - 1.0) * (squared - 1.0)
    )[MID : MID + 1]
    action = sum(density[:, at : at + 128] for at in range(0, field.shape[1], 128))
    loss = jnp.sum(action - logdet0[...] - logdet1[...], axis=1, keepdims=True)
    small[...] = jnp.zeros_like(small)
    slot = lax.broadcasted_iota(jnp.int32, (1, small.shape[1]), 1) == coords[0]
    for part in range(3):
        top = loss.astype(BF).astype(F32)
        small[3 + part : 4 + part, :] = jnp.where(slot, top, 0.0)
        loss = loss - top
    place = lax.broadcasted_iota(jnp.int32, field.shape, 0)
    upstream = (
        -2.0 * hopping * (ahead + behind) + 2.0 * field + 4.0 * quartic * (squared - 1.0) * field
    )
    upstream = jnp.where(jnp.logical_and(place >= 1, place <= 5), upstream, 0.0)
    grow = growth[...]
    grad_out[...] = output_gradient(upstream, moving, field_in[...], grow)
    base_out[...] = upstream * (frozen + moving * grow)
    taps = output_taps(grad_out[...], period)
    ready(w_last, second_in)
    second_gradient(w_last, second_in, taps, mids)
    ready(w_mid, first_in)
    first_gradient(period, mids, first_in, w_mid, stack, grad_first)
    bias_rows(small, grad_out[...], mids, grad_first[...])
    ready(w_first)
    narrow = gather_narrow(dot(w_first[...], grad_first[...]), -1, period)
    for d in range(3):
        part_out[d : d + 1, :] = frozen[MID - 1 + d : MID + d] * narrow[d : d + 1]


def weights_one_kernel(period, ready, coords, field_in, first_in, second_in, grad_out, mids, grad_first, small,
                       pick_l, pick_f, bulk, stack, turned):
    taps = output_taps(grad_out[...], period)
    frozen = 1.0 - oddness(field_in.shape, coords[0], period)
    ready(first_in, second_in, pick_l, pick_f)
    g_first = first_weights(period, frozen * field_in[...], grad_first[...], pick_f[...])
    fill_bulk(
        period, mids, first_in, second_in, taps, pick_l[...], g_first, small[...], stack, turned, bulk
    )


def back_zero_kernel(period, layout, ready, *refs):
    windows, refs = refs[:7], refs[7:]
    (base_in, growth, own_in, coords, field_in, bulk_one, first_in, second_in, w_last, w_mid, w_first,
     pick_l, pick_f,
     part_low, part_mid, part_high, send, keep,
     upstream_ref, mids, stack, turned, bulk, grad_first, small) = refs
    frozen = oddness(field_in.shape, coords[0], period)
    upstream_ref[...] = base_in[...]
    for r in range(1, 6):
        upstream_ref[r : r + 1, :] += (
            windows[r - 1][2:3, :] + windows[r][1:2, :] + windows[r + 1][0:1, :]
        )
    grad_output = output_gradient(upstream_ref[...], 1.0 - frozen, field_in[...], growth[...])
    taps = output_taps(grad_output, period)
    ready(w_last, second_in)
    second_gradient(w_last, second_in, taps, mids)
    ready(w_mid, first_in)
    first_gradient(period, mids, first_in, w_mid, stack, grad_first)
    small[...] = jnp.zeros_like(small)
    bias_rows(small, grad_output, mids, grad_first[...])
    ready(w_first, pick_f, pick_l)
    g_first = first_weights(period, frozen * field_in[...], grad_first[...], pick_f[...])
    fill_bulk(
        period, mids, first_in, second_in, taps, pick_l[...], g_first, small[...], stack, turned, bulk
    )
    ready(bulk_one)
    put_chunks(layout, coords, (bulk, bulk_one), send, keep)
    narrow = gather_narrow(dot(w_first[...], grad_first[...]), -1, period)
    base = upstream_ref[...] * (frozen + (1.0 - frozen) * growth[...])
    for d in range(3):
        row = frozen[MID - 1 + d : MID + d] * narrow[d : d + 1]
        if d == 1:
            row = row + base[MID : MID + 1]
        if d == 1:
            part_mid[0:1, :] = row
        else:
            (part_low if d == 0 else part_high)[...] = row
    part_mid[1:2, :] = own_in[...]


def force_kernel(ready, coords, above, middle, below, out):
    piece = out.shape[1]
    lanes = pl.ds(pl.multiple_of(coords[1] * piece, 128), piece)
    out[0:1, :] = above[:, lanes] + middle[0:1, lanes] + below[:, lanes]
    out[1:2, :] = middle[1:2, lanes]


def stage(jobs, after=()):
    arrays, outs, plan = [], [], []
    for kind, parts, group in jobs:
        first = len(arrays)
        arrays += group
        rows = group[0].shape[0]
        if kind == "split":
            sizes = [rows // parts] * parts
        elif kind == "sum":
            sizes = [rows]
        else:
            sizes = [sum(a.shape[0] for a in group)]
        plan.append((kind, first, len(group), len(outs), sizes))
        outs += [shape((n, 128), BF) for n in sizes]
    waits = len(after)

    def body(_, *refs):
        ins, results = refs[: len(arrays)], refs[len(arrays) + waits :]
        for kind, first, many, out, sizes in plan:
            group = ins[first : first + many]
            if kind == "join":
                at = 0
                for ref in group:
                    results[out][at : at + ref.shape[0], :] = ref[...]
                    at += ref.shape[0]
                continue
            at = 0
            for i, n in enumerate(sizes):
                results[out + i][...] = sum(ref[at : at + n, :].astype(F32) for ref in group).astype(BF)
                at += n

    got = kernel_call(body, outs, [], [*arrays, *after], 1_000_000, loose=after, vmem=12, bytes_moved=500_000)
    groups, at = [], 0
    for _, _, _, _, sizes in plan:
        groups.append(list(got[at : at + len(sizes)]))
        at += len(sizes)
    return groups


SMEM = pl.BlockSpec(memory_space=pltpu.SMEM)
VMEM = pl.BlockSpec(memory_space=pltpu.VMEM)
HBM = pl.BlockSpec(memory_space=pltpu.HBM)


HERE = "here"


def locate():
    index = lax.axis_index("xy")
    depth = lax.axis_size("xy") // 4
    core, y, z = index % 2, index // 2 % 2, index // 4
    chip = jnp.where(y == 0, z, 2 * depth - 1 - z)
    place = 2 * chip + jnp.where(chip % 2 == 0, core, 1 - core)
    return place, lax.axis_index("gz"), core, y, z


def kernel_call(body, outs, scratch, args, flops, late=(), loose=(), hbm_outs=0, aliases=None,
                vmem=VMEM_MB, bytes_moved=4_000_000):
    here = next((i for i, a in enumerate(args) if a is HERE), None)
    args = [a for a in args if a is not HERE]
    late = [id(a) for a in late]
    loose = [id(a) for a in loose]
    spec = lambda a: HBM if id(a) in late or id(a) in loose else VMEM
    where = [i for i, a in enumerate(args) if id(a) in late]
    many, extra = len(args), len(where)

    def whole(*refs):
        refs = list(refs)
        ins, rest = refs[:many], refs[many:]
        if extra:
            held, sems = rest[len(rest) - extra - 1 : -1], rest[-1]
            rest = rest[: len(rest) - extra - 1]
        waits = {}
        for n, i in enumerate(where):
            copy = pltpu.make_async_copy(ins[i], held[n], sems.at[n])
            copy.start()
            waits[id(held[n])] = copy
            ins[i] = held[n]

        def ready(*wanted):
            for ref in wanted:
                copy = waits.pop(id(ref), None)
                if copy is not None:
                    copy.wait()

        if here is not None:
            ins.insert(here, locate())
        body(ready, *ins, *rest)
        for copy in waits.values():
            copy.wait()

    held = [pltpu.VMEM(args[i].shape, args[i].dtype) for i in where]
    if extra:
        held.append(pltpu.SemaphoreType.DMA((extra,)))
    return pl.pallas_call(
        whole,
        out_shape=tuple(outs),
        in_specs=[spec(a) for a in args],
        out_specs=tuple([VMEM] * (len(outs) - hbm_outs) + [HBM] * hbm_outs),
        scratch_shapes=[*scratch, *held],
        input_output_aliases=aliases or {},
        compiler_params=pltpu.CompilerParams(vmem_limit_bytes=vmem * 2**20),
        cost_estimate=pl.CostEstimate(flops=flops, bytes_accessed=bytes_moved, transcendentals=0),
    )(*args)


def shape(dims, dtype=F32):
    return jax.ShapeDtypeStruct(dims, dtype)


def forward(period, layer, windows, coords, weights, channels, halves):
    length = windows[0].shape[1]
    outs = [
        shape((ROWS, length)),
        shape((2, length)),
        shape((1, length)),
        shape((1, 128)),
    ]
    if layer == 1:
        outs.append(shape((ROWS, length)))
    args = [*windows, coords, *weights]
    outs += [shape((3 * channels, length), BF)] * 2
    scratch = [
        pltpu.VMEM((5 * channels, length), BF),
        pltpu.VMEM((9 * channels, length), BF),
    ]
    body = functools.partial(forward_kernel, period, layer, halves)
    flops = 3 * 2 * TAPS * channels * channels * length
    return kernel_call(body, outs, scratch, args, flops)


def pack_ahead(layer, w_mid, after=()):
    channels = w_mid.shape[1]
    outs = [shape((9 * channels, 9 * channels), BF)]
    scratch = [pltpu.VMEM((TAP_ROWS * channels // 2, 2 * channels), F32)]
    body = functools.partial(pack_ahead_kernel, layer)
    return kernel_call(body, outs, scratch, [w_mid, *after], 1_000_000_000, loose=after)[0]


def pack_narrow(params, after):
    channels = params[0].shape[1]
    outs = [shape((channels, 5 * 256), BF), shape((3, 216, channels), BF), shape((128, 8))]
    scratch = [pltpu.VMEM((8, 128), F32)]
    got = kernel_call(
        pack_narrow_kernel, outs * 2, scratch, [*params, *after], 1_000_000_000, loose=after
    )
    return got[:3], got[3:]


def pack_back(matrices, narrow, picks, after):
    channels = narrow[0].shape[1]
    outs = [
        shape((channels, 3 * 512), BF),
        shape((9 * channels, 9 * channels), BF),
        shape((216, channels), BF),
    ]
    got = kernel_call(
        pack_back_kernel, outs * 2, [], [*matrices, *narrow, *picks, *after], 1_000_000_000, loose=after
    )
    return got[:3], got[3:]


def unpack(last, layout, volume, coords, pieces, channels, before, force=None, block=None):
    halves, depth, chunk = layout
    few = channels // 2
    arrays = [
        shape((2, channels, channels, TAPS)),
        shape((2, 2, channels, TAPS)),
        shape((2, channels, TAPS)),
    ]
    scratch = [
        pltpu.VMEM((2, 2 * halves * depth * chunk, 128), BF),
        pltpu.VMEM((TAP_ROWS * few // 2, 2 * channels), F32),
        pltpu.VMEM((2, few, channels, TAPS), F32),
        pltpu.VMEM((2, channels, TAPS), F32),
        pltpu.VMEM((2, few, TAPS), F32),
        pltpu.SemaphoreType.DMA((6,)),
    ]
    body = functools.partial(unpack_kernel, layout, volume, last)
    if not last:
        return kernel_call(
            body, arrays, scratch, [coords, pieces], 1_000_000_000, hbm_outs=3
        )
    extra = [shape((2, channels)), shape((2, channels)), shape((2, 2)), shape((1, 1)), shape(block), shape(block)]
    new = len(extra)

    def reordered(ready, coords, pieces, *refs):
        ins, outs, rest = refs[:4], refs[4 : 7 + new], refs[7 + new :]
        body(ready, coords, pieces, *ins, *outs[new:], *outs[:new], *rest)

    got = kernel_call(
        reordered, extra + arrays, scratch, [coords, pieces, force, *before], 1_000_000_000,
        loose=before, hbm_outs=3, aliases={2 + i: new + i for i in range(3)},
    )
    return [*got[new:], *got[:new]]


def permuters(count, halves, depth):
    xy = lambda fn: [(fn(a), a) for a in range(count)]

    def core(v):
        return lax.ppermute(v, "xy", xy(lambda a: a ^ 1))

    def y(v):
        return lax.ppermute(v, "xy", xy(lambda a: a ^ 2))

    def scatter(pieces):
        return [lax.ppermute(pieces[s], "xy", xy(lambda a, s=s: a ^ (4 * s))) for s in range(1, depth)]

    def gather(v):
        return [lax.ppermute(v, "xy", xy(lambda a, s=s: a ^ (4 * s))) for s in range(1, depth)]

    def square(v):
        out = []
        for rg in range(halves):
            for ry in range(2):
                if rg or ry:
                    pairs = [
                        ((a ^ (2 * ry)) * halves + (j + rg) % halves, a * halves + j)
                        for a in range(count)
                        for j in range(halves)
                    ]
                    out.append(lax.ppermute(v, ("xy", "gz"), pairs))
        return out

    return core, y, scatter, gather, square


def per_device(noise, w_first, b_first, w_mid, b_mid, w_last, b_last):
    period = noise.shape[3]
    count = lax.axis_size("xy")
    halves = lax.axis_size("gz")
    channels = w_mid.shape[2]
    order = ring_order(count)
    volume = float(noise.size * count * halves)
    depth = count // 4
    coords = HERE
    need = 45 * channels // 2 + channels + channels // 2
    chunk = -(-need // (2 * halves * depth * 16)) * 16
    layout = (halves, depth, chunk)

    def step(values, offset):
        return lax.ppermute(
            values, "xy", [(order[(p + offset) % count], order[p]) for p in range(count)]
        )

    whole = [
        lax.ppermute(
            noise,
            ("xy", "gz"),
            [
                (p * halves + (j + rel) % halves, order[p] * halves + j)
                for p in range(count)
                for j in range(halves)
            ],
        )
        for rel in range(halves)
    ]
    params = [
        w_mid.transpose(0, 2, 3, 1),
        w_first.transpose(0, 2, 3, 1).reshape(2, channels, TAPS),
        w_last.transpose(0, 2, 3, 1),
    ]
    back = spread_last_back()
    pad = ((0, 0), (0, 128 - TAPS))
    back_picks = [
        jnp.asarray(np.concatenate([back[0], back[1]], axis=1), BF),
        jnp.asarray(np.pad(spread_first_back(), pad), BF),
    ]
    pick_l, pick_f = jnp.asarray(pick_last(), BF), jnp.asarray(pick_first(), BF)
    matrices = [pack_ahead(0, params[0])]

    def join(ready, here, *refs):
        out, held = refs[-2:]
        rows = noise.shape[1] * noise.shape[2]
        piece = rows * period
        for rel in range(halves):
            for k in range(rows):
                y = k % noise.shape[2]
                held[:, k * period : (k + 1) * period] = refs[rel][0, k // noise.shape[2], y : y + 1, :]
            to = pl.multiple_of(lax.rem(here[1] + rel, halves) * piece, 128)
            out[:, pl.ds(to, piece)] = held[...]

    waits = (matrices[0],)
    (whole,) = kernel_call(
        join, [shape((1, noise.size * halves))], [pltpu.VMEM((1, noise.size), F32)],
        [HERE, *whole, *waits], 1000, loose=waits, bytes_moved=1000,
    )
    *bias, whole = lax.optimization_barrier((b_first, b_mid, b_last, whole))
    bias[2] = jnp.pad(bias[2], ((0, 0), (0, channels - 2)))
    narrow = pack_narrow([*params[1:3], jnp.stack(bias, axis=1).reshape(6, channels)], (whole,))

    def exchange(values):
        return [values if m == 0 else step(values, m) for m in range(-3, 4)]

    field0, state, _, logdet0, first0, second0 = forward(
        period, 0, exchange(whole), coords, (narrow[0][0], matrices[0], *narrow[0][1:]), channels, halves
    )
    matrices.append(pack_ahead(1, params[0], (logdet0,)))
    field1, state, own, logdet1, growth0, first1, second1 = forward(
        period, 1, exchange(state), coords, (narrow[1][0], matrices[1], *narrow[1][1:]), channels, halves
    )
    back_weights = pack_back(matrices, params[1:3], back_picks, (logdet1,))
    core, cross, scatter, gather, square = permuters(count, halves, depth)
    length = field0.shape[1]
    full = shape((ROWS, length))
    planes = shape((3 * channels, length), BF)
    wide = pltpu.VMEM((9 * channels, length), BF)
    bulk = (4 * halves * depth * chunk, 128)
    part = 4 * depth * chunk
    flops = 2 * TAPS * channels * channels * length

    weights = back_weights[1]
    base, parts, small, grad_out, mids, grad_first = kernel_call(
        functools.partial(back_one_kernel, period),
        [full, shape((3, length)), shape((16, channels)), shape((2 * ROWS, length)), planes,
         shape((channels, length), BF)],
        [pltpu.VMEM((ROWS, length), F32), pltpu.VMEM((ROWS, length), F32), wide],
        [*exchange(state), logdet0, logdet1, coords, field1, first1, second1, *weights],
        flops,
    )
    (bulk1,) = kernel_call(
        functools.partial(weights_one_kernel, period),
        [shape(bulk, BF)], [wide, wide],
        [coords, field1, first1, second1, grad_out, mids, grad_first, small, pick_l, pick_f],
        flops,
    )

    weights = back_weights[0]
    low, middle, high, send, keep = kernel_call(
        functools.partial(back_zero_kernel, period, layout),
        [shape((1, length)), shape((2, length)), shape((1, length))]
        + [shape((part, 128), BF)] * 2,
        [pltpu.VMEM((ROWS, length), F32), pltpu.VMEM((3 * channels, length), BF), wide, wide,
         pltpu.VMEM(bulk, BF), pltpu.VMEM((channels, length), BF),
         pltpu.VMEM((16, channels), F32)],
        [*exchange(parts), base, growth0, own, coords, field0, bulk1, first0, second0, *weights,
         pick_l, pick_f],
        2 * flops,
    )

    ((stay, away),) = stage([("split", 2, [keep, core(send)])])
    crossed = cross(away)
    (force,) = kernel_call(
        force_kernel, [shape((2, length // halves))], [],
        [coords, step(low, 1), middle, step(high, -1)], 1000, bytes_moved=1000,
    )
    (pieces,) = stage([("split", depth, [stay, crossed])], after=(force,))
    ((total,),) = stage([("sum", 1, [pieces[0], *scatter(pieces)])])
    ((line,),) = stage([("join", 1, [total, *gather(total)])])
    force = lax.ppermute(force, "xy", [(order[p], p) for p in range(count)])
    ((mine,),) = stage([("join", 1, [line, *square(line)])], after=(force,))
    other = core(mine)
    outs = unpack(False, layout, volume, coords, mine, channels, [])
    g_mid, g_last, g_first, gb_first, gb_mid, gb_last, loss, sample, force = unpack(
        True, layout, volume, coords, other, channels, list(outs), force, noise.shape
    )

    return (
        sample,
        force,
        loss.reshape(()),
        g_first.reshape(2, channels, 1, TAPS).transpose(0, 3, 1, 2),
        gb_first,
        g_mid.transpose(0, 3, 1, 2),
        gb_mid,
        g_last.transpose(0, 3, 1, 2),
        gb_last,
    )


def solution(mesh):
    return jax.shard_map(
        per_device,
        mesh=mesh,
        in_specs=(P("xy", "gz", None, None), P(), P(), P(), P(), P(), P()),
        out_specs=(
            P("xy", "gz", None, None),
            P("xy", "gz", None, None),
            P(),
            P(),
            P(),
            P(),
            P(),
            P(),
            P(),
        ),
        check_vma=False,
    )
```
